256 devices in a mesh: pb: 4 (over y), ka: 16 (over z, x_lo), ha: 4 (over x_hi, core).
Axes of the slice: x: 4 (x_hi: 2, x_lo: 2; x = x_hi * 2 + x_lo), y: 4, z: 8, core: 2. Of those that a mesh axis runs over, the one named last changes fastest.
Arguments:
- queries: bfloat16 [16384, 512], P(('pb', 'ka'), 'ha'), may hold values from -6 to 6
- key_rows: bfloat16 [16384, 512], P(('pb', 'ka'), 'ha'), may hold values from -6 to 6
- value_rows: bfloat16 [16384, 512], P(('pb', 'ka'), 'ha'), may hold values from -6 to 6
- outputs: bfloat16 [16384, 512], P(('pb', 'ka'), 'ha'), may hold values from -6 to 6
- out_grad: bfloat16 [16384, 512], P(('pb', 'ka'), 'ha'), may hold values from -6 to 6
- saved_lse: bfloat16 [16384, 4], P(('pb', 'ka'), 'ha'), may hold values from -1 to 12, as said below
- fold_map: int32 [128], replicated, may hold values from 0 to 127, as said below
Outputs:
- query_grad: bfloat16 [16384, 512], P(('pb', 'ka'), 'ha')
- key_grad: bfloat16 [16384, 512], P(('pb', 'ka'), 'ha')
- value_grad: bfloat16 [16384, 512], P(('pb', 'ka'), 'ha')
The draws below stay inside these ranges and needn't reach their ends.
Inputs may be any that keep to these rules, and one draw needn't show every extreme that they name: `fold_map`: stored blocks 2 d and 2 d + 1 hold a mirrored pair of blocks, b and 127 - b, in either order; every block is held once. `saved_lse`: close to the log-sum-exp of the row's visible scores.
All inputs are finite; a program needn't handle non-finite values.
Results may differ from the reference program's by a relative error of at most 0.0055.
Values may be sent and summed in bfloat16 or wider, within the bound.
No kernel may reach another device: no remote copies, remote signals or barrier semaphores. Data moves between devices by JAX's collectives and lax.ppermute only.
A program may use at most 64 MiB of HBM per device.

```python
import math
import jax
import jax.numpy as jnp
from jax import lax

HEAD_DIM = 128
HEADS = 4
SEQ = 16384
BLOCK_ROWS = 128
BLOCKS = 128
WIDTH = 512


def fold_blocks(key):
    pair_count = BLOCKS // 2
    pair_order = jax.random.permutation(jax.random.fold_in(key, 11), pair_count).astype(jnp.int32)
    flipped = jax.random.randint(jax.random.fold_in(key, 13), (pair_count,), 0, 2).astype(jnp.int32)
    first_block = jnp.where(flipped == 1, BLOCKS - 1 - pair_order, pair_order)
    second_block = BLOCKS - 1 - first_block
    return jnp.stack([first_block, second_block], axis=1).reshape(BLOCKS).astype(jnp.int32)


def draw_fold_map(key, part):
    return fold_blocks(key)


def draw_saved_lse(key, part):
    ordering = fold_blocks(key)
    key = jax.random.fold_in(key, 7)
    slots = jnp.arange(SEQ, dtype=jnp.int32)
    position = ordering[slots // BLOCK_ROWS] * BLOCK_ROWS + slots % BLOCK_ROWS
    center = jnp.log(position.astype(jnp.float32) + 1.0) + 0.5
    noise = 0.3 * jax.random.truncated_normal(key, -2.0, 2.0, (SEQ, HEADS), jnp.float32)
    return (center[:, None] + noise).astype(jnp.bfloat16)


def block_levels(rng, dims, shards, low, top_value):
    loudness = 1.0
    for axis_at, blocks in shards:
        heights = jax.random.uniform(jax.random.fold_in(jax.random.fold_in(rng, 6), axis_at), (blocks,), jnp.float32, low / len(shards), top_value / len(shards))
        loudness = loudness * jnp.repeat(jnp.exp(heights), dims[axis_at] // blocks).reshape((-1,) + (1,) * (len(dims) - 1 - axis_at))
    return loudness


def gaussian(rng, extent, deviation, most, split=(), kind=jnp.bfloat16):
    loudness = block_levels(rng, extent, split, -0.22, 0.18) if split else 1.0
    values = jax.random.normal(rng, extent, jnp.float32) * deviation * loudness
    return jnp.minimum(jnp.maximum(values, -most), most).astype(kind)


def setup_inputs(seed: int = 0) -> dict:
    splits = jax.random.split(jax.random.key(seed), 8)
    queries = gaussian(splits[0], (SEQ, WIDTH), 1.0, 6.0, ((0, 64), (1, 4)))
    key_rows = gaussian(splits[1], (SEQ, WIDTH), 1.0, 6.0, ((0, 64), (1, 4)))
    value_rows = gaussian(splits[2], (SEQ, WIDTH), 1.0, 6.0, ((0, 64), (1, 4)))
    outputs = gaussian(splits[3], (SEQ, WIDTH), 1.0, 6.0, ((0, 64), (1, 4)))
    out_grad = gaussian(splits[4], (SEQ, WIDTH), 1.0, 6.0, ((0, 64), (1, 4)))
    saved_lse = draw_saved_lse(jax.random.fold_in(splits[7], 71), 0)
    fold_map = draw_fold_map(jax.random.fold_in(splits[7], 71), 0)
    return dict(queries=queries, key_rows=key_rows, value_rows=value_rows, outputs=outputs, out_grad=out_grad, saved_lse=saved_lse, fold_map=fold_map)


def reference(queries, key_rows, value_rows, outputs, out_grad, saved_lse, fold_map):
    factor = 1.0 / math.sqrt(HEAD_DIM)
    seq_len = queries.shape[0]
    slots = jnp.arange(seq_len, dtype=jnp.int32)
    position = fold_map[slots // BLOCK_ROWS] * BLOCK_ROWS + slots % BLOCK_ROWS
    shaped = (seq_len, HEADS, HEAD_DIM)
    query_all = queries.reshape(shaped).astype(jnp.float32)
    key_all = key_rows.reshape(shaped).astype(jnp.float32)
    value_all = value_rows.reshape(shaped).astype(jnp.float32)
    grad_all = out_grad.reshape(shaped).astype(jnp.float32)
    saved_all = outputs.reshape(shaped).astype(jnp.float32)
    delta = jnp.einsum('qhd,qhd->qh', grad_all, saved_all).astype(jnp.bfloat16)
    delta = lax.optimization_barrier(delta).astype(jnp.float32)
    lse_all = saved_lse.astype(jnp.float32)
    block_len = math.gcd(seq_len, 512)

    def one_block(totals, number):
        key_sum, value_sum = totals
        first_row = (number * block_len).astype(jnp.int32)
        query_blk = lax.dynamic_slice_in_dim(query_all, first_row, block_len, 0)
        grad_blk = lax.dynamic_slice_in_dim(grad_all, first_row, block_len, 0)
        lse_blk = lax.dynamic_slice_in_dim(lse_all, first_row, block_len, 0)
        delta_blk = lax.dynamic_slice_in_dim(delta, first_row, block_len, 0)
        query_pos = lax.dynamic_slice_in_dim(position, first_row, block_len, 0)
        scores = jnp.einsum('qhd,khd->hqk', query_blk, key_all) * factor
        visible = position[None, :] <= query_pos[:, None]
        probs = jnp.where(visible[None], jnp.exp(scores - lse_blk.T[:, :, None]), 0.0)
        probs_low = lax.optimization_barrier(probs.astype(jnp.bfloat16)).astype(jnp.float32)
        value_sum = value_sum + jnp.einsum('hqk,qhd->khd', probs_low, grad_blk)
        dprobs = jnp.einsum('qhd,khd->hqk', grad_blk, value_all)
        dscores = probs * (dprobs - delta_blk.T[:, :, None])
        dscores_low = lax.optimization_barrier(dscores.astype(jnp.bfloat16)).astype(jnp.float32)
        query_part = jnp.einsum('hqk,khd->qhd', dscores_low, key_all)
        key_sum = key_sum + jnp.einsum('hqk,qhd->khd', dscores_low, query_blk)
        return ((key_sum, value_sum), query_part)
    empty = jnp.zeros(shaped, jnp.float32)
    totals, parts = lax.scan(one_block, (empty, empty), jnp.arange(seq_len // block_len, dtype=jnp.int32))
    full_width = HEADS * HEAD_DIM
    query_grad = (parts.reshape(seq_len, full_width) * factor).astype(jnp.bfloat16)
    key_grad = (totals[0].reshape(seq_len, full_width) * factor).astype(jnp.bfloat16)
    value_grad = totals[1].reshape(seq_len, full_width).astype(jnp.bfloat16)
    return (query_grad, key_grad, value_grad)
```

```python
import functools
import math

import jax
import jax.numpy as jnp
from jax import lax
from jax.experimental import pallas as pl
from jax.experimental.pallas import tpu as pltpu
from jax.sharding import Mesh, PartitionSpec as P

F32 = jnp.float32
BF16 = jnp.bfloat16
BLK = 128
DIM = 128
NZ = 8
NY = 8
LOG2E = math.log2(math.e)
FACTOR = 1.0 / math.sqrt(DIM)
VMEM_LIMIT = 48 * 1024 * 1024
YX = ("pb", "kx")
NT = (((1,), (1,)), ((), ()))


def dot(a, b):
    return jnp.dot(a, b, preferred_element_type=F32)


def dot_nt(a, b):
    return lax.dot_general(a, b, NT, preferred_element_type=F32)


def low_block(fold_ref, device):
    first = fold_ref[2 * device]
    second = fold_ref[2 * device + 1]
    return jnp.minimum(first, second), second < first


def prep_kernel(fold_ref, where_ref, q_ref, k_ref, v_ref, o_ref, g_ref, lse_ref, zout_ref, kout_ref):
    _, swapped = low_block(fold_ref, where_ref[0])
    low = pl.multiple_of(jnp.where(swapped, BLK, 0), BLK)
    high = pl.multiple_of(jnp.where(swapped, 0, BLK), BLK)
    rows = []
    for start in (low, high):
        prod = g_ref[pl.ds(start, BLK), :].astype(F32) * o_ref[pl.ds(start, BLK), :].astype(F32)
        delta = jnp.sum(prod.T, axis=0, keepdims=True)
        lse = jnp.broadcast_to(lse_ref[pl.ds(start, BLK), :].astype(F32), (BLK, DIM)).T[0:1, :]
        rows.append((lse, delta))
    stats = jnp.concatenate(
        [rows[0][0], rows[1][0], rows[0][1], rows[1][1], jnp.zeros((12, DIM), F32)], axis=0
    ).astype(BF16)
    for c in range(NZ):
        for at, ref in ((0, q_ref), (2 * BLK, g_ref)):
            zout_ref[c, at : at + BLK, :] = ref[pl.ds(low, BLK), :]
            zout_ref[c, at + BLK : at + 2 * BLK, :] = ref[pl.ds(high, BLK), :]
        zout_ref[c, 4 * BLK :, :] = stats
    for c in range(NY):
        for at, ref in ((0, k_ref), (2 * BLK, v_ref)):
            kout_ref[c, at : at + BLK, :] = ref[pl.ds(low, BLK), :]
            kout_ref[c, at + BLK : at + 2 * BLK, :] = ref[pl.ds(high, BLK), :]


def tile(k, v, kt, q, g, lse, delta, limit=None):
    s = dot_nt(k, q)
    p = jnp.exp2(s * (FACTOR * LOG2E) - lse)
    if limit is not None:
        shape = p.shape
        ahead = lax.broadcasted_iota(jnp.int32, shape, 0) - lax.broadcasted_iota(jnp.int32, shape, 1)
        p = jnp.where(ahead <= limit, p, 0.0)
    dp = dot_nt(v, g)
    ds = (p * (dp - delta)).astype(BF16)
    return dot(p.astype(BF16), g), dot(ds, q), dot(kt, ds)


def grad_kernel(
    fold_ref, where_ref, z_ref, y_ref, dq_ref, dkv_ref, dv_acc, dk_acc, dqt_acc, kt_ref, lse_ref, delta_ref
):
    me_z, me_y = where_ref[1], where_ref[2]
    dv_acc[...] = jnp.zeros_like(dv_acc)
    dk_acc[...] = jnp.zeros_like(dk_acc)
    dqt_acc[...] = jnp.zeros_like(dqt_acc)
    for j in range(NY):
        kt = y_ref[j, : 2 * BLK, :].T
        kt_ref[2 * j] = kt[:, :BLK]
        kt_ref[2 * j + 1] = kt[:, BLK:]
    for i in range(NZ):
        stats = z_ref[i, 4 * BLK :, :].astype(F32)
        for b in range(2):
            lse_ref[2 * i + b] = jnp.broadcast_to(stats[b : b + 1, :] * LOG2E, (8, DIM))
            delta_ref[2 * i + b] = jnp.broadcast_to(stats[2 + b : 3 + b, :], (8, DIM))

    def dense(ip, _):
        def two(at):
            return jnp.concatenate([z_ref[2 * ip, at : at + BLK, :], z_ref[2 * ip + 1, at : at + BLK, :]], 0)

        def row(ref):
            return jnp.concatenate([ref[4 * ip + 1, 0:1, :], ref[4 * ip + 3, 0:1, :]], 1)

        q, g = two(BLK), two(3 * BLK)
        lse, delta = row(lse_ref), row(delta_ref)
        total = jnp.zeros((DIM, 2 * BLK), F32)
        for jp in range(NY // 2):
            a, b = 2 * jp, 2 * jp + 1
            k = jnp.concatenate([y_ref[a, :BLK, :], y_ref[b, :BLK, :]], 0)
            v = jnp.concatenate([y_ref[a, 2 * BLK : 3 * BLK, :], y_ref[b, 2 * BLK : 3 * BLK, :]], 0)
            kt = jnp.concatenate([kt_ref[2 * a], kt_ref[2 * b]], 1)
            dv, dk, dqt = tile(k, v, kt, q, g, lse, delta)
            dv_acc[2 * a] += dv[:BLK]
            dv_acc[2 * b] += dv[BLK:]
            dk_acc[2 * a] += dk[:BLK]
            dk_acc[2 * b] += dk[BLK:]
            total += dqt
        dqt_acc[4 * ip + 1] += total[:, :BLK]
        dqt_acc[4 * ip + 3] += total[:, BLK:]
        return 0

    lax.fori_loop(0, NZ // 2, dense, 0)

    def one(i, j, half, limit):
        at = pl.multiple_of(half * BLK, BLK)
        dv, dk, dqt = tile(
            y_ref[j, pl.ds(at, BLK), :],
            y_ref[j, pl.ds(2 * BLK + at, BLK), :],
            kt_ref[2 * j + half],
            z_ref[i, pl.ds(at, BLK), :],
            z_ref[i, pl.ds(2 * BLK + at, BLK), :],
            lse_ref[2 * i + half, 0:1, :],
            delta_ref[2 * i + half, 0:1, :],
            limit,
        )
        dv_acc[2 * j + half] += dv
        dk_acc[2 * j + half] += dk
        dqt_acc[2 * i + half] += dqt

    def sparse(i, _):
        device_i = where_ref[3] + 2 * i
        low_i, _ = low_block(fold_ref, device_i)
        for j in range(NY):
            low_j, _ = low_block(fold_ref, where_ref[4] + (j // 2) * 16 + j % 2)
            half = jnp.where(low_j < low_i, 0, 1)
            own = jnp.logical_and(i == me_z, j == me_y)
            one(i, j, half, jnp.where(own, 0, BLK))
        return 0

    lax.fori_loop(0, NZ, sparse, 0)
    one(me_z, me_y, 0, 0)

    for b in range(2 * NZ):
        dq_ref[b // 2, (b % 2) * BLK : (b % 2 + 1) * BLK, :] = dqt_acc[b].T.astype(BF16)
    for b in range(2 * NY):
        at = (b % 2) * BLK
        dkv_ref[b // 2, at : at + BLK, :] = dk_acc[b].astype(BF16)
        dkv_ref[b // 2, 2 * BLK + at : 3 * BLK + at, :] = dv_acc[b].astype(BF16)


def sum_kernel(fold_ref, where_ref, dq_ref, dkv_ref, q_ref, k_ref, v_ref):
    _, swapped = low_block(fold_ref, where_ref[0])
    for part in range(2):
        to = pl.multiple_of(jnp.where(swapped, (1 - part) * BLK, part * BLK), BLK)
        at = part * BLK

        def total(ref, start):
            out = ref[0, start : start + BLK, :].astype(F32)
            for c in range(1, ref.shape[0]):
                out += ref[c, start : start + BLK, :].astype(F32)
            return out

        q_ref[pl.ds(to, BLK), :] = (total(dq_ref, at) * FACTOR).astype(BF16)
        k_ref[pl.ds(to, BLK), :] = (total(dkv_ref, at) * FACTOR).astype(BF16)
        v_ref[pl.ds(to, BLK), :] = total(dkv_ref, 2 * BLK + at).astype(BF16)


def body(queries, key_rows, value_rows, outputs, out_grad, saved_lse, fold_map):
    pb, kz, kx = lax.axis_index("pb"), lax.axis_index("kz"), lax.axis_index("kx")
    where = jnp.stack([pb * 16 + kz * 2 + kx, kz, pb * 2 + kx, pb * 16 + kx, kz * 2]).astype(jnp.int32)
    smem = pl.BlockSpec(memory_space=pltpu.SMEM)
    vmem = pl.BlockSpec(memory_space=pltpu.VMEM)
    params = pltpu.CompilerParams(vmem_limit_bytes=VMEM_LIMIT)
    z_rows = 4 * BLK + 16

    def call(kernel, shapes, count, scratch=()):
        return pl.pallas_call(
            kernel,
            out_shape=[jax.ShapeDtypeStruct(s, BF16) for s in shapes],
            in_specs=[smem, smem] + [vmem] * count,
            out_specs=[vmem] * len(shapes),
            scratch_shapes=list(scratch),
            compiler_params=params,
        )

    zout, kout = call(prep_kernel, [(NZ, z_rows, DIM), (NY, 4 * BLK, DIM)], 6)(
        fold_map, where, queries, key_rows, value_rows, outputs, out_grad, saved_lse
    )
    y_all = lax.all_to_all(kout, YX, 0, 0)
    z_all = lax.all_to_all(zout, "kz", 0, 0)
    acc = lambda n: pltpu.VMEM((2 * n, BLK, DIM), F32)
    dq, dkv = call(
        grad_kernel,
        [(NZ, 2 * BLK, DIM), (NY, 4 * BLK, DIM)],
        2,
        [
            acc(NY),
            acc(NY),
            acc(NZ),
            pltpu.VMEM((2 * NY, DIM, BLK), BF16),
            pltpu.VMEM((2 * NZ, 8, DIM), F32),
            pltpu.VMEM((2 * NZ, 8, DIM), F32),
        ],
    )(fold_map, where, z_all, y_all)
    dkv = lax.all_to_all(dkv, YX, 0, 0)
    dq = lax.all_to_all(dq, "kz", 0, 0)
    return tuple(call(sum_kernel, [(2 * BLK, DIM)] * 3, 2)(fold_map, where, dq, dkv))


def solution(mesh):
    fine = Mesh(mesh.devices.reshape(4, 8, 2, 2, 2), ("pb", "kz", "kx", "hx", "hc"))
    rows = P(("pb", "kz", "kx"), ("hx", "hc"))
    return jax.shard_map(
        body,
        mesh=fine,
        in_specs=(rows,) * 6 + (P(),),
        out_specs=(rows,) * 3,
        check_vma=False,
    )
```

```python
import functools
import math

import jax
import jax.numpy as jnp
from jax import lax
from jax.experimental import pallas as pl
from jax.experimental.pallas import tpu as pltpu
from jax.sharding import Mesh, PartitionSpec as P

F32 = jnp.float32
BF16 = jnp.bfloat16
BLK = 128
DIM = 128
LOG2E = math.log2(math.e)
FACTOR = 1.0 / math.sqrt(DIM)
VMEM_LIMIT = 48 * 1024 * 1024
NT = (((1,), (1,)), ((), ()))
Q_ROWS = 4 * BLK + 16
K_ROWS = 4 * BLK


def dot(a, b):
    return jnp.dot(a, b, preferred_element_type=F32)


def dot_nt(a, b):
    return lax.dot_general(a, b, NT, preferred_element_type=F32)


def ring(value, size):
    return lax.rem(value + size, size)


def low_block(fold_ref, device):
    first = fold_ref[2 * device]
    second = fold_ref[2 * device + 1]
    return jnp.minimum(first, second), second < first


def device_row(y, z, x):
    return y * 16 + z * 2 + x


def prep_kernel(fold_ref, where_ref, q_ref, k_ref, v_ref, o_ref, g_ref, lse_ref, zout_ref, kout_ref):
    _, swapped = low_block(fold_ref, device_row(where_ref[0], where_ref[1], where_ref[2]))
    low = pl.multiple_of(jnp.where(swapped, BLK, 0), BLK)
    high = pl.multiple_of(jnp.where(swapped, 0, BLK), BLK)
    rows = []
    for start in (low, high):
        prod = g_ref[pl.ds(start, BLK), :].astype(F32) * o_ref[pl.ds(start, BLK), :].astype(F32)
        delta = jnp.sum(prod.T, axis=0, keepdims=True)
        lse = jnp.broadcast_to(lse_ref[pl.ds(start, BLK), :].astype(F32), (BLK, DIM)).T[0:1, :]
        rows.append((lse, delta))
    stats = jnp.concatenate(
        [rows[0][0], rows[1][0], rows[0][1], rows[1][1], jnp.zeros((12, DIM), F32)], axis=0
    ).astype(BF16)
    for out_ref, at, ref in (
        (zout_ref, 0, q_ref),
        (zout_ref, 2 * BLK, g_ref),
        (kout_ref, 0, k_ref),
        (kout_ref, 2 * BLK, v_ref),
    ):
        out_ref[at : at + BLK, :] = ref[pl.ds(low, BLK), :]
        out_ref[at + BLK : at + 2 * BLK, :] = ref[pl.ds(high, BLK), :]
    zout_ref[4 * BLK :, :] = stats


def tile(k, v, kt, q, g, lse, delta, visible=None):
    s = dot_nt(k, q)
    p = jnp.exp2(s * (FACTOR * LOG2E) - lse)
    if visible is not None:
        p = jnp.where(visible, p, 0.0)
    dp = dot_nt(v, g)
    ds = (p * (dp - delta)).astype(BF16)
    return dot(p.astype(BF16), g), dot(ds, q), dot(kt, ds)


def grad_kernel(turn, fold_ref, where_ref, *refs):
    q_refs, y_ref = refs[:4], refs[4]
    refs = refs[5:]
    if turn > 0:
        dqin_ref, refs = refs[0], refs[1:]
    if turn < 3:
        dqt_acc, dkv_ref, dv_acc, dk_acc, kt_ref, lse_ref, delta_ref = refs
    else:
        dq_refs, (dkv_ref, dv_acc, dk_acc, kt_ref, lse_ref, delta_ref, dqt_acc) = refs[:4], refs[4:]
    y, z, x = where_ref[0], where_ref[1], where_ref[2]
    dv_acc[...] = jnp.zeros_like(dv_acc)
    dk_acc[...] = jnp.zeros_like(dk_acc)
    dqt_acc[...] = dqin_ref[...] if turn > 0 else jnp.zeros_like(dqt_acc)
    for j in range(2):
        kt = y_ref[j, : 2 * BLK, :].T
        kt_ref[2 * j] = kt[:, :BLK]
        kt_ref[2 * j + 1] = kt[:, BLK:]
    for i in range(8):
        stats = q_refs[i // 2][i % 2, 4 * BLK :, :].astype(F32)
        for b in range(2):
            lse_ref[2 * i + b] = jnp.broadcast_to(stats[b : b + 1, :] * LOG2E, (8, DIM))
            delta_ref[2 * i + b] = jnp.broadcast_to(stats[2 + b : 3 + b, :], (8, DIM))

    k = jnp.concatenate([y_ref[0, :BLK, :], y_ref[1, :BLK, :]], 0)
    v = jnp.concatenate([y_ref[0, 2 * BLK : 3 * BLK, :], y_ref[1, 2 * BLK : 3 * BLK, :]], 0)
    kt = jnp.concatenate([kt_ref[0], kt_ref[2]], 1)
    for s in range(4):
        ref = q_refs[s]
        q = jnp.concatenate([ref[0, BLK : 2 * BLK, :], ref[1, BLK : 2 * BLK, :]], 0)
        g = jnp.concatenate([ref[0, 3 * BLK : 4 * BLK, :], ref[1, 3 * BLK : 4 * BLK, :]], 0)
        lse = jnp.concatenate([lse_ref[4 * s + 1, 0:1, :], lse_ref[4 * s + 3, 0:1, :]], 1)
        delta = jnp.concatenate([delta_ref[4 * s + 1, 0:1, :], delta_ref[4 * s + 3, 0:1, :]], 1)
        dv, dk, dqt = tile(k, v, kt, q, g, lse, delta)
        dv_acc[0] += dv[:BLK]
        dv_acc[2] += dv[BLK:]
        dk_acc[0] += dk[:BLK]
        dk_acc[2] += dk[BLK:]
        dqt_acc[4 * s + 1] += dqt[:, :BLK]
        dqt_acc[4 * s + 3] += dqt[:, BLK:]

    def one(i, j, half, visible):
        at = half * BLK if isinstance(half, int) else pl.multiple_of(half * BLK, BLK)
        ref = q_refs[i // 2]
        dv, dk, dqt = tile(
            y_ref[j, pl.ds(at, BLK), :],
            y_ref[j, pl.ds(2 * BLK + at, BLK), :],
            kt_ref[2 * j + half],
            ref[i % 2, pl.ds(at, BLK), :],
            ref[i % 2, pl.ds(2 * BLK + at, BLK), :],
            lse_ref[2 * i + half, 0:1, :],
            delta_ref[2 * i + half, 0:1, :],
            visible,
        )
        dv_acc[2 * j + half] += dv
        dk_acc[2 * j + half] += dk
        dqt_acc[2 * i + half] += dqt

    y_at = ring(y + (0, 3, 1, 2)[turn], 4)
    z_at = (z, ring(z + 7, 8), ring(z + 1, 8), ring(z + jnp.where(lax.rem(z, 2) == 0, 2, 6), 8))
    for i in range(8):
        low_i, _ = low_block(fold_ref, device_row(y, z_at[i // 2], x if i % 2 == 0 else 1 - x))
        for j in range(2):
            if turn == 0 and i == 0 and j == 0:
                shape = (BLK, BLK)
                diagonal = lax.broadcasted_iota(jnp.int32, shape, 0) <= lax.broadcasted_iota(jnp.int32, shape, 1)
                one(i, j, 0, diagonal)
                one(i, j, 1, diagonal)
            else:
                low_j, _ = low_block(fold_ref, device_row(y_at, ring(z + 4 * j, 8), x))
                one(i, j, jnp.where(low_j < low_i, 0, 1), None)

    for b in range(4):
        at = (b % 2) * BLK
        dkv_ref[b // 2, at : at + BLK, :] = dk_acc[b].astype(dkv_ref.dtype)
        dkv_ref[b // 2, 2 * BLK + at : 3 * BLK + at, :] = dv_acc[b].astype(dkv_ref.dtype)
    if turn == 3:
        for b in range(16):
            ref = dq_refs[b // 4]
            at = (b % 2) * BLK
            ref[(b // 2) % 2, at : at + BLK, :] = dqt_acc[b].T.astype(ref.dtype)


def meet_kernel(own_ref, a_ref, b_ref, c_ref, keep_ref, send_ref):
    for part, out_ref in ((0, keep_ref), (1, send_ref)):
        total = own_ref[part].astype(F32)
        for ref in (a_ref, b_ref, c_ref):
            total += ref[part].astype(F32)
        out_ref[...] = total.astype(out_ref.dtype)


def last_kernel(fold_ref, where_ref, dq_ref, dqx_ref, dkv_ref, dkvz_ref, q_ref, k_ref, v_ref):
    _, swapped = low_block(fold_ref, device_row(where_ref[0], where_ref[1], where_ref[2]))
    for part in range(2):
        to = pl.multiple_of(jnp.where(swapped, (1 - part) * BLK, part * BLK), BLK)
        at = part * BLK

        def total(ref, other, start):
            return ref[start : start + BLK, :] + other[start : start + BLK, :].astype(F32)

        q_ref[pl.ds(to, BLK), :] = (total(dq_ref, dqx_ref, at) * FACTOR).astype(BF16)
        k_ref[pl.ds(to, BLK), :] = (total(dkv_ref, dkvz_ref, at) * FACTOR).astype(BF16)
        v_ref[pl.ds(to, BLK), :] = total(dkv_ref, dkvz_ref, 2 * BLK + at).astype(BF16)


def z_step(step):
    return [(i, (i + step) % 8) for i in range(8)]


def y_step(step):
    return [(i, (i + step) % 4) for i in range(4)]


Z_PAIRS = [(i, (i - 2) % 8 if i % 2 == 0 else (i + 2) % 8) for i in range(8)]
Z_BACK = [(b, a) for a, b in Z_PAIRS]
X_SWAP = [(0, 1), (1, 0)]


def call(kernel, outs, operands, scalars=(), scratch=(), **options):
    smem = pl.BlockSpec(memory_space=pltpu.SMEM)
    vmem = pl.BlockSpec(memory_space=pltpu.VMEM)
    return pl.pallas_call(
        kernel,
        out_shape=[jax.ShapeDtypeStruct(s, t) for s, t in outs],
        in_specs=[smem] * len(scalars) + [vmem] * len(operands),
        out_specs=[vmem] * len(outs),
        scratch_shapes=list(scratch),
        compiler_params=pltpu.CompilerParams(vmem_limit_bytes=VMEM_LIMIT),
        **options,
    )(*scalars, *operands)


def body(queries, key_rows, value_rows, outputs, out_grad, saved_lse, fold_map):
    where = jnp.stack([lax.axis_index("pb"), lax.axis_index("kz"), lax.axis_index("kx")]).astype(jnp.int32)
    scalars = (fold_map, where)
    mine_q, mine_k = call(
        prep_kernel,
        [((Q_ROWS, DIM), BF16), ((K_ROWS, DIM), BF16)],
        (queries, key_rows, value_rows, outputs, out_grad, saved_lse),
        scalars,
    )
    q0 = jnp.stack([mine_q, lax.ppermute(mine_q, "kx", X_SWAP)])
    k0 = jnp.stack([mine_k, lax.ppermute(mine_k, "kz", z_step(4))])
    q_sets = [q0] + [lax.ppermute(q0, "kz", p) for p in (z_step(1), z_step(-1), Z_PAIRS)]
    k_sets = [k0] + [lax.ppermute(k0, "pb", y_step(s)) for s in (1, -1, 2)]

    acc = pltpu.VMEM((4, BLK, DIM), F32)
    row = pltpu.VMEM((16, 8, DIM), F32)
    scratch = [acc, acc, pltpu.VMEM((4, DIM, BLK), BF16), row, row]
    dq_acc = ((16, DIM, BLK), F32)
    cost = pl.CostEstimate(flops=16 * 2 * 5 * 4 * BLK**3 // 2, bytes_accessed=1 << 20, transcendentals=0)
    dkv = []
    dq = None
    for turn in range(4):
        operands = q_sets + [k_sets[turn]] + ([dq] if turn else [])
        dkv_out = ((2, K_ROWS, DIM), F32 if turn == 0 else BF16)
        if turn < 3:
            dq, part = call(
                functools.partial(grad_kernel, turn),
                [dq_acc, dkv_out],
                operands,
                scalars,
                scratch,
                input_output_aliases={7: 0} if turn else {},
                cost_estimate=cost,
            )
        else:
            *dqs, part = call(
                functools.partial(grad_kernel, turn),
                [((2, 2 * BLK, DIM), F32 if s == 0 else BF16) for s in range(4)] + [dkv_out],
                operands,
                scalars,
                scratch + [pltpu.VMEM(*dq_acc)],
                cost_estimate=cost,
            )
        dkv.append(part)

    dkv_back = [lax.ppermute(dkv[t], "pb", y_step(s)) for t, s in ((1, -1), (2, 1), (3, 2))]
    dq_back = [lax.ppermute(dqs[t], "kz", p) for t, p in ((1, z_step(-1)), (2, z_step(1)), (3, Z_BACK))]

    def meet(own, back):
        shape = own.shape[1:]
        return call(meet_kernel, [(shape, F32), (shape, BF16)], [own] + back)

    dkv_keep, dkv_send = meet(dkv[0], dkv_back)
    dkv_last = lax.ppermute(dkv_send, "kz", z_step(4))
    dq_keep, dq_send = meet(dqs[0], dq_back)
    dq_last = lax.ppermute(dq_send, "kx", X_SWAP)
    grads = [((2 * BLK, DIM), BF16)] * 3
    return tuple(call(last_kernel, grads, (dq_keep, dq_last, dkv_keep, dkv_last), scalars))


def solution(mesh):
    fine = Mesh(mesh.devices.reshape(4, 8, 2, 2, 2), ("pb", "kz", "kx", "hx", "hc"))
    rows = P(("pb", "kz", "kx"), ("hx", "hc"))
    return jax.shard_map(
        body,
        mesh=fine,
        in_specs=(rows,) * 6 + (P(),),
        out_specs=(rows,) * 3,
        check_vma=False,
    )
```

```python
import functools
import math

import jax
import jax.numpy as jnp
from jax import lax
from jax.experimental import pallas as pl
from jax.experimental.pallas import tpu as pltpu
from jax.sharding import Mesh, PartitionSpec as P

F32 = jnp.float32
BF16 = jnp.bfloat16
BLK = 128
DIM = 128
LOG2E = math.log2(math.e)
FACTOR = 1.0 / math.sqrt(DIM)
VMEM_LIMIT = 48 * 1024 * 1024
PREP_VMEM = 62 * 1024 * 1024
BLOCKS = 128
HIDE = 1e30
Y_FROM = (0, 2, 3, 1)
NT = (((1,), (1,)), ((), ()))
Q_ROWS = 4 * BLK + 16
K_ROWS = 4 * BLK


def dot(a, b):
    return jnp.dot(a, b, preferred_element_type=F32)


def dot_nt(a, b):
    return lax.dot_general(a, b, NT, preferred_element_type=F32)


def ring(value, size):
    return lax.rem(value + size, size)


def low_block(fold_ref, device):
    first = fold_ref[2 * device]
    second = fold_ref[2 * device + 1]
    return jnp.minimum(first, second), second < first


def place(info_ref):
    return info_ref[BLOCKS], info_ref[BLOCKS + 1], info_ref[BLOCKS + 2]


def device_row(y, z, x):
    return y * 16 + z * 2 + x


def prep_kernel(where_ref, *refs):
    sources, (zout_ref, kout_ref), buffers, sems = refs[:7], refs[7:9], refs[9:16], refs[16]
    copies = [pltpu.make_async_copy(s, b, sems.at[n]) for n, (s, b) in enumerate(zip(sources, buffers))]
    for copy in copies:
        copy.start()
    for copy in copies:
        copy.wait()
    fold_ref, q_ref, k_ref, v_ref, o_ref, g_ref, lse_ref = buffers
    _, swapped = low_block(fold_ref, device_row(where_ref[0], where_ref[1], where_ref[2]))
    low = pl.multiple_of(jnp.where(swapped, BLK, 0), BLK)
    high = pl.multiple_of(jnp.where(swapped, 0, BLK), BLK)
    lse = lse_ref[...].astype(F32)
    halves = (lse[:, :BLK], lse[:, BLK:])
    rows = [jnp.where(swapped, halves[1], halves[0]), jnp.where(swapped, halves[0], halves[1])]
    for start in (low, high):
        prod = g_ref[pl.ds(start, BLK), :].astype(F32) * o_ref[pl.ds(start, BLK), :].astype(F32)
        rows.append(jnp.sum(prod.T, axis=0, keepdims=True))
    zout_ref[4 * BLK :, :] = jnp.concatenate(rows + [jnp.zeros((12, DIM), F32)], axis=0).astype(BF16)
    for out_ref, at, ref in (
        (zout_ref, 0, q_ref),
        (zout_ref, 2 * BLK, g_ref),
        (kout_ref, 0, k_ref),
        (kout_ref, 2 * BLK, v_ref),
    ):
        out_ref[at : at + BLK, :] = ref[pl.ds(low, BLK), :]
        out_ref[at + BLK : at + 2 * BLK, :] = ref[pl.ds(high, BLK), :]


def tile(k, v, kt, q, g, lses, delta, diagonal=False):
    s = dot_nt(k, q)
    probs = []
    for b, lse in enumerate(lses):
        p = jnp.exp2(s[b * BLK : (b + 1) * BLK] * (FACTOR * LOG2E) - lse)
        if diagonal and b == 0:
            shape = (BLK, BLK)
            seen = lax.broadcasted_iota(jnp.int32, shape, 0) <= lax.broadcasted_iota(jnp.int32, shape, 1)
            p = jnp.concatenate([jnp.where(seen, p[:, :BLK], 0.0), p[:, BLK:]], 1)
        probs.append(p)
    p = jnp.concatenate(probs, 0)
    dp = dot_nt(v, g)
    ds = (p * (dp - delta)).astype(BF16)
    return dot(p.astype(BF16), g), dot(ds, q), dot(kt, ds)


def grad_kernel(turn, info_ref, *refs):
    q_refs, y_ref, refs = refs[:4], refs[4], refs[5:]
    if turn > 0:
        dqin_ref, refs = refs[0], refs[1:]
    if turn < 3:
        dq_ref, dkv_ref, dv_acc, dk_acc = refs
    else:
        kept_ref, back_ref, refs = refs[0], refs[1], refs[2:]
        dq_refs, (dkv_ref, sum_ref, dv_acc, dk_acc) = refs[:4], refs[4:]
    y, z, x = place(info_ref)
    y_at = ring(y + Y_FROM[turn], 4)
    z_at = (z, ring(z + 7, 8), ring(z + 1, 8), ring(z + jnp.where(lax.rem(z, 2) == 0, 2, 6), 8))
    low_j = [low_block(info_ref, device_row(y_at, ring(z + 4 * j, 8), x))[0] for j in range(2)]

    def keys(at):
        return jnp.concatenate([y_ref[j, at : at + BLK, :] for j in range(2)], 0)

    k_low, k_high, v_low, v_high = (keys(b * BLK) for b in range(4))
    kt_low, kt_high = k_low.T, k_high.T

    def add(at, dv, dk, fresh):
        rows = slice(at, at + 2 * BLK)
        dv_acc[rows] = dv if fresh else dv_acc[rows] + dv
        dk_acc[rows] = dk if fresh else dk_acc[rows] + dk

    for pair in range(2):
        chunks = [(s, a) for s in (2 * pair, 2 * pair + 1) for a in range(2)]

        def rows(at):
            return jnp.concatenate([q_refs[s][a, at : at + BLK, :] for s, a in chunks], 0)

        stats = [q_refs[s][a, 4 * BLK :, :].astype(F32) for s, a in chunks]
        lse_low, lse_high, delta_low, delta_high = (
            jnp.concatenate([st[r : r + 1, :] for st in stats], 1) * (LOG2E if r < 2 else 1.0) for r in range(4)
        )
        low_i = [low_block(info_ref, device_row(y, z_at[s], 1 - x if a else x))[0] for s, a in chunks]
        own = turn == 0 and pair == 0

        def hide(j, low):
            parts = []
            for n, li in enumerate(low_i):
                seen = low_j[j] < li if low else li < low_j[j]
                hidden = jnp.float32(0.0) if own and n == 0 and j == 0 else jnp.where(seen, 0.0, HIDE)
                parts.append(jnp.full((1, BLK), hidden, F32))
            return jnp.concatenate(parts, 1)

        q_low, q_high, g_low, g_high = (rows(b * BLK) for b in range(4))
        fresh = pair == 0
        dv, dk, dq_high = tile(k_low, v_low, kt_low, q_high, g_high, [lse_high] * 2, delta_high)
        add(0, dv, dk, fresh)
        lses = [lse_high + hide(j, False) for j in range(2)]
        dv, dk, more = tile(k_high, v_high, kt_high, q_high, g_high, lses, delta_high, own)
        add(2 * BLK, dv, dk, fresh)
        dq_high += more
        lses = [lse_low + hide(j, True) for j in range(2)]
        dv, dk, dq_low = tile(k_low, v_low, kt_low, q_low, g_low, lses, delta_low, own)
        add(0, dv, dk, False)
        columns = slice(pair * 4 * BLK, (pair + 1) * 4 * BLK)
        for b, dq in ((0, dq_low), (1, dq_high)):
            if turn > 0:
                dq = dqin_ref[b, :, columns] + dq
            if turn < 3:
                dq_ref[b, :, columns] = dq
            else:
                for n, (s, a) in enumerate(chunks):
                    ref = dq_refs[s]
                    ref[a, b * BLK : (b + 1) * BLK, :] = dq[:, n * BLK : (n + 1) * BLK].T.astype(ref.dtype)

    for j in range(2):
        for b in range(2):
            source = slice((2 * b + j) * BLK, (2 * b + j + 1) * BLK)
            dkv_ref[j, b * BLK : (b + 1) * BLK, :] = dk_acc[source].astype(dkv_ref.dtype)
            dkv_ref[j, (2 + b) * BLK : (3 + b) * BLK, :] = dv_acc[source].astype(dkv_ref.dtype)
    if turn == 3:
        sum_ref[...] = kept_ref[...] + back_ref[...].astype(F32)


def meet_kernel(own_ref, *refs):
    *back_refs, keep_ref, send_ref = refs
    for part, out_ref in ((0, keep_ref), (1, send_ref)):
        total = own_ref[part]
        for ref in back_refs:
            total += ref[part].astype(F32)
        out_ref[...] = total.astype(out_ref.dtype)


def last_kernel(info_ref, dq_ref, dqx_ref, dkv_ref, dkvz_ref, q_ref, k_ref, v_ref):
    _, swapped = low_block(info_ref, device_row(*place(info_ref)))
    for part in range(2):
        to = pl.multiple_of(jnp.where(swapped, (1 - part) * BLK, part * BLK), BLK)
        at = part * BLK

        def total(ref, other, start):
            return ref[start : start + BLK, :] + other[start : start + BLK, :].astype(F32)

        q_ref[pl.ds(to, BLK), :] = (total(dq_ref, dqx_ref, at) * FACTOR).astype(BF16)
        k_ref[pl.ds(to, BLK), :] = (total(dkv_ref, dkvz_ref, at) * FACTOR).astype(BF16)
        v_ref[pl.ds(to, BLK), :] = total(dkv_ref, dkvz_ref, 2 * BLK + at).astype(BF16)


def z_step(step):
    return [(i, (i + step) % 8) for i in range(8)]


def y_step(step):
    return [(i, (i + step) % 4) for i in range(4)]


Z_PAIRS = [(i, (i - 2) % 8 if i % 2 == 0 else (i + 2) % 8) for i in range(8)]
Z_BACK = [(b, a) for a, b in Z_PAIRS]
X_SWAP = [(0, 1), (1, 0)]


def call(kernel, outs, operands, info=None, scratch=(), in_specs=None, vmem_limit=VMEM_LIMIT, **options):
    smem = pl.BlockSpec(memory_space=pltpu.SMEM)
    vmem = pl.BlockSpec(memory_space=pltpu.VMEM)
    scalars = [] if info is None else [info]
    return pl.pallas_call(
        kernel,
        out_shape=[jax.ShapeDtypeStruct(s, t) for s, t in outs],
        in_specs=[smem] * len(scalars) + (in_specs or [vmem] * len(operands)),
        out_specs=[vmem] * len(outs),
        scratch_shapes=list(scratch),
        compiler_params=pltpu.CompilerParams(vmem_limit_bytes=vmem_limit),
        **options,
    )(*scalars, *operands)


def body(queries, key_rows, value_rows, outputs, out_grad, saved_lse, fold_map):
    where = jnp.stack([lax.axis_index(name) for name in ("pb", "kz", "kx")]).astype(jnp.int32)
    info = jnp.concatenate([fold_map, where])
    operands = (fold_map, queries, key_rows, value_rows, outputs, out_grad, saved_lse.T)
    mine_q, mine_k = call(
        prep_kernel,
        [((Q_ROWS, DIM), BF16), ((K_ROWS, DIM), BF16)],
        operands,
        where,
        [pltpu.SMEM(a.shape, a.dtype) if a is fold_map else pltpu.VMEM(a.shape, a.dtype) for a in operands]
        + [pltpu.SemaphoreType.DMA((len(operands),))],
        in_specs=[pl.BlockSpec(memory_space=pltpu.HBM)] * len(operands),
        vmem_limit=PREP_VMEM,
    )
    q0 = jnp.stack([mine_q, lax.ppermute(mine_q, "kx", X_SWAP)])
    k0 = jnp.stack([mine_k, lax.ppermute(mine_k, "kz", z_step(4))])
    q_sets = [q0] + [lax.ppermute(q0, "kz", p) for p in (z_step(1), z_step(-1), Z_PAIRS)]
    k_sets = [k0] + [lax.ppermute(k0, "pb", y_step(-s)) for s in Y_FROM[1:]]

    acc = pltpu.VMEM((4 * BLK, DIM), F32)
    dq_acc = ((2, DIM, 8 * BLK), F32)
    dkv_acc = ((2, K_ROWS, DIM), F32)
    cost = pl.CostEstimate(flops=16 * 2 * 5 * 4 * BLK**3 // 2, bytes_accessed=1 << 20, transcendentals=0)
    back = []
    for turn in range(4):
        operands = q_sets + [k_sets[turn]] + ([dq] if turn else [])
        outs = [dq_acc, dkv_acc if turn == 0 else ((2, K_ROWS, DIM), BF16)]
        options = dict(input_output_aliases={6: 0}) if turn else {}
        if turn == 3:
            operands += [kept, back[0]]
            outs = [((2, 2 * BLK, DIM), F32 if s == 0 else BF16) for s in range(4)] + [outs[1], dkv_acc]
            options = {}
        kernel = functools.partial(grad_kernel, turn)
        *dq, part = call(kernel, outs, operands, info, [acc, acc], cost_estimate=cost, **options)
        if turn == 0:
            (dq,), kept = dq, part
        elif turn < 3:
            (dq,) = dq
            back.append(lax.ppermute(part, "pb", y_step(Y_FROM[turn])))
        else:
            *dq, last = dq
            kept = part
            back.append(lax.ppermute(last, "pb", y_step(Y_FROM[turn])))
    dq_back = [lax.ppermute(dq[t], "kz", p) for t, p in ((1, z_step(-1)), (2, z_step(1)), (3, Z_BACK))]

    def meet(own, partners):
        shape = own.shape[1:]
        return call(meet_kernel, [(shape, F32), (shape, BF16)], [own] + partners)

    dkv_keep, dkv_send = meet(kept, back[1:])
    dkv_last = lax.ppermute(dkv_send, "kz", z_step(4))
    dq_keep, dq_send = meet(dq[0], dq_back)
    dq_last = lax.ppermute(dq_send, "kx", X_SWAP)
    grads = [((2 * BLK, DIM), BF16)] * 3
    return tuple(call(last_kernel, grads, (dq_keep, dq_last, dkv_keep, dkv_last), info))


def solution(mesh):
    fine = Mesh(mesh.devices.reshape(4, 8, 2, 2, 2), ("pb", "kz", "kx", "hx", "hc"))
    rows = P(("pb", "kz", "kx"), ("hx", "hc"))
    return jax.shard_map(
        body,
        mesh=fine,
        in_specs=(rows,) * 6 + (P(),),
        out_specs=(rows,) * 3,
        check_vma=False,
    )
```

```python
import functools
import math

import jax
import jax.numpy as jnp
from jax import lax
from jax.experimental import pallas as pl
from jax.experimental.pallas import tpu as pltpu
from jax.sharding import Mesh, PartitionSpec as P

F32 = jnp.float32
BF16 = jnp.bfloat16
BLK = 128
DIM = 128
LOG2E = math.log2(math.e)
FACTOR = 1.0 / math.sqrt(DIM)
VMEM_LIMIT = 48 * 1024 * 1024
PREP_VMEM = 62 * 1024 * 1024
BLOCKS = 128
HIDE = 1e30
Y_FROM = (0, 2, 3, 1)
NT = (((1,), (1,)), ((), ()))
Q_ROWS = 4 * BLK + 16
K_ROWS = 4 * BLK


def dot(a, b):
    return jnp.dot(a, b, preferred_element_type=F32)


def dot_nt(a, b):
    return lax.dot_general(a, b, NT, preferred_element_type=F32)


def ring(value, size):
    return lax.rem(value + size, size)


def low_block(fold_ref, device):
    first = fold_ref[2 * device]
    second = fold_ref[2 * device + 1]
    return jnp.minimum(first, second), second < first


def place(info_ref):
    return info_ref[BLOCKS], info_ref[BLOCKS + 1], info_ref[BLOCKS + 2]


def device_row(y, z, x):
    return y * 16 + z * 2 + x


def prep_kernel(where_ref, *refs):
    sources, (zout_ref, kout_ref), buffers, sems = refs[:7], refs[7:9], refs[9:16], refs[16]
    copies = [pltpu.make_async_copy(s, b, sems.at[n]) for n, (s, b) in enumerate(zip(sources, buffers))]
    for copy in copies:
        copy.start()
    for copy in copies:
        copy.wait()
    fold_ref, q_ref, k_ref, v_ref, o_ref, g_ref, lse_ref = buffers
    _, swapped = low_block(fold_ref, device_row(where_ref[0], where_ref[1], where_ref[2]))
    low = pl.multiple_of(jnp.where(swapped, BLK, 0), BLK)
    high = pl.multiple_of(jnp.where(swapped, 0, BLK), BLK)
    lse = lse_ref[...].astype(F32)
    halves = (lse[:, :BLK], lse[:, BLK:])
    rows = [jnp.where(swapped, halves[1], halves[0]), jnp.where(swapped, halves[0], halves[1])]
    for start in (low, high):
        prod = g_ref[pl.ds(start, BLK), :].astype(F32) * o_ref[pl.ds(start, BLK), :].astype(F32)
        rows.append(jnp.sum(prod.T, axis=0, keepdims=True))
    zout_ref[4 * BLK :, :] = jnp.concatenate(rows + [jnp.zeros((12, DIM), F32)], axis=0).astype(BF16)
    for out_ref, at, ref in (
        (zout_ref, 0, q_ref),
        (zout_ref, 2 * BLK, g_ref),
        (kout_ref, 0, k_ref),
        (kout_ref, 2 * BLK, v_ref),
    ):
        out_ref[at : at + BLK, :] = ref[pl.ds(low, BLK), :]
        out_ref[at + BLK : at + 2 * BLK, :] = ref[pl.ds(high, BLK), :]


def tile(k, v, kt, q, g, lses, delta, diagonal=False):
    s = dot_nt(k, q)
    probs = []
    for b, lse in enumerate(lses):
        p = jnp.exp2(s[b * BLK : (b + 1) * BLK] * (FACTOR * LOG2E) - lse)
        if diagonal and b == 0:
            shape = (BLK, BLK)
            seen = lax.broadcasted_iota(jnp.int32, shape, 0) <= lax.broadcasted_iota(jnp.int32, shape, 1)
            p = jnp.concatenate([jnp.where(seen, p[:, :BLK], 0.0), p[:, BLK:]], 1)
        probs.append(p)
    p = jnp.concatenate(probs, 0)
    dp = dot_nt(v, g)
    ds = (p * (dp - delta)).astype(BF16)
    return dot(p.astype(BF16), g), dot(ds, q), dot(kt, ds)


def grad_kernel(turn, groups, first, ends, info_ref, *refs):
    refs = list(refs)

    def take(count):
        taken = refs[:count]
        del refs[:count]
        return taken

    q_refs, (y_ref,) = take(len(groups)), take(1)
    dqin_refs = take(0 if first else len(groups))
    (dkvin_ref,) = take(1) if ends == "close" else (None,)
    kept_ref, back_ref = take(2) if ends == "last" else (None, None)
    dq_refs, (dkv_ref,) = take(len(groups)), take(1)
    (sum_ref,) = take(1) if ends == "last" else (None,)
    dv_acc, dk_acc = refs
    y, z, x = place(info_ref)
    y_at = ring(y + Y_FROM[turn], 4)
    z_at = (z, ring(z + 7, 8), ring(z + 1, 8), ring(z + jnp.where(lax.rem(z, 2) == 0, 2, 6), 8))
    low_j = [low_block(info_ref, device_row(y_at, ring(z + 4 * j, 8), x))[0] for j in range(2)]

    def keys(at):
        return jnp.concatenate([y_ref[j, at : at + BLK, :] for j in range(2)], 0)

    k_low, k_high, v_low, v_high = (keys(b * BLK) for b in range(4))
    kt_low, kt_high = k_low.T, k_high.T

    def add(at, dv, dk, fresh):
        rows = slice(at, at + 2 * BLK)
        dv_acc[rows] = dv if fresh else dv_acc[rows] + dv
        dk_acc[rows] = dk if fresh else dk_acc[rows] + dk

    for turn_at, (group, q_ref) in enumerate(zip(groups, q_refs)):

        def rows(at):
            return jnp.concatenate([q_ref[s, at : at + BLK, :] for s in range(4)], 0)

        stats = [q_ref[s, 4 * BLK :, :].astype(F32) for s in range(4)]
        lse_low, lse_high, delta_low, delta_high = (
            jnp.concatenate([st[r : r + 1, :] for st in stats], 1) * (LOG2E if r < 2 else 1.0) for r in range(4)
        )
        low_i = [low_block(info_ref, device_row(y, z_at[s], 1 - x if group else x))[0] for s in range(4)]
        own = turn == 0 and group == 0

        def hide(j, low):
            parts = []
            for n, li in enumerate(low_i):
                seen = low_j[j] < li if low else li < low_j[j]
                hidden = jnp.float32(0.0) if own and n == 0 and j == 0 else jnp.where(seen, 0.0, HIDE)
                parts.append(jnp.full((1, BLK), hidden, F32))
            return jnp.concatenate(parts, 1)

        q_low, q_high, g_low, g_high = (rows(b * BLK) for b in range(4))
        fresh = turn_at == 0
        dv, dk, dq_high = tile(k_low, v_low, kt_low, q_high, g_high, [lse_high] * 2, delta_high)
        add(0, dv, dk, fresh)
        lses = [lse_high + hide(j, False) for j in range(2)]
        dv, dk, more = tile(k_high, v_high, kt_high, q_high, g_high, lses, delta_high, own)
        add(2 * BLK, dv, dk, fresh)
        dq_high += more
        lses = [lse_low + hide(j, True) for j in range(2)]
        dv, dk, dq_low = tile(k_low, v_low, kt_low, q_low, g_low, lses, delta_low, own)
        add(0, dv, dk, False)
        ref = dq_refs[turn_at]
        for b, dq in ((0, dq_low), (1, dq_high)):
            if not first:
                dq = dqin_refs[turn_at][b] + dq
            if ends == "last":
                for s in range(4):
                    ref[s, b * BLK : (b + 1) * BLK, :] = dq[:, s * BLK : (s + 1) * BLK].T.astype(ref.dtype)
            else:
                ref[b] = dq

    for j in range(2):
        for b in range(2):
            source = slice((2 * b + j) * BLK, (2 * b + j + 1) * BLK)
            for at, part in ((b, dk_acc[source]), (2 + b, dv_acc[source])):
                rows = slice(at * BLK, (at + 1) * BLK)
                if ends == "close":
                    part = dkvin_ref[j, rows, :] + part
                dkv_ref[j, rows, :] = part.astype(dkv_ref.dtype)
    if ends == "last":
        sum_ref[...] = kept_ref[...] + back_ref[...].astype(F32)


def meet_kernel(own_ref, *refs):
    *back_refs, keep_ref, send_ref = refs
    for part, out_ref in ((0, keep_ref), (1, send_ref)):
        total = own_ref[part]
        for ref in back_refs:
            total += ref[part].astype(F32)
        out_ref[...] = total.astype(out_ref.dtype)


def cross_kernel(own_ref, back_ref, keep_ref, *send_refs):
    for s, out_ref in enumerate((keep_ref, *send_refs)):
        out_ref[...] = (own_ref[s] + back_ref[s].astype(F32)).astype(out_ref.dtype)


def last_kernel(info_ref, dq_ref, dqa_ref, dqb_ref, dqc_ref, dkv_ref, dkvz_ref, q_ref, k_ref, v_ref):
    _, swapped = low_block(info_ref, device_row(*place(info_ref)))
    for part in range(2):
        to = pl.multiple_of(jnp.where(swapped, (1 - part) * BLK, part * BLK), BLK)

        def total(ref, others, at):
            out = ref[at : at + BLK, :]
            for other in others:
                out += other[at : at + BLK, :].astype(F32)
            return out

        q_ref[pl.ds(to, BLK), :] = (total(dq_ref, (dqa_ref, dqb_ref, dqc_ref), part * BLK) * FACTOR).astype(BF16)
        k_ref[pl.ds(to, BLK), :] = (total(dkv_ref, (dkvz_ref,), part * BLK) * FACTOR).astype(BF16)
        v_ref[pl.ds(to, BLK), :] = total(dkv_ref, (dkvz_ref,), (2 + part) * BLK).astype(BF16)


def z_step(step):
    return [(i, (i + step) % 8) for i in range(8)]


def y_step(step):
    return [(i, (i + step) % 4) for i in range(4)]


Z_PAIRS = [(i, (i - 2) % 8 if i % 2 == 0 else (i + 2) % 8) for i in range(8)]
Z_BACK = [(b, a) for a, b in Z_PAIRS]
X_SWAP = [(0, 1), (1, 0)]


def call(kernel, outs, operands, info=None, scratch=(), in_specs=None, vmem_limit=VMEM_LIMIT, **options):
    smem = pl.BlockSpec(memory_space=pltpu.SMEM)
    vmem = pl.BlockSpec(memory_space=pltpu.VMEM)
    scalars = [] if info is None else [info]
    return pl.pallas_call(
        kernel,
        out_shape=[jax.ShapeDtypeStruct(s, t) for s, t in outs],
        in_specs=[smem] * len(scalars) + (in_specs or [vmem] * len(operands)),
        out_specs=[vmem] * len(outs),
        scratch_shapes=list(scratch),
        compiler_params=pltpu.CompilerParams(vmem_limit_bytes=vmem_limit),
        **options,
    )(*scalars, *operands)


def body(queries, key_rows, value_rows, outputs, out_grad, saved_lse, fold_map):
    where = jnp.stack([lax.axis_index(name) for name in ("pb", "kz", "kx")]).astype(jnp.int32)
    info = jnp.concatenate([fold_map, where])
    operands = (fold_map, queries, key_rows, value_rows, outputs, out_grad, saved_lse.T)
    mine_q, mine_k = call(
        prep_kernel,
        [((Q_ROWS, DIM), BF16), ((K_ROWS, DIM), BF16)],
        operands,
        where,
        [pltpu.SMEM(a.shape, a.dtype) if a is fold_map else pltpu.VMEM(a.shape, a.dtype) for a in operands]
        + [pltpu.SemaphoreType.DMA((len(operands),))],
        in_specs=[pl.BlockSpec(memory_space=pltpu.HBM)] * len(operands),
        vmem_limit=PREP_VMEM,
    )
    other_k = lax.ppermute(mine_k, "kz", z_step(4))
    arrived = [lax.ppermute(mine_q, "kz", p) for p in (z_step(1), z_step(-1), Z_PAIRS)]
    q_mine = jnp.pad(mine_q[None], ((0, 3), (0, 0), (0, 0)))
    for s, part in enumerate(arrived):
        q_mine = lax.dynamic_update_slice(q_mine, part[None], (s + 1, 0, 0))
    q_mine, other_k = lax.optimization_barrier((q_mine, other_k))
    k0 = jnp.stack([mine_k, other_k])
    q_sets = [q_mine, lax.ppermute(q_mine, "kx", X_SWAP)]
    k_sets = [k0] + [lax.ppermute(k0, "pb", y_step(-s)) for s in Y_FROM[1:]]

    acc = pltpu.VMEM((4 * BLK, DIM), F32)
    dq_acc = ((2, DIM, 4 * BLK), F32)
    dkv_acc = ((2, K_ROWS, DIM), F32)
    dkv_out = ((2, K_ROWS, DIM), BF16)

    def grad(turn, groups, first, ends, operands, outs):
        flops = 10 * len(groups) * 3 * (2 * BLK) * (4 * BLK) * DIM
        return call(
            functools.partial(grad_kernel, turn, groups, first, ends),
            outs,
            [q_sets[g] for g in groups] + [k_sets[turn]] + operands,
            info,
            [acc, acc],
            cost_estimate=pl.CostEstimate(flops=flops, bytes_accessed=1 << 20, transcendentals=0),
        )

    def send_back(turn, part):
        return lax.ppermute(part, "pb", y_step(Y_FROM[turn]))

    dq0, kept = grad(0, (0,), True, "", [], [dq_acc, dkv_acc])
    dq1, kept = grad(0, (1,), True, "close", [kept], [dq_acc, dkv_acc])
    *dqs, part = grad(1, (0, 1), False, "", [dq0, dq1], [dq_acc, dq_acc, dkv_out])
    back1 = send_back(1, part)
    *dqs, part = grad(2, (0, 1), False, "", dqs, [dq_acc, dq_acc, dkv_out])
    back2 = send_back(2, part)
    dq_out = (4, 2 * BLK, DIM)
    dq_keep, dq_send, part, kept = grad(
        3, (0, 1), False, "last", dqs + [kept, back1], [(dq_out, F32), (dq_out, BF16), dkv_out, dkv_acc]
    )
    back3 = send_back(3, part)
    dq_back = lax.ppermute(dq_send, "kx", X_SWAP)
    chunk = (2 * BLK, DIM)
    dq_keep, *dq_send = call(cross_kernel, [(chunk, F32)] + [(chunk, BF16)] * 3, (dq_keep, dq_back))
    dq_back = [lax.ppermute(d, "kz", p) for d, p in zip(dq_send, (z_step(-1), z_step(1), Z_BACK))]
    shape = (K_ROWS, DIM)
    dkv_keep, dkv_send = call(meet_kernel, [(shape, F32), (shape, BF16)], [kept, back2, back3])
    dkv_back = lax.ppermute(dkv_send, "kz", z_step(4))
    return tuple(call(last_kernel, [(chunk, BF16)] * 3, (dq_keep, *dq_back, dkv_keep, dkv_back), info))


def solution(mesh):
    fine = Mesh(mesh.devices.reshape(4, 8, 2, 2, 2), ("pb", "kz", "kx", "hx", "hc"))
    rows = P(("pb", "kz", "kx"), ("hx", "hc"))
    return jax.shard_map(
        body,
        mesh=fine,
        in_specs=(rows,) * 6 + (P(),),
        out_specs=(rows,) * 3,
        check_vma=False,
    )
```

```python
import functools
import math

import jax
import jax.numpy as jnp
from jax import lax
from jax.experimental import pallas as pl
from jax.experimental.pallas import tpu as pltpu
from jax.sharding import Mesh, PartitionSpec as P

F32 = jnp.float32
BF16 = jnp.bfloat16
BLK = 128
DIM = 128
LOG2E = math.log2(math.e)
FACTOR = 1.0 / math.sqrt(DIM)
VMEM_LIMIT = 48 * 1024 * 1024
PREP_VMEM = 62 * 1024 * 1024
FLOPS = 10 * 2 * 3 * (2 * BLK) * (4 * BLK) * DIM
HIDE = 1e30
Y_FROM = (0, 2, 3, 1)
NT = (((1,), (1,)), ((), ()))
Q_ROWS = 4 * BLK + 16
K_ROWS = 4 * BLK


def dot(a, b):
    return jnp.dot(a, b, preferred_element_type=F32)


def dot_nt(a, b):
    return lax.dot_general(a, b, NT, preferred_element_type=F32)


def ring(value, size):
    return lax.rem(value + size, size)


def blocks(fold_ref, y, z, x):
    device = y * 16 + z * 2 + x
    first = fold_ref[2 * device]
    second = fold_ref[2 * device + 1]
    low = pl.multiple_of(jnp.where(second < first, BLK, 0), BLK)
    high = pl.multiple_of(jnp.where(second < first, 0, BLK), BLK)
    return jnp.minimum(first, second), (low, high)


def prep_kernel(q_ref, k_ref, v_ref, o_ref, g_ref, lse_ref, qout_ref, kout_ref, g_buf, o_buf, lse_buf, stats_buf, sems):
    half = 2 * BLK
    loads = [
        pltpu.make_async_copy(s, d, sems.at[n])
        for n, (s, d) in enumerate(((g_ref, g_buf), (o_ref, o_buf), (lse_ref, lse_buf)))
    ]
    moves = [
        pltpu.make_async_copy(s, d, sems.at[3 + n])
        for n, (s, d) in enumerate(
            (
                (q_ref, qout_ref.at[:half]),
                (g_ref, qout_ref.at[half : 2 * half]),
                (k_ref, kout_ref.at[:half]),
                (v_ref, kout_ref.at[half:]),
            )
        )
    ]
    for copy in loads + moves:
        copy.start()
    for copy in loads:
        copy.wait()
    lse = lse_buf[...].astype(F32)
    rows = [lse[:, :BLK], lse[:, BLK:]]
    for start in (0, BLK):
        prod = g_buf[start : start + BLK, :].astype(F32) * o_buf[start : start + BLK, :].astype(F32)
        rows.append(jnp.sum(prod.T, axis=0, keepdims=True))
    stats_buf[...] = jnp.concatenate(rows + [jnp.zeros((12, DIM), F32)], axis=0).astype(BF16)
    moves.append(pltpu.make_async_copy(stats_buf, qout_ref.at[2 * half :], sems.at[7]))
    moves[-1].start()
    for copy in moves:
        copy.wait()


def tile(k, v, kt, q, g, lses, delta, diagonal=None):
    s = dot_nt(k, q)
    probs = []
    for b, lse in enumerate(lses):
        p = jnp.exp2(s[b * BLK : (b + 1) * BLK] * (FACTOR * LOG2E) - lse)
        if b == diagonal:
            shape = (BLK, BLK)
            seen = lax.broadcasted_iota(jnp.int32, shape, 0) <= lax.broadcasted_iota(jnp.int32, shape, 1)
            p = jnp.concatenate([jnp.where(seen, p[:, :BLK], 0.0), p[:, BLK:]], 1)
        probs.append(p)
    p = jnp.concatenate(probs, 0)
    dp = dot_nt(v, g)
    ds = (p * (dp - delta)).astype(BF16)
    return dot(p.astype(BF16), g), dot(ds, q), dot(kt, ds)


def grad_kernel(turn, js, first, final, fold_ref, *refs):
    q_refs, y_ref, refs = refs[:4], refs[4], refs[5:]
    if not first:
        dqin_ref, refs = refs[0], refs[1:]
    if final:
        dq_refs, (dkv_ref, dv_acc, dk_acc) = refs[:4], refs[4:]
    else:
        dq_ref, dkv_ref, dv_acc, dk_acc = refs
    y, z, x = (lax.axis_index(name) for name in ("pb", "kz", "kx"))
    y_at = ring(y + Y_FROM[turn], 4)
    z_at = (z, ring(z + 7, 8), ring(z + 1, 8), ring(z + jnp.where(lax.rem(z, 2) == 0, 2, 6), 8))
    low_j, starts_j = zip(*(blocks(fold_ref, y_at, ring(z + 4 * j, 8), x) for j in js))
    count = len(js)
    half = count * BLK

    def keys(array):
        parts = [
            y_ref[n, pl.ds(array * 2 * BLK + starts_j[n][b], BLK), :] for b in range(2) for n in range(count)
        ]
        return jnp.concatenate(parts, 0)

    k, v = keys(0), keys(1)
    kt = k.T

    for pair in range(2):
        chunks = [(s, a) for s in (2 * pair, 2 * pair + 1) for a in range(2)]
        low_i, starts_i = zip(*(blocks(fold_ref, y, z_at[s], 1 - x if a else x) for s, a in chunks))

        def queries(array, b):
            parts = [q_refs[s][a, pl.ds(array * 2 * BLK + at[b], BLK), :] for (s, a), at in zip(chunks, starts_i)]
            return jnp.concatenate(parts, 0)

        def stats(row, scale):
            low, high = [], []
            for (s, a), at in zip(chunks, starts_i):
                both = q_refs[s][a, 4 * BLK :, :].astype(F32)
                upper, lower = both[row : row + 1, :], both[row + 1 : row + 2, :]
                low.append(jnp.where(at[0] == 0, upper, lower) * scale)
                high.append(jnp.where(at[0] == 0, lower, upper) * scale)
            return jnp.concatenate(low, 1), jnp.concatenate(high, 1)

        lse_low, lse_high = stats(0, LOG2E)
        delta_low, delta_high = stats(2, 1.0)
        own = turn == 0 and js[0] == 0 and pair == 0

        def hide(m, low):
            parts = []
            for n, li in enumerate(low_i):
                seen = low_j[m] < li if low else li < low_j[m]
                hidden = jnp.float32(0.0) if own and n == 0 and m == 0 else jnp.where(seen, 0.0, HIDE)
                parts.append(jnp.full((1, BLK), hidden, F32))
            return jnp.concatenate(parts, 1)

        lses = [lse_high] * count + [lse_high + hide(m, False) for m in range(count)]
        dv, dk, dq_high = tile(
            k, v, kt, queries(0, 1), queries(1, 1), lses, delta_high, count if own else None
        )
        dv_acc[...] = dv if pair == 0 else dv_acc[...] + dv
        dk_acc[...] = dk if pair == 0 else dk_acc[...] + dk
        lses = [lse_low + hide(m, True) for m in range(count)]
        dv, dk, dq_low = tile(
            k[:half], v[:half], kt[:, :half], queries(0, 0), queries(1, 0), lses, delta_low, 0 if own else None
        )
        dv_acc[:half] += dv
        dk_acc[:half] += dk
        columns = slice(pair * 4 * BLK, (pair + 1) * 4 * BLK)
        for b, dq in ((0, dq_low), (1, dq_high)):
            if not first:
                dq = dqin_ref[b, :, columns] + dq
            if not final:
                dq_ref[b, :, columns] = dq
            else:
                for n, (s, a) in enumerate(chunks):
                    ref = dq_refs[s]
                    ref[a, pl.ds(starts_i[n][b], BLK), :] = dq[:, n * BLK : (n + 1) * BLK].T.astype(ref.dtype)

    for n in range(count):
        for b in range(2):
            source = slice(b * half + n * BLK, b * half + (n + 1) * BLK)
            at = starts_j[n][b]
            dkv_ref[n, pl.ds(at, BLK), :] = dk_acc[source].astype(dkv_ref.dtype)
            dkv_ref[n, pl.ds(2 * BLK + at, BLK), :] = dv_acc[source].astype(dkv_ref.dtype)


def meet_kernel(own_ref, other_ref, *refs):
    *back_refs, keep_ref, send_ref = refs
    for part, (start_ref, out_ref) in enumerate(((own_ref, keep_ref), (other_ref, send_ref))):
        total = start_ref[...]
        for ref in back_refs:
            total += ref[part].astype(F32)
        out_ref[...] = total.astype(out_ref.dtype)


def last_kernel(dq_ref, dqx_ref, dkv_ref, dkvz_ref, q_ref, k_ref, v_ref):
    q_ref[...] = ((dq_ref[...] + dqx_ref[...].astype(F32)) * FACTOR).astype(BF16)
    dkv = dkv_ref[...] + dkvz_ref[...].astype(F32)
    k_ref[...] = (dkv[: 2 * BLK] * FACTOR).astype(BF16)
    v_ref[...] = dkv[2 * BLK :].astype(BF16)


def z_step(step):
    return [(i, (i + step) % 8) for i in range(8)]


def y_step(step):
    return [(i, (i + step) % 4) for i in range(4)]


Z_PAIRS = [(i, (i - 2) % 8 if i % 2 == 0 else (i + 2) % 8) for i in range(8)]
Z_BACK = [(b, a) for a, b in Z_PAIRS]
X_SWAP = [(0, 1), (1, 0)]


def call(kernel, outs, operands, fold=None, scratch=(), in_specs=None, vmem_limit=VMEM_LIMIT, **options):
    smem = pl.BlockSpec(memory_space=pltpu.SMEM)
    vmem = pl.BlockSpec(memory_space=pltpu.VMEM)
    scalars = [] if fold is None else [fold]
    return pl.pallas_call(
        kernel,
        out_shape=[jax.ShapeDtypeStruct(s, t) for s, t in outs],
        in_specs=[smem] * len(scalars) + (in_specs or [vmem] * len(operands)),
        out_specs=[pl.BlockSpec(memory_space=pltpu.HBM) if in_specs else vmem] * len(outs),
        scratch_shapes=list(scratch),
        compiler_params=pltpu.CompilerParams(vmem_limit_bytes=vmem_limit),
        **options,
    )(*scalars, *operands)


def body(queries, key_rows, value_rows, outputs, out_grad, saved_lse, fold_map):
    operands = (queries, key_rows, value_rows, outputs, out_grad, saved_lse.T)
    rows = pltpu.VMEM((2 * BLK, DIM), BF16)
    mine_q, mine_k = call(
        prep_kernel,
        [((Q_ROWS, DIM), BF16), ((K_ROWS, DIM), BF16)],
        operands,
        scratch=[
            rows,
            rows,
            pltpu.VMEM((1, 2 * BLK), BF16),
            pltpu.VMEM((Q_ROWS - 4 * BLK, DIM), BF16),
            pltpu.SemaphoreType.DMA((8,)),
        ],
        in_specs=[pl.BlockSpec(memory_space=pltpu.HBM)] * len(operands),
        vmem_limit=PREP_VMEM,
    )
    other_k = lax.ppermute(mine_k, "kz", z_step(4))
    q0 = jnp.stack([mine_q, lax.ppermute(mine_q, "kx", X_SWAP)])
    _, other_k = lax.optimization_barrier((q0, other_k))
    k0 = jnp.stack([mine_k, other_k])
    q_sets = [q0] + [lax.ppermute(q0, "kz", p) for p in (z_step(1), z_step(-1), Z_PAIRS)]
    k_sets = [k0] + [lax.ppermute(k0, "pb", y_step(-s)) for s in Y_FROM[1:]]

    dq = []
    dkv = {}
    order = ((0, (0,)), (1, (0, 1)), (2, (0, 1)), (3, (0, 1)), (0, (1,)))
    for turn, js in order:
        first, final = (turn, js) == order[0], (turn, js) == order[-1]
        key_set = (mine_k, other_k)[js[0]][None] if turn == 0 else k_sets[turn]
        outs = [((2, DIM, 8 * BLK), F32)]
        if final:
            outs = [((2, 2 * BLK, DIM), F32 if s == 0 else BF16) for s in range(4)]
        acc = pltpu.VMEM((2 * len(js) * BLK, DIM), F32)
        *dq, part = call(
            functools.partial(grad_kernel, turn, js, first, final),
            outs + [((len(js), K_ROWS, DIM), BF16 if turn else F32)],
            q_sets + [key_set] + ([] if first else dq),
            fold_map,
            [acc, acc],
            cost_estimate=pl.CostEstimate(flops=FLOPS * len(js) // 2, bytes_accessed=1 << 20, transcendentals=0),
            input_output_aliases={} if first or final else {6: 0},
        )
        dkv[turn, js] = lax.ppermute(part, "pb", y_step(Y_FROM[turn])) if turn else part[0]
    dq_back = [lax.ppermute(dq[t], "kz", p) for t, p in ((1, z_step(-1)), (2, z_step(1)), (3, Z_BACK))]

    def meet(own, other, partners):
        return call(meet_kernel, [(own.shape, F32), (own.shape, BF16)], [own, other] + partners)

    dkv_keep, dkv_send = meet(dkv[0, (0,)], dkv[0, (1,)], [dkv[t, (0, 1)] for t in (1, 2, 3)])
    dkv_last = lax.ppermute(dkv_send, "kz", z_step(4))
    dq_keep, dq_send = meet(dq[0][0], dq[0][1], dq_back)
    dq_last = lax.ppermute(dq_send, "kx", X_SWAP)
    return tuple(call(last_kernel, [((2 * BLK, DIM), BF16)] * 3, (dq_keep, dq_last, dkv_keep, dkv_last)))


def solution(mesh):
    fine = Mesh(mesh.devices.reshape(4, 8, 2, 2, 2), ("pb", "kz", "kx", "hx", "hc"))
    rows = P(("pb", "kz", "kx"), ("hx", "hc"))
    return jax.shard_map(
        body,
        mesh=fine,
        in_specs=(rows,) * 6 + (P(),),
        out_specs=(rows,) * 3,
        check_vma=False,
    )
```

```python
import functools
import math

import jax
import jax.numpy as jnp
from jax import lax
from jax.experimental import pallas as pl
from jax.experimental.pallas import tpu as pltpu
from jax.sharding import Mesh, PartitionSpec as P

F32 = jnp.float32
BF16 = jnp.bfloat16
BLK = 128
DIM = 128
LOG2E = math.log2(math.e)
FACTOR = 1.0 / math.sqrt(DIM)
VMEM_LIMIT = 48 * 1024 * 1024
PREP_VMEM = 62 * 1024 * 1024
FLOPS = 10 * 2 * 3 * (2 * BLK) * (4 * BLK) * DIM
HIDE = 1e30
Y_FROM = (0, 2, 3, 1)
NT = (((1,), (1,)), ((), ()))
Q_ROWS = 4 * BLK + 16
K_ROWS = 4 * BLK


def dot(a, b):
    return jnp.dot(a, b, preferred_element_type=F32)


def dot_nt(a, b):
    return lax.dot_general(a, b, NT, preferred_element_type=F32)


def ring(value, size):
    return lax.rem(value + size, size)


def blocks(fold_ref, y, z, x):
    device = y * 16 + z * 2 + x
    first = fold_ref[2 * device]
    second = fold_ref[2 * device + 1]
    low = pl.multiple_of(jnp.where(second < first, BLK, 0), BLK)
    high = pl.multiple_of(jnp.where(second < first, 0, BLK), BLK)
    return jnp.minimum(first, second), (low, high)


def prep_kernel(*refs):
    sources, (qout_ref, kout_ref), buffers, (stats_buf, sems) = refs[:6], refs[6:8], refs[8:14], refs[14:]
    half = 2 * BLK
    targets = (qout_ref.at[half : 2 * half], None, None, kout_ref.at[:half], kout_ref.at[half:], qout_ref.at[:half])
    loads = [pltpu.make_async_copy(s, d, sems.at[n]) for n, (s, d) in enumerate(zip(sources, buffers))]
    stores = [pltpu.make_async_copy(s, d, sems.at[6 + n]) for n, (s, d) in enumerate(zip(buffers, targets)) if d is not None]
    for copy in loads:
        copy.start()
    for n in (0, 1, 2):
        loads[n].wait()
    stores[0].start()
    g_buf, o_buf, lse_buf = buffers[:3]
    lse = lse_buf[...].astype(F32)
    rows = [lse[:, :BLK], lse[:, BLK:]]
    for start in (0, BLK):
        prod = g_buf[start : start + BLK, :].astype(F32) * o_buf[start : start + BLK, :].astype(F32)
        rows.append(jnp.sum(prod.T, axis=0, keepdims=True))
    for n in (3, 4, 5):
        loads[n].wait()
        stores[n - 2].start()
    stats_buf[...] = jnp.concatenate(rows + [jnp.zeros((12, DIM), F32)], axis=0).astype(BF16)
    stores.append(pltpu.make_async_copy(stats_buf, qout_ref.at[2 * half :], sems.at[7]))
    stores[-1].start()
    for copy in stores:
        copy.wait()


def tile(k, v, kt, q, g, lses, delta, diagonal=None):
    s = dot_nt(k, q)
    probs = []
    for b, lse in enumerate(lses):
        p = jnp.exp2(s[b * BLK : (b + 1) * BLK] * (FACTOR * LOG2E) - lse)
        if b == diagonal:
            shape = (BLK, BLK)
            seen = lax.broadcasted_iota(jnp.int32, shape, 0) <= lax.broadcasted_iota(jnp.int32, shape, 1)
            p = jnp.concatenate([jnp.where(seen, p[:, :BLK], 0.0), p[:, BLK:]], 1)
        probs.append(p)
    p = jnp.concatenate(probs, 0)
    dp = dot_nt(v, g)
    ds = (p * (dp - delta)).astype(BF16)
    return dot(p.astype(BF16), g), dot(ds, q), dot(kt, ds)


def grad_kernel(turn, js, first, final, fold_ref, *refs):
    q_refs, y_ref, refs = refs[:4], refs[4], refs[5:]
    if not first:
        dqin_ref, refs = refs[0], refs[1:]
    if final:
        kept_ref, back_ref, refs = refs[0], refs[1], refs[2:]
        dq_refs, (sum_ref, dkv_ref, dv_acc, dk_acc) = refs[:4], refs[4:]
    else:
        dq_ref, dkv_ref, dv_acc, dk_acc = refs
    y, z, x = (lax.axis_index(name) for name in ("pb", "kz", "kx"))
    y_at = ring(y + Y_FROM[turn], 4)
    z_at = (z, ring(z + 7, 8), ring(z + 1, 8), ring(z + jnp.where(lax.rem(z, 2) == 0, 2, 6), 8))
    low_j, starts_j = zip(*(blocks(fold_ref, y_at, ring(z + 4 * j, 8), x) for j in js))
    count = len(js)
    half = count * BLK

    def keys(array):
        parts = [
            y_ref[n, pl.ds(array * 2 * BLK + starts_j[n][b], BLK), :] for b in range(2) for n in range(count)
        ]
        return jnp.concatenate(parts, 0)

    k, v = keys(0), keys(1)
    kt = k.T

    for pair in range(2):
        chunks = [(s, a) for s in (2 * pair, 2 * pair + 1) for a in range(2)]
        low_i, starts_i = zip(*(blocks(fold_ref, y, z_at[s], 1 - x if a else x) for s, a in chunks))

        def queries(array, b):
            parts = [q_refs[s][a, pl.ds(array * 2 * BLK + at[b], BLK), :] for (s, a), at in zip(chunks, starts_i)]
            return jnp.concatenate(parts, 0)

        def stats(row, scale):
            low, high = [], []
            for (s, a), at in zip(chunks, starts_i):
                both = q_refs[s][a, 4 * BLK :, :].astype(F32)
                upper, lower = both[row : row + 1, :], both[row + 1 : row + 2, :]
                low.append(jnp.where(at[0] == 0, upper, lower) * scale)
                high.append(jnp.where(at[0] == 0, lower, upper) * scale)
            return jnp.concatenate(low, 1), jnp.concatenate(high, 1)

        lse_low, lse_high = stats(0, LOG2E)
        delta_low, delta_high = stats(2, 1.0)
        own = turn == 0 and js[0] == 0 and pair == 0

        def hide(m, low):
            parts = []
            for n, li in enumerate(low_i):
                seen = low_j[m] < li if low else li < low_j[m]
                hidden = jnp.float32(0.0) if own and n == 0 and m == 0 else jnp.where(seen, 0.0, HIDE)
                parts.append(jnp.full((1, BLK), hidden, F32))
            return jnp.concatenate(parts, 1)

        lses = [lse_high] * count + [lse_high + hide(m, False) for m in range(count)]
        dv, dk, dq_high = tile(
            k, v, kt, queries(0, 1), queries(1, 1), lses, delta_high, count if own else None
        )
        dv_acc[...] = dv if pair == 0 else dv_acc[...] + dv
        dk_acc[...] = dk if pair == 0 else dk_acc[...] + dk
        lses = [lse_low + hide(m, True) for m in range(count)]
        dv, dk, dq_low = tile(
            k[:half], v[:half], kt[:, :half], queries(0, 0), queries(1, 0), lses, delta_low, 0 if own else None
        )
        dv_acc[:half] += dv
        dk_acc[:half] += dk
        columns = slice(pair * 4 * BLK, (pair + 1) * 4 * BLK)
        for b, dq in ((0, dq_low), (1, dq_high)):
            if not first:
                dq = dqin_ref[b, :, columns] + dq
            if not final:
                dq_ref[b, :, columns] = dq
            else:
                for n, (s, a) in enumerate(chunks):
                    ref = dq_refs[s]
                    ref[a, pl.ds(starts_i[n][b], BLK), :] = dq[:, n * BLK : (n + 1) * BLK].T.astype(ref.dtype)

    for n in range(count):
        for b in range(2):
            source = slice(b * half + n * BLK, b * half + (n + 1) * BLK)
            at = starts_j[n][b]
            for array, acc in ((0, dk_acc), (1, dv_acc)):
                rows = pl.ds(array * 2 * BLK + at, BLK)
                part = acc[source]
                if final:
                    part = part + back_ref[1, rows, :].astype(F32)
                dkv_ref[n, rows, :] = part.astype(dkv_ref.dtype)
    if final:
        sum_ref[...] = kept_ref[...] + back_ref[0].astype(F32)


def meet_kernel(own_ref, other_ref, *refs):
    *back_refs, keep_ref, send_ref = refs
    for part, (start_ref, out_ref) in enumerate(((own_ref, keep_ref), (other_ref, send_ref))):
        total = start_ref[...]
        for ref in back_refs:
            total += ref[part].astype(F32)
        out_ref[...] = total.astype(out_ref.dtype)


def last_kernel(dq_ref, dqx_ref, dkv_ref, dkvz_ref, q_ref, k_ref, v_ref):
    q_ref[...] = ((dq_ref[...] + dqx_ref[...].astype(F32)) * FACTOR).astype(BF16)
    dkv = dkv_ref[...] + dkvz_ref[...].astype(F32)
    k_ref[...] = (dkv[: 2 * BLK] * FACTOR).astype(BF16)
    v_ref[...] = dkv[2 * BLK :].astype(BF16)


def z_step(step):
    return [(i, (i + step) % 8) for i in range(8)]


def y_step(step):
    return [(i, (i + step) % 4) for i in range(4)]


Z_PAIRS = [(i, (i - 2) % 8 if i % 2 == 0 else (i + 2) % 8) for i in range(8)]
Z_BACK = [(b, a) for a, b in Z_PAIRS]
X_SWAP = [(0, 1), (1, 0)]


def call(kernel, outs, operands, fold=None, scratch=(), in_specs=None, vmem_limit=VMEM_LIMIT, **options):
    smem = pl.BlockSpec(memory_space=pltpu.SMEM)
    vmem = pl.BlockSpec(memory_space=pltpu.VMEM)
    scalars = [] if fold is None else [fold]
    return pl.pallas_call(
        kernel,
        out_shape=[jax.ShapeDtypeStruct(s, t) for s, t in outs],
        in_specs=[smem] * len(scalars) + (in_specs or [vmem] * len(operands)),
        out_specs=[pl.BlockSpec(memory_space=pltpu.HBM) if in_specs else vmem] * len(outs),
        scratch_shapes=list(scratch),
        compiler_params=pltpu.CompilerParams(vmem_limit_bytes=vmem_limit),
        **options,
    )(*scalars, *operands)


def body(queries, key_rows, value_rows, outputs, out_grad, saved_lse, fold_map):
    operands = (out_grad, outputs, saved_lse.T, key_rows, value_rows, queries)
    buffers = [pltpu.VMEM(a.shape, a.dtype) for a in operands]
    mine_q, mine_k = call(
        prep_kernel,
        [((Q_ROWS, DIM), BF16), ((K_ROWS, DIM), BF16)],
        operands,
        scratch=buffers + [pltpu.VMEM((Q_ROWS - 4 * BLK, DIM), BF16), pltpu.SemaphoreType.DMA((12,))],
        in_specs=[pl.BlockSpec(memory_space=pltpu.HBM)] * len(operands),
        vmem_limit=PREP_VMEM,
    )
    other_k = lax.ppermute(mine_k, "kz", z_step(4))
    q0 = lax.optimization_barrier(jnp.pad(mine_q[None], ((0, 1), (0, 0), (0, 0))))
    q0 = lax.dynamic_update_slice(q0, lax.ppermute(mine_q, "kx", X_SWAP)[None], (1, 0, 0))
    _, other_k = lax.optimization_barrier((q0, other_k))
    k0 = jnp.stack([mine_k, other_k])
    q_sets = [q0] + [lax.ppermute(q0, "kz", p) for p in (z_step(1), z_step(-1), Z_PAIRS)]
    k_sets = [k0] + [lax.ppermute(k0, "pb", y_step(-s)) for s in Y_FROM[1:]]

    dq = []
    dkv = {}
    order = ((0, (0,)), (1, (0, 1)), (2, (0, 1)), (3, (0, 1)), (0, (1,)))
    for turn, js in order:
        first, final = (turn, js) == order[0], (turn, js) == order[-1]
        key_set = (mine_k, other_k)[js[0]][None] if turn == 0 else k_sets[turn]
        outs = [((2, DIM, 8 * BLK), F32)]
        if final:
            outs = [((2, 2 * BLK, DIM), F32 if s == 0 else BF16) for s in range(4)] + [((K_ROWS, DIM), F32)]
        acc = pltpu.VMEM((2 * len(js) * BLK, DIM), F32)
        *dq, part = call(
            functools.partial(grad_kernel, turn, js, first, final),
            outs + [((len(js), K_ROWS, DIM), BF16 if turn else F32)],
            q_sets + [key_set] + ([] if first else dq) + ([dkv[0, (0,)], dkv[1, (0, 1)]] if final else []),
            fold_map,
            [acc, acc],
            cost_estimate=pl.CostEstimate(flops=FLOPS * len(js) // 2, bytes_accessed=1 << 20, transcendentals=0),
            input_output_aliases={} if first or final else {6: 0},
        )
        dkv[turn, js] = lax.ppermute(part, "pb", y_step(Y_FROM[turn])) if turn else part[0]
    dq_back = [lax.ppermute(dq[t], "kz", p) for t, p in ((1, z_step(-1)), (2, z_step(1)), (3, Z_BACK))]

    def meet(own, other, partners):
        return call(meet_kernel, [(own.shape, F32), (own.shape, BF16)], [own, other] + partners)

    dkv_keep, dkv_send = meet(dq[4], dkv[0, (1,)], [dkv[t, (0, 1)] for t in (2, 3)])
    dkv_last = lax.ppermute(dkv_send, "kz", z_step(4))
    dq_keep, dq_send = meet(dq[0][0], dq[0][1], dq_back)
    dq_last = lax.ppermute(dq_send, "kx", X_SWAP)
    return tuple(call(last_kernel, [((2 * BLK, DIM), BF16)] * 3, (dq_keep, dq_last, dkv_keep, dkv_last)))


def solution(mesh):
    fine = Mesh(mesh.devices.reshape(4, 8, 2, 2, 2), ("pb", "kz", "kx", "hx", "hc"))
    rows = P(("pb", "kz", "kx"), ("hx", "hc"))
    return jax.shard_map(
        body,
        mesh=fine,
        in_specs=(rows,) * 6 + (P(),),
        out_specs=(rows,) * 3,
        check_vma=False,
    )
```

```python
import functools
import math

import jax
import jax.numpy as jnp
from jax import lax
from jax.experimental import pallas as pl
from jax.experimental.pallas import tpu as pltpu
from jax.sharding import Mesh, PartitionSpec as P

F32 = jnp.float32
BF16 = jnp.bfloat16
BLK = 128
DIM = 128
LOG2E = math.log2(math.e)
FACTOR = 1.0 / math.sqrt(DIM)
VMEM_LIMIT = 48 * 1024 * 1024
PREP_VMEM = 62 * 1024 * 1024
FLOPS = 10 * 2 * 3 * (2 * BLK) * (4 * BLK) * DIM
HIDE = 1e30
Y_FROM = (0, 2, 3, 1)
NT = (((1,), (1,)), ((), ()))
ROWS = 4 * BLK + 16


def dot(a, b):
    return jnp.dot(a, b, preferred_element_type=F32)


def dot_nt(a, b):
    return lax.dot_general(a, b, NT, preferred_element_type=F32)


def prep_kernel(*refs):
    sources, (qout_ref, kout_ref), buffers, refs = refs[:7], refs[7:9], refs[9:16], refs[16:]
    qrows_buf, krows_buf, load_sems, store_sems = refs
    loads = [pltpu.make_async_copy(s, d, load_sems.at[n]) for n, (s, d) in enumerate(zip(sources, buffers))]
    for copy in loads:
        copy.start()
    stores = []

    def store(source, target):
        stores.append(pltpu.make_async_copy(source, target, store_sems.at[len(stores)]))
        stores[-1].start()

    def store_blocks(n, out_ref, at):
        loads[n].wait()
        store(buffers[n].at[pl.ds(low_at, BLK)], out_ref.at[at : at + BLK])
        store(buffers[n].at[pl.ds(high_at, BLK)], out_ref.at[at + BLK : at + 2 * BLK])

    fold_ref, g_buf, o_buf, lse_buf = buffers[:4]
    device = lax.axis_index("pb") * 16 + lax.axis_index("kz") * 2 + lax.axis_index("kx")
    loads[0].wait()
    first, second = fold_ref[2 * device], fold_ref[2 * device + 1]
    swapped = second < first
    low_at = pl.multiple_of(jnp.where(swapped, BLK, 0), BLK)
    high_at = pl.multiple_of(jnp.where(swapped, 0, BLK), BLK)
    low = jnp.minimum(first, second).astype(F32)
    krows_buf[...] = jnp.full(krows_buf.shape, low, F32).astype(BF16)
    store(krows_buf, kout_ref.at[4 * BLK :])
    store_blocks(1, qout_ref, 2 * BLK)
    loads[2].wait()
    loads[3].wait()
    lse = lse_buf[...].astype(F32)
    rows = [jnp.where(swapped, lse[:, BLK:], lse[:, :BLK]), jnp.where(swapped, lse[:, :BLK], lse[:, BLK:])]
    for at in (low_at, high_at):
        prod = g_buf[pl.ds(at, BLK), :].astype(F32) * o_buf[pl.ds(at, BLK), :].astype(F32)
        rows.append(jnp.sum(prod.T, axis=0, keepdims=True))
    rows.append(jnp.full((1, DIM), low, F32))
    rows.append(jnp.full((1, DIM), jnp.where(swapped, 1.0, 0.0), F32))
    qrows_buf[...] = jnp.concatenate(rows + [jnp.zeros((10, DIM), F32)], axis=0).astype(BF16)
    store(qrows_buf, qout_ref.at[4 * BLK :])
    store_blocks(6, qout_ref, 0)
    store_blocks(4, kout_ref, 0)
    store_blocks(5, kout_ref, 2 * BLK)
    for copy in stores:
        copy.wait()


def tile(k, v, kt, q, g, lses, delta, diagonal=None):
    s = dot_nt(k, q)
    probs = []
    for b, lse in enumerate(lses):
        p = jnp.exp2(s[b * BLK : (b + 1) * BLK] * (FACTOR * LOG2E) - lse)
        if b == diagonal:
            shape = (BLK, BLK)
            seen = lax.broadcasted_iota(jnp.int32, shape, 0) <= lax.broadcasted_iota(jnp.int32, shape, 1)
            p = jnp.concatenate([jnp.where(seen, p[:, :BLK], 0.0), p[:, BLK:]], 1)
        probs.append(p)
    p = jnp.concatenate(probs, 0)
    dp = dot_nt(v, g)
    ds = (p * (dp - delta)).astype(BF16)
    return dot(p.astype(BF16), g), dot(ds, q), dot(kt, ds)


def grad_kernel(js, plan, own, *refs):
    refs = list(refs)

    def take(count):
        taken = refs[:count]
        del refs[:count]
        return taken

    q_refs, (y_ref,) = take(2 * len(plan)), take(1)
    dqin_refs = [None if first else take(1)[0] for first, _ in plan]
    dq_refs = [take(2 if last else 1) for _, last in plan]
    dkv_ref, dv_acc, dk_acc = refs
    count = len(js)
    half = count * BLK

    def keys(array):
        at = array * 2 * BLK
        return jnp.concatenate([y_ref[j, at + b * BLK : at + (b + 1) * BLK, :] for b in range(2) for j in js], 0)

    k, v = keys(0), keys(1)
    kt = k.T
    low_j = [jnp.concatenate([y_ref[j, 4 * BLK :, :].astype(F32)[0:1, :]] * 4, 1) for j in js]

    for n, (first, last) in enumerate(plan):
        pair = q_refs[2 * n : 2 * n + 2]
        chunks = [(ref, a) for ref in pair for a in range(2)]

        def queries(array, b):
            at = (2 * array + b) * BLK
            return jnp.concatenate([ref[a, at : at + BLK, :] for ref, a in chunks], 0)

        tiles = [ref[a, 4 * BLK :, :].astype(F32) for ref, a in chunks]
        lse_low, lse_high, delta_low, delta_high, low_i = (
            jnp.concatenate([t[r : r + 1, :] for t in tiles], 1) for r in range(5)
        )
        lse_low, lse_high = lse_low * LOG2E, lse_high * LOG2E
        diagonal = own and n == 0

        lses = [lse_high] * count + [lse_high + jnp.where(low_i <= low, 0.0, HIDE) for low in low_j]
        dv, dk, dq_high = tile(
            k, v, kt, queries(0, 1), queries(1, 1), lses, delta_high, count if diagonal else None
        )
        dv_acc[...] = dv if n == 0 else dv_acc[...] + dv
        dk_acc[...] = dk if n == 0 else dk_acc[...] + dk
        lses = [lse_low + jnp.where(low <= low_i, 0.0, HIDE) for low in low_j]
        dv, dk, dq_low = tile(
            k[:half], v[:half], kt[:, :half], queries(0, 0), queries(1, 0), lses, delta_low, 0 if diagonal else None
        )
        dv_acc[:half] += dv
        dk_acc[:half] += dk
        for b, dq in ((0, dq_low), (1, dq_high)):
            if not first:
                dq = dqin_refs[n][b] + dq
            if not last:
                dq_refs[n][0][b] = dq
            else:
                for c in range(4):
                    ref = dq_refs[n][c // 2]
                    ref[c % 2, b * BLK : (b + 1) * BLK, :] = dq[:, c * BLK : (c + 1) * BLK].T.astype(ref.dtype)

    for m in range(count):
        for b in range(2):
            source = slice(b * half + m * BLK, b * half + (m + 1) * BLK)
            for array, acc in ((0, dk_acc), (1, dv_acc)):
                at = (2 * array + b) * BLK
                dkv_ref[m, at : at + BLK, :] = acc[source].astype(dkv_ref.dtype)


def meet_kernel(parts, *refs):
    out_refs = refs[-2:]
    for half, out_ref in enumerate(out_refs):
        total = None
        for ref, index in zip(refs, parts):
            if index[half] is not None:
                part = ref[index[half]].astype(F32)
                total = part if total is None else total + part
        out_ref[...] = total.astype(out_ref.dtype)


def last_kernel(rows_ref, dq_ref, dqx_ref, dkv_ref, dkvz_ref, q_ref, k_ref, v_ref):
    swapped = rows_ref[0, 4 * BLK :, :].astype(F32)[5:6, :] > 0.5

    def restore(out_ref, total):
        low, high = total[:BLK], total[BLK:]
        out_ref[:BLK, :] = jnp.where(swapped, high, low).astype(BF16)
        out_ref[BLK:, :] = jnp.where(swapped, low, high).astype(BF16)

    restore(q_ref, (dq_ref[...] + dqx_ref[...].astype(F32)) * FACTOR)
    dkv = dkv_ref[...] + dkvz_ref[...].astype(F32)
    restore(k_ref, dkv[: 2 * BLK] * FACTOR)
    restore(v_ref, dkv[2 * BLK :])


def z_step(step):
    return [(i, (i + step) % 8) for i in range(8)]


def y_step(step):
    return [(i, (i + step) % 4) for i in range(4)]


Z_PAIRS = [(i, (i - 2) % 8 if i % 2 == 0 else (i + 2) % 8) for i in range(8)]
Z_BACK = [(b, a) for a, b in Z_PAIRS]
X_SWAP = [(0, 1), (1, 0)]


def call(kernel, outs, operands, scratch=(), hbm=False, **options):
    space = pl.BlockSpec(memory_space=pltpu.HBM if hbm else pltpu.VMEM)
    return pl.pallas_call(
        kernel,
        out_shape=[jax.ShapeDtypeStruct(s, t) for s, t in outs],
        in_specs=[space] * len(operands),
        out_specs=[space] * len(outs),
        scratch_shapes=list(scratch),
        compiler_params=pltpu.CompilerParams(vmem_limit_bytes=PREP_VMEM if hbm else VMEM_LIMIT),
        **options,
    )(*operands)


def body(queries, key_rows, value_rows, outputs, out_grad, saved_lse, fold_map):
    operands = (fold_map, out_grad, outputs, saved_lse.T, key_rows, value_rows, queries)
    buffers = [(pltpu.SMEM if n == 0 else pltpu.VMEM)(a.shape, a.dtype) for n, a in enumerate(operands)]
    rows = pltpu.VMEM((ROWS - 4 * BLK, DIM), BF16)
    sems = [pltpu.SemaphoreType.DMA((7,)), pltpu.SemaphoreType.DMA((10,))]
    payload = ((ROWS, DIM), BF16)
    mine_q, mine_k = call(prep_kernel, [payload] * 2, operands, buffers + [rows] * 2 + sems, hbm=True)

    def beside(mine, other):
        both = lax.optimization_barrier(jnp.pad(mine[None], ((0, 1), (0, 0), (0, 0))))
        return lax.dynamic_update_slice(both, other[None], (1, 0, 0))

    other_k = lax.ppermute(mine_k, "kz", z_step(4))
    q0 = beside(mine_q, lax.ppermute(mine_q, "kx", X_SWAP))
    _, other_k = lax.optimization_barrier((q0, other_k))
    k0 = jnp.stack([mine_k, other_k])
    q_sets = [q0] + [lax.ppermute(q0, "kz", p) for p in (z_step(1), z_step(-1), Z_PAIRS)]
    k_sets = [k0] + [lax.ppermute(k0, "pb", y_step(-s)) for s in Y_FROM[1:]]
    q_pairs = ([q_sets[0], q_sets[3]], [q_sets[1], q_sets[2]])

    def grad(turn, js, pairs, dq_in, last, dkv_type):
        plan = tuple((d is None, e) for d, e in zip(dq_in, last))
        outs = []
        for pair, end in zip(pairs, last):
            if end:
                outs += [((2, 2 * BLK, DIM), F32 if (pair, s) == (0, 0) else BF16) for s in range(2)]
            else:
                outs.append(((2, DIM, 4 * BLK), F32))
        acc = pltpu.VMEM((2 * len(js) * BLK, DIM), F32)
        units = len(js) * len(pairs)
        *dq, part = call(
            functools.partial(grad_kernel, js, plan, turn == 0 and js[0] == 0 and pairs[0] == 0),
            outs + [((len(js), 4 * BLK, DIM), dkv_type)],
            [q for p in pairs for q in q_pairs[p]] + [k_sets[turn]] + [d for d in dq_in if d is not None],
            [acc, acc],
            cost_estimate=pl.CostEstimate(flops=FLOPS * units // 4, bytes_accessed=1 << 20, transcendentals=0),
        )
        return dq, part

    def send_back(turn, part):
        return lax.ppermute(part, "pb", y_step(Y_FROM[turn]))

    (dq0,), own = grad(0, (0, 1), (0,), (None,), (False,), F32)
    (dq1,), own_a = grad(0, (0,), (1,), (None,), (False,), F32)
    (dq0, dq1), part = grad(1, (0, 1), (0, 1), (dq0, dq1), (False, False), BF16)
    back = [send_back(1, part)]
    (dq0, dq1), part = grad(2, (0, 1), (0, 1), (dq0, dq1), (False, False), BF16)
    back.append(send_back(2, part))
    (dq_keep, dq_z2, dq1), part = grad(3, (0, 1), (0, 1), (dq0, dq1), (True, False), BF16)
    back.append(send_back(3, part))
    dq1, back[0] = lax.optimization_barrier((dq1, back[0]))
    (dq_left, dq_right), own_b = grad(0, (1,), (1,), (dq1,), (True,), F32)
    dq_back = [lax.ppermute(d, "kz", p) for d, p in ((dq_left, z_step(-1)), (dq_right, z_step(1)), (dq_z2, Z_BACK))]

    def meet(operands, parts, shape):
        return call(functools.partial(meet_kernel, parts), [(shape, F32), (shape, BF16)], operands)

    both = (0, 1)
    dkv_keep, dkv_send = meet([own, own_a, own_b] + back, [both, (0, None), (None, 0)] + [both] * 3, (4 * BLK, DIM))
    dkv_last = lax.ppermute(dkv_send, "kz", z_step(4))
    dq_keep, dq_send = meet([dq_keep] + dq_back, [both] * 4, (2 * BLK, DIM))
    dq_last = lax.ppermute(dq_send, "kx", X_SWAP)
    return tuple(call(last_kernel, [((2 * BLK, DIM), BF16)] * 3, (q0, dq_keep, dq_last, dkv_keep, dkv_last)))


def solution(mesh):
    fine = Mesh(mesh.devices.reshape(4, 8, 2, 2, 2), ("pb", "kz", "kx", "hx", "hc"))
    rows = P(("pb", "kz", "kx"), ("hx", "hc"))
    return jax.shard_map(
        body,
        mesh=fine,
        in_specs=(rows,) * 6 + (P(),),
        out_specs=(rows,) * 3,
        check_vma=False,
    )
```

```python
import functools
import math

import jax
import jax.numpy as jnp
from jax import lax
from jax.experimental import pallas as pl
from jax.experimental.pallas import tpu as pltpu
from jax.sharding import Mesh, PartitionSpec as P

F32 = jnp.float32
BF16 = jnp.bfloat16
BLK = 128
DIM = 128
LOG2E = math.log2(math.e)
FACTOR = 1.0 / math.sqrt(DIM)
VMEM_LIMIT = 48 * 1024 * 1024
PREP_VMEM = 62 * 1024 * 1024
COST = pl.CostEstimate(flops=500000000, bytes_accessed=1000000, transcendentals=0)
HIDE = 1e30
Y_FROM = (0, 2, 3, 1)
NT = (((1,), (1,)), ((), ()))
ROWS = 4 * BLK + 16


def dot(a, b):
    return jnp.dot(a, b, preferred_element_type=F32)


def dot_nt(a, b):
    return lax.dot_general(a, b, NT, preferred_element_type=F32)


def prep_kernel(*refs):
    sources, (qout_ref, kout_ref), buffers, refs = refs[:7], refs[7:9], refs[9:16], refs[16:]
    qrows_buf, krows_buf, load_sems, store_sems = refs
    loads = [pltpu.make_async_copy(s, d, load_sems.at[n]) for n, (s, d) in enumerate(zip(sources, buffers))]
    for copy in loads:
        copy.start()
    stores = []

    def store(source, target):
        stores.append(pltpu.make_async_copy(source, target, store_sems.at[len(stores)]))
        stores[-1].start()

    def store_blocks(n, out_ref, at):
        loads[n].wait()
        store(buffers[n].at[pl.ds(low_at, BLK)], out_ref.at[at : at + BLK])
        store(buffers[n].at[pl.ds(high_at, BLK)], out_ref.at[at + BLK : at + 2 * BLK])

    fold_ref, g_buf, o_buf, lse_buf = buffers[:4]
    device = lax.axis_index("pb") * 16 + lax.axis_index("kz") * 2 + lax.axis_index("kx")
    loads[0].wait()
    first, second = fold_ref[2 * device], fold_ref[2 * device + 1]
    swapped = second < first
    low_at = pl.multiple_of(jnp.where(swapped, BLK, 0), BLK)
    high_at = pl.multiple_of(jnp.where(swapped, 0, BLK), BLK)
    low = jnp.minimum(first, second).astype(F32)
    krows_buf[...] = jnp.full(krows_buf.shape, low, F32).astype(BF16)
    store(krows_buf, kout_ref.at[4 * BLK :])
    store_blocks(1, qout_ref, 2 * BLK)
    loads[2].wait()
    loads[3].wait()
    lse = lse_buf[...].astype(F32)
    rows = [jnp.where(swapped, lse[:, BLK:], lse[:, :BLK]), jnp.where(swapped, lse[:, :BLK], lse[:, BLK:])]
    for at in (low_at, high_at):
        prod = g_buf[pl.ds(at, BLK), :].astype(F32) * o_buf[pl.ds(at, BLK), :].astype(F32)
        rows.append(jnp.sum(prod.T, axis=0, keepdims=True))
    rows.append(jnp.full((1, DIM), low, F32))
    rows.append(jnp.full((1, DIM), jnp.where(swapped, 1.0, 0.0), F32))
    qrows_buf[...] = jnp.concatenate(rows + [jnp.zeros((10, DIM), F32)], axis=0).astype(BF16)
    store(qrows_buf, qout_ref.at[4 * BLK :])
    store_blocks(6, qout_ref, 0)
    store_blocks(4, kout_ref, 0)
    store_blocks(5, kout_ref, 2 * BLK)
    for copy in stores:
        copy.wait()


def tile(k, v, kt, q, g, lses, delta, diagonal=None):
    s = dot_nt(k, q)
    probs = []
    for b, lse in enumerate(lses):
        p = jnp.exp2(s[b * BLK : (b + 1) * BLK] * (FACTOR * LOG2E) - lse)
        if b == diagonal:
            shape = (BLK, BLK)
            seen = lax.broadcasted_iota(jnp.int32, shape, 0) <= lax.broadcasted_iota(jnp.int32, shape, 1)
            p = jnp.concatenate([jnp.where(seen, p[:, :BLK], 0.0), p[:, BLK:]], 1)
        probs.append(p)
    p = jnp.concatenate(probs, 0)
    dp = dot_nt(v, g)
    ds = (p * (dp - delta)).astype(BF16)
    return dot(p.astype(BF16), g), dot(ds, q), dot(kt, ds)


def grad_kernel(js, plan, own, add, split, *refs):
    refs = list(refs)

    def take(count):
        taken = refs[:count]
        del refs[:count]
        return taken

    q_refs, (y_ref,) = take(2 * len(plan)), take(1)
    dqin_refs = [None if first else take(1)[0] for first, _ in plan]
    addin_ref = refs.pop(0) if add else None
    dq_refs = [take(2 if last else 1) for _, last in plan]
    dkv_refs = take(len(js)) if split else [refs.pop(0)]
    dv_acc, dk_acc = refs
    count = len(js)
    half = count * BLK

    def keys(array):
        at = array * 2 * BLK
        return jnp.concatenate([y_ref[j, at + b * BLK : at + (b + 1) * BLK, :] for b in range(2) for j in js], 0)

    k, v = keys(0), keys(1)
    kt = k.T
    low_j = [jnp.concatenate([y_ref[j, 4 * BLK :, :].astype(F32)[0:1, :]] * 4, 1) for j in js]

    for n, (first, last) in enumerate(plan):
        pair = q_refs[2 * n : 2 * n + 2]
        chunks = [(ref, a) for ref in pair for a in range(2)]

        def queries(array, b):
            at = (2 * array + b) * BLK
            return jnp.concatenate([ref[a, at : at + BLK, :] for ref, a in chunks], 0)

        tiles = [ref[a, 4 * BLK :, :].astype(F32) for ref, a in chunks]
        lse_low, lse_high, delta_low, delta_high, low_i = (
            jnp.concatenate([t[r : r + 1, :] for t in tiles], 1) for r in range(5)
        )
        lse_low, lse_high = lse_low * LOG2E, lse_high * LOG2E
        diagonal = own and n == 0

        lses = [lse_high] * count + [lse_high + jnp.where(low_i <= low, 0.0, HIDE) for low in low_j]
        dv, dk, dq_high = tile(
            k, v, kt, queries(0, 1), queries(1, 1), lses, delta_high, count if diagonal else None
        )
        dv_acc[...] = dv if n == 0 else dv_acc[...] + dv
        dk_acc[...] = dk if n == 0 else dk_acc[...] + dk
        lses = [lse_low + jnp.where(low <= low_i, 0.0, HIDE) for low in low_j]
        dv, dk, dq_low = tile(
            k[:half], v[:half], kt[:, :half], queries(0, 0), queries(1, 0), lses, delta_low, 0 if diagonal else None
        )
        dv_acc[:half] += dv
        dk_acc[:half] += dk
        for b, dq in ((0, dq_low), (1, dq_high)):
            if not first:
                dq = dqin_refs[n][b] + dq
            if not last:
                dq_refs[n][0][b] = dq
            else:
                for c in range(4):
                    ref = dq_refs[n][c // 2]
                    ref[c % 2, b * BLK : (b + 1) * BLK, :] = dq[:, c * BLK : (c + 1) * BLK].T.astype(ref.dtype)

    for m in range(count):
        for b in range(2):
            source = slice(b * half + m * BLK, b * half + (m + 1) * BLK)
            for array, acc in ((0, dk_acc), (1, dv_acc)):
                rows = slice((2 * array + b) * BLK, (2 * array + b + 1) * BLK)
                part = acc[source]
                if add:
                    part = addin_ref[m, rows, :] + part
                if split:
                    dkv_refs[m][rows, :] = part.astype(BF16)
                else:
                    dkv_refs[0][m, rows, :] = part.astype(dkv_refs[0].dtype)


def meet_kernel(parts, *refs):
    out_refs = refs[-2:]
    for half, out_ref in enumerate(out_refs):
        total = None
        for ref, index in zip(refs, parts):
            if index[half] is not None:
                part = ref[index[half]].astype(F32)
                total = part if total is None else total + part
        out_ref[...] = total.astype(out_ref.dtype)


def last_kernel(rows_ref, dq_ref, dqx_ref, dkv_ref, dkvz_ref, dkvy_ref, dkvyz_ref, q_ref, k_ref, v_ref):
    swapped = rows_ref[0, 4 * BLK :, :].astype(F32)[5:6, :] > 0.5

    def restore(out_ref, total):
        low, high = total[:BLK], total[BLK:]
        out_ref[:BLK, :] = jnp.where(swapped, high, low).astype(BF16)
        out_ref[BLK:, :] = jnp.where(swapped, low, high).astype(BF16)

    restore(q_ref, (dq_ref[...] + dqx_ref[...].astype(F32)) * FACTOR)
    dkv = dkv_ref[...]
    for ref in (dkvz_ref, dkvy_ref, dkvyz_ref):
        dkv += ref[...].astype(F32)
    restore(k_ref, dkv[: 2 * BLK] * FACTOR)
    restore(v_ref, dkv[2 * BLK :])


def z_step(step):
    return [(i, (i + step) % 8) for i in range(8)]


def y_step(step):
    return [(i, (i + step) % 4) for i in range(4)]


Z_PAIRS = [(i, (i - 2) % 8 if i % 2 == 0 else (i + 2) % 8) for i in range(8)]
Z_BACK = [(b, a) for a, b in Z_PAIRS]
X_SWAP = [(0, 1), (1, 0)]


def call(kernel, outs, operands, scratch=(), hbm=False, **options):
    space = pl.BlockSpec(memory_space=pltpu.HBM if hbm else pltpu.VMEM)
    return pl.pallas_call(
        kernel,
        out_shape=[jax.ShapeDtypeStruct(s, t) for s, t in outs],
        in_specs=[space] * len(operands),
        out_specs=[space] * len(outs),
        scratch_shapes=list(scratch),
        compiler_params=pltpu.CompilerParams(vmem_limit_bytes=PREP_VMEM if hbm else VMEM_LIMIT),
        **options,
    )(*operands)


def body(queries, key_rows, value_rows, outputs, out_grad, saved_lse, fold_map):
    operands = (fold_map, out_grad, outputs, saved_lse.T, key_rows, value_rows, queries)
    buffers = [(pltpu.SMEM if n == 0 else pltpu.VMEM)(a.shape, a.dtype) for n, a in enumerate(operands)]
    rows = pltpu.VMEM((ROWS - 4 * BLK, DIM), BF16)
    sems = [pltpu.SemaphoreType.DMA((7,)), pltpu.SemaphoreType.DMA((10,))]
    payload = ((ROWS, DIM), BF16)
    mine_q, mine_k = call(prep_kernel, [payload] * 2, operands, buffers + [rows] * 2 + sems, hbm=True)

    def beside(mine, other):
        both = lax.optimization_barrier(jnp.pad(mine[None], ((0, 1), (0, 0), (0, 0))))
        return lax.dynamic_update_slice(both, other[None], (1, 0, 0))

    other_k = lax.ppermute(mine_k, "kz", z_step(4))
    q0 = beside(mine_q, lax.ppermute(mine_q, "kx", X_SWAP))
    _, other_k = lax.optimization_barrier((q0, other_k))
    k0 = jnp.stack([mine_k, other_k])
    q_sets = [q0] + [lax.ppermute(q0, "kz", p) for p in (z_step(1), z_step(-1), Z_PAIRS)]
    k_sets = [k0] + [lax.ppermute(k0, "pb", y_step(-s)) for s in Y_FROM[1:]]
    q_pairs = ([q_sets[0], q_sets[3]], [q_sets[1], q_sets[2]])

    def grad(turn, js, pairs, dq_in, last, dkv_type, add=None, split=False):
        plan = tuple((d is None, e) for d, e in zip(dq_in, last))
        outs = []
        for pair, end in zip(pairs, last):
            if end:
                outs += [((2, 2 * BLK, DIM), F32 if (pair, s) == (0, 0) else BF16) for s in range(2)]
            else:
                outs.append(((2, DIM, 4 * BLK), F32))
        dkv_out = [((4 * BLK, DIM), BF16)] * len(js) if split else [((len(js), 4 * BLK, DIM), dkv_type)]
        acc = pltpu.VMEM((2 * len(js) * BLK, DIM), F32)
        results = call(
            functools.partial(grad_kernel, js, plan, turn == 0 and pairs[0] == 0, add is not None, split),
            outs + dkv_out,
            [q for p in pairs for q in q_pairs[p]] + [k_sets[turn]] + [d for d in (*dq_in, add) if d is not None],
            [acc, acc],
            cost_estimate=COST,
        )
        return results[: len(outs)], results[len(outs) :]

    def send_back(turn, part):
        return lax.ppermute(part, "pb", y_step(Y_FROM[turn]))

    both = (0, 1)
    (dq1,), (own1,) = grad(0, both, (1,), (None,), (False,), F32)
    k_sets[0], own1 = lax.optimization_barrier((k_sets[0], own1))
    (dq0,), (own0,) = grad(0, both, (0,), (None,), (False,), F32)
    (dq0, dq1), (part,) = grad(1, both, both, (dq0, dq1), (False, False), BF16)
    back1 = send_back(1, part)
    (dq0, dq1), (part,) = grad(2, both, both, (dq0, dq1), (False, False), BF16)
    back2 = send_back(2, part)
    (dq_keep, *dqs), (part, part_far) = grad(3, both, both, (dq0, dq1), (True, True), BF16, split=True)
    back3 = send_back(3, part)
    far = [(y * 8 + z, (y + Y_FROM[3]) % 4 * 8 + (z + 4) % 8) for y in range(4) for z in range(8)]
    back_far = lax.ppermute(part_far, ("pb", "kz"), far)
    dqs[0], back1 = lax.optimization_barrier((dqs[0], back1))
    dq_back = [lax.ppermute(d, "kz", p) for d, p in zip(dqs, (Z_BACK, z_step(-1), z_step(1)))]

    def meet(operands, parts, shape):
        return call(functools.partial(meet_kernel, parts), [(shape, F32), (shape, BF16)], operands)

    dkv_keep, dkv_send = meet(
        [own0, own1, back1, back2], [both] * 4, (4 * BLK, DIM)
    )
    dkv_last = lax.ppermute(dkv_send, "kz", z_step(4))
    dq_keep, dq_send = meet([dq_keep] + dq_back, [both] * 4, (2 * BLK, DIM))
    dq_last = lax.ppermute(dq_send, "kx", X_SWAP)
    operands = (q0, dq_keep, dq_last, dkv_keep, dkv_last, back3, back_far)
    return tuple(call(last_kernel, [((2 * BLK, DIM), BF16)] * 3, operands))


def solution(mesh):
    fine = Mesh(mesh.devices.reshape(4, 8, 2, 2, 2), ("pb", "kz", "kx", "hx", "hc"))
    rows = P(("pb", "kz", "kx"), ("hx", "hc"))
    return jax.shard_map(
        body,
        mesh=fine,
        in_specs=(rows,) * 6 + (P(),),
        out_specs=(rows,) * 3,
        check_vma=False,
    )
```

```python
import functools
import math

import jax
import jax.numpy as jnp
from jax import lax
from jax.experimental import pallas as pl
from jax.experimental.pallas import tpu as pltpu
from jax.sharding import Mesh, PartitionSpec as P

F32 = jnp.float32
BF16 = jnp.bfloat16
BLK = 128
DIM = 128
LOG2E = math.log2(math.e)
FACTOR = 1.0 / math.sqrt(DIM)
VMEM_LIMIT = 48 * 1024 * 1024
PREP_VMEM = 62 * 1024 * 1024
COST = pl.CostEstimate(flops=500000000, bytes_accessed=1000000, transcendentals=0)
HIDE = 1e30
Y_FROM = (0, 2, 3, 1)
NT = (((1,), (1,)), ((), ()))
ROWS = 4 * BLK + 16


def dot(a, b):
    return jnp.dot(a, b, preferred_element_type=F32)


def dot_nt(a, b):
    return lax.dot_general(a, b, NT, preferred_element_type=F32)


def prep_kernel(*refs):
    sources, (qout_ref, kout_ref), buffers, refs = refs[:7], refs[7:9], refs[9:16], refs[16:]
    qrows_buf, krows_buf, load_sems, store_sems = refs
    loads = [pltpu.make_async_copy(s, d, load_sems.at[n]) for n, (s, d) in enumerate(zip(sources, buffers))]
    for copy in loads:
        copy.start()
    stores = []

    def store(source, target):
        stores.append(pltpu.make_async_copy(source, target, store_sems.at[len(stores)]))
        stores[-1].start()

    def store_blocks(n, out_ref, at):
        loads[n].wait()
        store(buffers[n].at[pl.ds(low_at, BLK)], out_ref.at[at : at + BLK])
        store(buffers[n].at[pl.ds(high_at, BLK)], out_ref.at[at + BLK : at + 2 * BLK])

    fold_ref, g_buf, o_buf, lse_buf = buffers[:4]
    device = lax.axis_index("pb") * 16 + lax.axis_index("kz") * 2 + lax.axis_index("kx")
    loads[0].wait()
    first, second = fold_ref[2 * device], fold_ref[2 * device + 1]
    swapped = second < first
    low_at = pl.multiple_of(jnp.where(swapped, BLK, 0), BLK)
    high_at = pl.multiple_of(jnp.where(swapped, 0, BLK), BLK)
    low = jnp.minimum(first, second).astype(F32)
    krows_buf[...] = jnp.full(krows_buf.shape, low, F32).astype(BF16)
    store(krows_buf, kout_ref.at[4 * BLK :])
    store_blocks(1, qout_ref, 2 * BLK)
    loads[2].wait()
    loads[3].wait()
    lse = lse_buf[...].astype(F32)
    rows = [jnp.where(swapped, lse[:, BLK:], lse[:, :BLK]), jnp.where(swapped, lse[:, :BLK], lse[:, BLK:])]
    for at in (low_at, high_at):
        prod = g_buf[pl.ds(at, BLK), :].astype(F32) * o_buf[pl.ds(at, BLK), :].astype(F32)
        rows.append(jnp.sum(prod.T, axis=0, keepdims=True))
    rows.append(jnp.full((1, DIM), low, F32))
    rows.append(jnp.full((1, DIM), jnp.where(swapped, 1.0, 0.0), F32))
    qrows_buf[...] = jnp.concatenate(rows + [jnp.zeros((10, DIM), F32)], axis=0).astype(BF16)
    store(qrows_buf, qout_ref.at[4 * BLK :])
    store_blocks(6, qout_ref, 0)
    store_blocks(4, kout_ref, 0)
    store_blocks(5, kout_ref, 2 * BLK)
    for copy in stores:
        copy.wait()


def tile(k, v, kt, q, g, lses, delta, diagonal=None):
    s = dot_nt(k, q)
    probs = []
    for b, lse in enumerate(lses):
        p = jnp.exp2(s[b * BLK : (b + 1) * BLK] * (FACTOR * LOG2E) - lse)
        if b == diagonal:
            shape = (BLK, BLK)
            seen = lax.broadcasted_iota(jnp.int32, shape, 0) <= lax.broadcasted_iota(jnp.int32, shape, 1)
            p = jnp.concatenate([jnp.where(seen, p[:, :BLK], 0.0), p[:, BLK:]], 1)
        probs.append(p)
    p = jnp.concatenate(probs, 0)
    dp = dot_nt(v, g)
    ds = (p * (dp - delta)).astype(BF16)
    return dot(p.astype(BF16), g), dot(ds, q), dot(kt, ds)


def grad_kernel(js, plan, own, add, split, *refs):
    refs = list(refs)

    def take(count):
        taken = refs[:count]
        del refs[:count]
        return taken

    q_refs, (y_ref,) = take(2 * len(plan)), take(1)
    dqin_refs = [None if first else take(1)[0] for first, _ in plan]
    addin_ref = refs.pop(0) if add else None
    dq_refs = [take(2 if last else 1) for _, last in plan]
    dkv_refs = take(len(js)) if split else [refs.pop(0)]
    dv_acc, dk_acc = refs
    count = len(js)
    half = count * BLK

    def keys(array):
        at = array * 2 * BLK
        return jnp.concatenate([y_ref[j, at + b * BLK : at + (b + 1) * BLK, :] for b in range(2) for j in js], 0)

    k, v = keys(0), keys(1)
    kt = k.T
    low_j = [jnp.concatenate([y_ref[j, 4 * BLK :, :].astype(F32)[0:1, :]] * 4, 1) for j in js]

    for n, (first, last) in enumerate(plan):
        pair = q_refs[2 * n : 2 * n + 2]
        chunks = [(ref, a) for ref in pair for a in range(2)]

        def queries(array, b):
            at = (2 * array + b) * BLK
            return jnp.concatenate([ref[a, at : at + BLK, :] for ref, a in chunks], 0)

        tiles = [ref[a, 4 * BLK :, :].astype(F32) for ref, a in chunks]
        lse_low, lse_high, delta_low, delta_high, low_i = (
            jnp.concatenate([t[r : r + 1, :] for t in tiles], 1) for r in range(5)
        )
        lse_low, lse_high = lse_low * LOG2E, lse_high * LOG2E
        diagonal = own and n == 0

        lses = [lse_high] * count + [lse_high + jnp.where(low_i <= low, 0.0, HIDE) for low in low_j]
        dv, dk, dq_high = tile(
            k, v, kt, queries(0, 1), queries(1, 1), lses, delta_high, count if diagonal else None
        )
        dv_acc[...] = dv if n == 0 else dv_acc[...] + dv
        dk_acc[...] = dk if n == 0 else dk_acc[...] + dk
        lses = [lse_low + jnp.where(low <= low_i, 0.0, HIDE) for low in low_j]
        dv, dk, dq_low = tile(
            k[:half], v[:half], kt[:, :half], queries(0, 0), queries(1, 0), lses, delta_low, 0 if diagonal else None
        )
        dv_acc[:half] += dv
        dk_acc[:half] += dk
        for b, dq in ((0, dq_low), (1, dq_high)):
            if not first:
                dq = dqin_refs[n][b] + dq
            if not last:
                dq_refs[n][0][b] = dq
            else:
                for c in range(4):
                    ref = dq_refs[n][c // 2]
                    ref[c % 2, b * BLK : (b + 1) * BLK, :] = dq[:, c * BLK : (c + 1) * BLK].T.astype(ref.dtype)

    for m in range(count):
        for b in range(2):
            source = slice(b * half + m * BLK, b * half + (m + 1) * BLK)
            for array, acc in ((0, dk_acc), (1, dv_acc)):
                rows = slice((2 * array + b) * BLK, (2 * array + b + 1) * BLK)
                part = acc[source]
                if add:
                    part = addin_ref[m, rows, :] + part
                if split:
                    dkv_refs[m][rows, :] = part.astype(BF16)
                else:
                    dkv_refs[0][m, rows, :] = part.astype(dkv_refs[0].dtype)


def meet_kernel(parts, *refs):
    out_refs = refs[-2:]
    for half, out_ref in enumerate(out_refs):
        total = None
        for ref, index in zip(refs, parts):
            if index[half] is not None:
                part = ref[index[half]].astype(F32)
                total = part if total is None else total + part
        out_ref[...] = total.astype(out_ref.dtype)


def last_kernel(rows_ref, dq_ref, dqx_ref, dkv_ref, dkvz_ref, q_ref, k_ref, v_ref):
    swapped = rows_ref[0, 4 * BLK :, :].astype(F32)[5:6, :] > 0.5

    def restore(out_ref, total):
        low, high = total[:BLK], total[BLK:]
        out_ref[:BLK, :] = jnp.where(swapped, high, low).astype(BF16)
        out_ref[BLK:, :] = jnp.where(swapped, low, high).astype(BF16)

    restore(q_ref, (dq_ref[...] + dqx_ref[...].astype(F32)) * FACTOR)
    dkv = dkv_ref[...] + dkvz_ref[...].astype(F32)
    restore(k_ref, dkv[: 2 * BLK] * FACTOR)
    restore(v_ref, dkv[2 * BLK :])


def z_step(step):
    return [(i, (i + step) % 8) for i in range(8)]


def y_step(step):
    return [(i, (i + step) % 4) for i in range(4)]


Z_PAIRS = [(i, (i - 2) % 8 if i % 2 == 0 else (i + 2) % 8) for i in range(8)]
Z_BACK = [(b, a) for a, b in Z_PAIRS]
X_SWAP = [(0, 1), (1, 0)]


def call(kernel, outs, operands, scratch=(), hbm=False, **options):
    space = pl.BlockSpec(memory_space=pltpu.HBM if hbm else pltpu.VMEM)
    return pl.pallas_call(
        kernel,
        out_shape=[jax.ShapeDtypeStruct(s, t) for s, t in outs],
        in_specs=[space] * len(operands),
        out_specs=[space] * len(outs),
        scratch_shapes=list(scratch),
        compiler_params=pltpu.CompilerParams(vmem_limit_bytes=PREP_VMEM if hbm else VMEM_LIMIT),
        **options,
    )(*operands)


def body(queries, key_rows, value_rows, outputs, out_grad, saved_lse, fold_map):
    operands = (fold_map, out_grad, outputs, saved_lse.T, key_rows, value_rows, queries)
    buffers = [(pltpu.SMEM if n == 0 else pltpu.VMEM)(a.shape, a.dtype) for n, a in enumerate(operands)]
    rows = pltpu.VMEM((ROWS - 4 * BLK, DIM), BF16)
    sems = [pltpu.SemaphoreType.DMA((7,)), pltpu.SemaphoreType.DMA((10,))]
    payload = ((ROWS, DIM), BF16)
    mine_q, mine_k = call(prep_kernel, [payload] * 2, operands, buffers + [rows] * 2 + sems, hbm=True)

    def beside(mine, other):
        both = lax.optimization_barrier(jnp.pad(mine[None], ((0, 1), (0, 0), (0, 0))))
        return lax.dynamic_update_slice(both, other[None], (1, 0, 0))

    other_k = lax.ppermute(mine_k, "kz", z_step(4))
    q0 = beside(mine_q, lax.ppermute(mine_q, "kx", X_SWAP))
    _, other_k = lax.optimization_barrier((q0, other_k))
    k0 = jnp.stack([mine_k, other_k])
    q_sets = [q0] + [lax.ppermute(q0, "kz", p) for p in (z_step(1), z_step(-1), Z_PAIRS)]
    k_sets = [k0] + [lax.ppermute(k0, "pb", y_step(-s)) for s in Y_FROM[1:]]
    q_pairs = ([q_sets[0], q_sets[3]], [q_sets[1], q_sets[2]])

    def grad(turn, js, pairs, dq_in, last, dkv_type, add=None, split=False):
        plan = tuple((d is None, e) for d, e in zip(dq_in, last))
        outs = []
        for pair, end in zip(pairs, last):
            if end:
                outs += [((2, 2 * BLK, DIM), F32 if (pair, s) == (0, 0) else BF16) for s in range(2)]
            else:
                outs.append(((2, DIM, 4 * BLK), F32))
        dkv_out = [((4 * BLK, DIM), BF16)] * len(js) if split else [((len(js), 4 * BLK, DIM), dkv_type)]
        acc = pltpu.VMEM((2 * len(js) * BLK, DIM), F32)
        results = call(
            functools.partial(grad_kernel, js, plan, turn == 0 and pairs[0] == 0, add is not None, split),
            outs + dkv_out,
            [q for p in pairs for q in q_pairs[p]] + [k_sets[turn]] + [d for d in (*dq_in, add) if d is not None],
            [acc, acc],
            cost_estimate=COST,
        )
        return results[: len(outs)], results[len(outs) :]

    def send_back(turn, part):
        return lax.ppermute(part, "pb", y_step(Y_FROM[turn]))

    both = (0, 1)
    (dq1,), (own_a,) = grad(0, (0,), (1,), (None,), (False,), F32)
    q_pairs[0][1], dq1 = lax.optimization_barrier((q_pairs[0][1], dq1))
    (dq1,), (own_b,) = grad(0, (1,), (1,), (dq1,), (False,), F32)
    (dq0, dq1), (part,) = grad(1, both, both, (None, dq1), (False, False), BF16)
    back1 = send_back(1, part)
    (dq0, dq1), (part,) = grad(2, both, both, (dq0, dq1), (False, False), BF16)
    back2 = send_back(2, part)
    (dq0, *dqs), (part,) = grad(3, both, both, (dq0, dq1), (False, True), BF16)
    back3 = send_back(3, part)
    (dq_keep, dq_z2), (own0,) = grad(0, both, (0,), (dq0,), (True,), F32)
    dq_z2, back1, back2 = lax.optimization_barrier((dq_z2, back1, back2))
    dqs.insert(0, dq_z2)
    dq_back = [lax.ppermute(d, "kz", p) for d, p in zip(dqs, (Z_BACK, z_step(-1), z_step(1)))]

    def meet(operands, parts, shape):
        return call(functools.partial(meet_kernel, parts), [(shape, F32), (shape, BF16)], operands)

    dkv_keep, dkv_send = meet(
        [own0, own_a, own_b, back1, back2, back3], [both, (0, None), (None, 0)] + [both] * 3, (4 * BLK, DIM)
    )
    dkv_last = lax.ppermute(dkv_send, "kz", z_step(4))
    dq_keep, dq_send = meet([dq_keep] + dq_back, [both] * 4, (2 * BLK, DIM))
    dq_last = lax.ppermute(dq_send, "kx", X_SWAP)
    operands = (q0, dq_keep, dq_last, dkv_keep, dkv_last)
    return tuple(call(last_kernel, [((2 * BLK, DIM), BF16)] * 3, operands))


def solution(mesh):
    fine = Mesh(mesh.devices.reshape(4, 8, 2, 2, 2), ("pb", "kz", "kx", "hx", "hc"))
    rows = P(("pb", "kz", "kx"), ("hx", "hc"))
    return jax.shard_map(
        body,
        mesh=fine,
        in_specs=(rows,) * 6 + (P(),),
        out_specs=(rows,) * 3,
        check_vma=False,
    )
```

```python
import functools
import math

import jax
import jax.numpy as jnp
from jax import lax
from jax.experimental import pallas as pl
from jax.experimental.pallas import tpu as pltpu
from jax.sharding import Mesh, PartitionSpec as P

F32 = jnp.float32
BF16 = jnp.bfloat16
BLK = 128
DIM = 128
LOG2E = math.log2(math.e)
FACTOR = 1.0 / math.sqrt(DIM)
VMEM_LIMIT = 48 * 1024 * 1024
PREP_VMEM = 62 * 1024 * 1024
COST = pl.CostEstimate(flops=500000000, bytes_accessed=1000000, transcendentals=0)
HIDE = 1e30
Y_FROM = (0, 2, 3, 1)
NT = (((1,), (1,)), ((), ()))
ROWS = 4 * BLK + 16


def dot(a, b):
    return jnp.dot(a, b, preferred_element_type=F32)


def dot_nt(a, b):
    return lax.dot_general(a, b, NT, preferred_element_type=F32)


def prep_kernel(*refs):
    sources, (qout_ref, kout_ref), buffers, refs = refs[:7], refs[7:9], refs[9:16], refs[16:]
    qrows_buf, krows_buf, load_sems, store_sems = refs
    loads = [pltpu.make_async_copy(s, d, load_sems.at[n]) for n, (s, d) in enumerate(zip(sources, buffers))]
    for copy in loads:
        copy.start()
    stores = []

    def store(source, target):
        stores.append(pltpu.make_async_copy(source, target, store_sems.at[len(stores)]))
        stores[-1].start()

    def store_blocks(n, out_ref, at):
        loads[n].wait()
        store(buffers[n].at[pl.ds(low_at, BLK)], out_ref.at[at : at + BLK])
        store(buffers[n].at[pl.ds(high_at, BLK)], out_ref.at[at + BLK : at + 2 * BLK])

    fold_ref, g_buf, o_buf, lse_buf = buffers[:4]
    device = lax.axis_index("pb") * 16 + lax.axis_index("kz") * 2 + lax.axis_index("kx")
    loads[0].wait()
    first, second = fold_ref[2 * device], fold_ref[2 * device + 1]
    swapped = second < first
    low_at = pl.multiple_of(jnp.where(swapped, BLK, 0), BLK)
    high_at = pl.multiple_of(jnp.where(swapped, 0, BLK), BLK)
    low = jnp.minimum(first, second).astype(F32)
    krows_buf[...] = jnp.full(krows_buf.shape, low, F32).astype(BF16)
    store(krows_buf, kout_ref.at[4 * BLK :])
    store_blocks(1, qout_ref, 2 * BLK)
    loads[2].wait()
    loads[3].wait()
    lse = lse_buf[...].astype(F32)
    rows = [jnp.where(swapped, lse[:, BLK:], lse[:, :BLK]), jnp.where(swapped, lse[:, :BLK], lse[:, BLK:])]
    for at in (low_at, high_at):
        prod = g_buf[pl.ds(at, BLK), :].astype(F32) * o_buf[pl.ds(at, BLK), :].astype(F32)
        rows.append(jnp.sum(prod.T, axis=0, keepdims=True))
    rows.append(jnp.full((1, DIM), low, F32))
    rows.append(jnp.full((1, DIM), jnp.where(swapped, 1.0, 0.0), F32))
    qrows_buf[...] = jnp.concatenate(rows + [jnp.zeros((10, DIM), F32)], axis=0).astype(BF16)
    store(qrows_buf, qout_ref.at[4 * BLK :])
    store_blocks(6, qout_ref, 0)
    store_blocks(4, kout_ref, 0)
    store_blocks(5, kout_ref, 2 * BLK)
    for copy in stores:
        copy.wait()


def tile(k, v, kt, q, g, lses, delta, diagonal=None):
    s = dot_nt(k, q)
    probs = []
    for b, lse in enumerate(lses):
        p = jnp.exp2(s[b * BLK : (b + 1) * BLK] * (FACTOR * LOG2E) - lse)
        if b == diagonal:
            shape = (BLK, BLK)
            seen = lax.broadcasted_iota(jnp.int32, shape, 0) <= lax.broadcasted_iota(jnp.int32, shape, 1)
            p = jnp.concatenate([jnp.where(seen, p[:, :BLK], 0.0), p[:, BLK:]], 1)
        probs.append(p)
    p = jnp.concatenate(probs, 0)
    dp = dot_nt(v, g)
    ds = (p * (dp - delta)).astype(BF16)
    return dot(p.astype(BF16), g), dot(ds, q), dot(kt, ds)


def grad_kernel(js, plan, own, add, split, *refs):
    refs = list(refs)

    def take(count):
        taken = refs[:count]
        del refs[:count]
        return taken

    q_refs, (y_ref,) = take(2 * len(plan)), take(1)
    dqin_refs = [None if first else take(1)[0] for first, _ in plan]
    addin_ref = refs.pop(0) if add else None
    dq_refs = [take(2 if last else 1) for _, last in plan]
    dkv_refs = take(len(js)) if split else [refs.pop(0)]
    dv_acc, dk_acc = refs
    count = len(js)
    half = count * BLK

    def keys(array):
        at = array * 2 * BLK
        return jnp.concatenate([y_ref[j, at + b * BLK : at + (b + 1) * BLK, :] for b in range(2) for j in js], 0)

    k, v = keys(0), keys(1)
    kt = k.T
    low_j = [jnp.concatenate([y_ref[j, 4 * BLK :, :].astype(F32)[0:1, :]] * 4, 1) for j in js]

    for n, (first, last) in enumerate(plan):
        pair = q_refs[2 * n : 2 * n + 2]
        chunks = [(ref, a) for ref in pair for a in range(2)]

        def queries(array, b):
            at = (2 * array + b) * BLK
            return jnp.concatenate([ref[a, at : at + BLK, :] for ref, a in chunks], 0)

        tiles = [ref[a, 4 * BLK :, :].astype(F32) for ref, a in chunks]
        lse_low, lse_high, delta_low, delta_high, low_i = (
            jnp.concatenate([t[r : r + 1, :] for t in tiles], 1) for r in range(5)
        )
        lse_low, lse_high = lse_low * LOG2E, lse_high * LOG2E
        diagonal = own and n == 0

        lses = [lse_high] * count + [lse_high + jnp.where(low_i <= low, 0.0, HIDE) for low in low_j]
        dv, dk, dq_high = tile(
            k, v, kt, queries(0, 1), queries(1, 1), lses, delta_high, count if diagonal else None
        )
        dv_acc[...] = dv if n == 0 else dv_acc[...] + dv
        dk_acc[...] = dk if n == 0 else dk_acc[...] + dk
        lses = [lse_low + jnp.where(low <= low_i, 0.0, HIDE) for low in low_j]
        dv, dk, dq_low = tile(
            k[:half], v[:half], kt[:, :half], queries(0, 0), queries(1, 0), lses, delta_low, 0 if diagonal else None
        )
        dv_acc[:half] += dv
        dk_acc[:half] += dk
        for b, dq in ((0, dq_low), (1, dq_high)):
            if not first:
                dq = dqin_refs[n][b] + dq
            if not last:
                dq_refs[n][0][b] = dq
            else:
                for c in range(4):
                    ref = dq_refs[n][c // 2]
                    ref[c % 2, b * BLK : (b + 1) * BLK, :] = dq[:, c * BLK : (c + 1) * BLK].T.astype(ref.dtype)

    for m in range(count):
        for b in range(2):
            source = slice(b * half + m * BLK, b * half + (m + 1) * BLK)
            for array, acc in ((0, dk_acc), (1, dv_acc)):
                rows = slice((2 * array + b) * BLK, (2 * array + b + 1) * BLK)
                part = acc[source]
                if add:
                    part = addin_ref[m, rows, :] + part
                if split:
                    dkv_refs[m][rows, :] = part.astype(BF16)
                else:
                    dkv_refs[0][m, rows, :] = part.astype(dkv_refs[0].dtype)


def meet_kernel(parts, *refs):
    out_refs = refs[-2:]
    for half, out_ref in enumerate(out_refs):
        total = None
        for ref, index in zip(refs, parts):
            if index[half] is not None:
                part = ref[index[half]].astype(F32)
                total = part if total is None else total + part
        out_ref[...] = total.astype(out_ref.dtype)


def last_kernel(rows_ref, dq_ref, dqx_ref, dkv_ref, dkvz_ref, q_ref, k_ref, v_ref):
    swapped = rows_ref[0, 4 * BLK :, :].astype(F32)[5:6, :] > 0.5

    def restore(out_ref, total):
        low, high = total[:BLK], total[BLK:]
        out_ref[:BLK, :] = jnp.where(swapped, high, low).astype(BF16)
        out_ref[BLK:, :] = jnp.where(swapped, low, high).astype(BF16)

    restore(q_ref, (dq_ref[...] + dqx_ref[...].astype(F32)) * FACTOR)
    dkv = dkv_ref[...] + dkvz_ref[...].astype(F32)
    restore(k_ref, dkv[: 2 * BLK] * FACTOR)
    restore(v_ref, dkv[2 * BLK :])


def z_step(step):
    return [(i, (i + step) % 8) for i in range(8)]


def y_step(step):
    return [(i, (i + step) % 4) for i in range(4)]


Z_PAIRS = [(i, (i - 2) % 8 if i % 2 == 0 else (i + 2) % 8) for i in range(8)]
Z_BACK = [(b, a) for a, b in Z_PAIRS]
X_SWAP = [(0, 1), (1, 0)]


def call(kernel, outs, operands, scratch=(), hbm=False, **options):
    space = pl.BlockSpec(memory_space=pltpu.HBM if hbm else pltpu.VMEM)
    return pl.pallas_call(
        kernel,
        out_shape=[jax.ShapeDtypeStruct(s, t) for s, t in outs],
        in_specs=[space] * len(operands),
        out_specs=[space] * len(outs),
        scratch_shapes=list(scratch),
        compiler_params=pltpu.CompilerParams(vmem_limit_bytes=PREP_VMEM if hbm else VMEM_LIMIT),
        **options,
    )(*operands)


def body(queries, key_rows, value_rows, outputs, out_grad, saved_lse, fold_map):
    operands = (fold_map, out_grad, outputs, saved_lse.T, key_rows, value_rows, queries)
    buffers = [(pltpu.SMEM if n == 0 else pltpu.VMEM)(a.shape, a.dtype) for n, a in enumerate(operands)]
    rows = pltpu.VMEM((ROWS - 4 * BLK, DIM), BF16)
    sems = [pltpu.SemaphoreType.DMA((7,)), pltpu.SemaphoreType.DMA((10,))]
    payload = ((ROWS, DIM), BF16)
    mine_q, mine_k = call(prep_kernel, [payload] * 2, operands, buffers + [rows] * 2 + sems, hbm=True)

    def beside(mine, other):
        both = lax.optimization_barrier(jnp.pad(mine[None], ((0, 1), (0, 0), (0, 0))))
        return lax.dynamic_update_slice(both, other[None], (1, 0, 0))

    other_k = lax.ppermute(mine_k, "kz", z_step(4))
    q0 = beside(mine_q, lax.ppermute(mine_q, "kx", X_SWAP))
    _, other_k = lax.optimization_barrier((q0, other_k))
    k0 = jnp.stack([mine_k, other_k])
    q_sets = [q0] + [lax.ppermute(q0, "kz", p) for p in (z_step(1), z_step(-1), Z_PAIRS)]
    k_sets = [k0] + [lax.ppermute(k0, "pb", y_step(-s)) for s in Y_FROM[1:]]
    q_pairs = ([q_sets[0], q_sets[3]], [q_sets[1], q_sets[2]])

    def grad(turn, js, pairs, dq_in, last, dkv_type, add=None, split=False):
        plan = tuple((d is None, e) for d, e in zip(dq_in, last))
        outs = []
        for pair, end in zip(pairs, last):
            if end:
                outs += [((2, 2 * BLK, DIM), F32 if (pair, s) == (0, 0) else BF16) for s in range(2)]
            else:
                outs.append(((2, DIM, 4 * BLK), F32))
        dkv_out = [((4 * BLK, DIM), BF16)] * len(js) if split else [((len(js), 4 * BLK, DIM), dkv_type)]
        acc = pltpu.VMEM((2 * len(js) * BLK, DIM), F32)
        results = call(
            functools.partial(grad_kernel, js, plan, turn == 0 and pairs[0] == 0, add is not None, split),
            outs + dkv_out,
            [q for p in pairs for q in q_pairs[p]] + [k_sets[turn]] + [d for d in (*dq_in, add) if d is not None],
            [acc, acc],
            cost_estimate=COST,
        )
        return results[: len(outs)], results[len(outs) :]

    def send_back(turn, part):
        return lax.ppermute(part, "pb", y_step(Y_FROM[turn]))

    both = (0, 1)
    (dq1,), (own_a,) = grad(0, (0,), (1,), (None,), (False,), F32)
    q_pairs[0][1], dq1 = lax.optimization_barrier((q_pairs[0][1], dq1))
    (dq1,), (own_b,) = grad(0, (1,), (1,), (dq1,), (False,), F32)
    (dq0, dq1), (part,) = grad(1, both, both, (None, dq1), (False, False), BF16)
    back1 = send_back(1, part)
    (dq0, dq1), (part,) = grad(2, both, both, (dq0, dq1), (False, False), BF16)
    back2 = send_back(2, part)
    (dq0, *dqs), (part,) = grad(3, both, both, (dq0, dq1), (False, True), BF16)
    back3 = send_back(3, part)
    dq0, back1 = lax.optimization_barrier((dq0, back1))
    (dq_keep, dq_z2), (own0,) = grad(0, both, (0,), (dq0,), (True,), F32)
    dq_z2, back2 = lax.optimization_barrier((dq_z2, back2))
    dqs.insert(0, dq_z2)
    dq_back = [lax.ppermute(d, "kz", p) for d, p in zip(dqs, (Z_BACK, z_step(-1), z_step(1)))]

    def meet(operands, parts, shape):
        return call(functools.partial(meet_kernel, parts), [(shape, F32), (shape, BF16)], operands)

    dkv_keep, dkv_send = meet(
        [own0, own_a, own_b, back1, back2, back3], [both, (0, None), (None, 0)] + [both] * 3, (4 * BLK, DIM)
    )
    dkv_last = lax.ppermute(dkv_send, "kz", z_step(4))
    dq_keep, dq_send = meet([dq_keep] + dq_back, [both] * 4, (2 * BLK, DIM))
    dq_last = lax.ppermute(dq_send, "kx", X_SWAP)
    operands = (q0, dq_keep, dq_last, dkv_keep, dkv_last)
    return tuple(call(last_kernel, [((2 * BLK, DIM), BF16)] * 3, operands))


def solution(mesh):
    fine = Mesh(mesh.devices.reshape(4, 8, 2, 2, 2), ("pb", "kz", "kx", "hx", "hc"))
    rows = P(("pb", "kz", "kx"), ("hx", "hc"))
    return jax.shard_map(
        body,
        mesh=fine,
        in_specs=(rows,) * 6 + (P(),),
        out_specs=(rows,) * 3,
        check_vma=False,
    )
```

```python
import functools
import math

import jax
import jax.numpy as jnp
from jax import lax
from jax.experimental import pallas as pl
from jax.experimental.pallas import tpu as pltpu
from jax.sharding import Mesh, PartitionSpec as P

F32 = jnp.float32
BF16 = jnp.bfloat16
BLK = 128
DIM = 128
LOG2E = math.log2(math.e)
FACTOR = 1.0 / math.sqrt(DIM)
VMEM_LIMIT = 48 * 1024 * 1024
PREP_VMEM = 62 * 1024 * 1024
COST = pl.CostEstimate(flops=500000000, bytes_accessed=1000000, transcendentals=0)
HIDE = 1e30
Y_FROM = (0, 2, 3, 1)
NT = (((1,), (1,)), ((), ()))
ROWS = 4 * BLK + 16


def dot(a, b):
    return jnp.dot(a, b, preferred_element_type=F32)


def dot_nt(a, b):
    return lax.dot_general(a, b, NT, preferred_element_type=F32)


def prep_kernel(*refs):
    sources, (qout_ref, kout_ref), buffers, refs = refs[:7], refs[7:9], refs[9:16], refs[16:]
    qrows_buf, krows_buf, load_sems, store_sems = refs
    loads = [pltpu.make_async_copy(s, d, load_sems.at[n]) for n, (s, d) in enumerate(zip(sources, buffers))]
    for copy in loads:
        copy.start()
    stores = []

    def store(source, target):
        stores.append(pltpu.make_async_copy(source, target, store_sems.at[len(stores)]))
        stores[-1].start()

    def store_blocks(n, out_ref, at):
        loads[n].wait()
        store(buffers[n].at[pl.ds(low_at, BLK)], out_ref.at[at : at + BLK])
        store(buffers[n].at[pl.ds(high_at, BLK)], out_ref.at[at + BLK : at + 2 * BLK])

    fold_ref, g_buf, o_buf, lse_buf = buffers[:4]
    device = lax.axis_index("pb") * 16 + lax.axis_index("kz") * 2 + lax.axis_index("kx")
    loads[0].wait()
    first, second = fold_ref[2 * device], fold_ref[2 * device + 1]
    swapped = second < first
    low_at = pl.multiple_of(jnp.where(swapped, BLK, 0), BLK)
    high_at = pl.multiple_of(jnp.where(swapped, 0, BLK), BLK)
    low = jnp.minimum(first, second).astype(F32)
    krows_buf[...] = jnp.full(krows_buf.shape, low, F32).astype(BF16)
    store(krows_buf, kout_ref.at[4 * BLK :])
    store_blocks(1, qout_ref, 2 * BLK)
    loads[2].wait()
    loads[3].wait()
    lse = lse_buf[...].astype(F32)
    rows = [jnp.where(swapped, lse[:, BLK:], lse[:, :BLK]), jnp.where(swapped, lse[:, :BLK], lse[:, BLK:])]
    for at in (low_at, high_at):
        prod = g_buf[pl.ds(at, BLK), :].astype(F32) * o_buf[pl.ds(at, BLK), :].astype(F32)
        rows.append(jnp.sum(prod.T, axis=0, keepdims=True))
    rows.append(jnp.full((1, DIM), low, F32))
    rows.append(jnp.full((1, DIM), jnp.where(swapped, 1.0, 0.0), F32))
    qrows_buf[...] = jnp.concatenate(rows + [jnp.zeros((10, DIM), F32)], axis=0).astype(BF16)
    store(qrows_buf, qout_ref.at[4 * BLK :])
    store_blocks(6, qout_ref, 0)
    store_blocks(4, kout_ref, 0)
    store_blocks(5, kout_ref, 2 * BLK)
    for copy in stores:
        copy.wait()


def tile(k, v, kt, q, g, lses, delta, diagonal=None):
    s = dot_nt(k, q)
    probs = []
    for b, lse in enumerate(lses):
        p = jnp.exp2(s[b * BLK : (b + 1) * BLK] * (FACTOR * LOG2E) - lse)
        if b == diagonal:
            shape = (BLK, BLK)
            seen = lax.broadcasted_iota(jnp.int32, shape, 0) <= lax.broadcasted_iota(jnp.int32, shape, 1)
            p = jnp.concatenate([jnp.where(seen, p[:, :BLK], 0.0), p[:, BLK:]], 1)
        probs.append(p)
    p = jnp.concatenate(probs, 0)
    dp = dot_nt(v, g)
    ds = (p * (dp - delta)).astype(BF16)
    return dot(p.astype(BF16), g), dot(ds, q), dot(kt, ds)


def grad_kernel(js, plan, own, add, split, *refs):
    refs = list(refs)

    def take(count):
        taken = refs[:count]
        del refs[:count]
        return taken

    q_refs, (y_ref,) = take(2 * len(plan)), take(1)
    dqin_refs = [None if first else take(1)[0] for first, _ in plan]
    addin_ref = refs.pop(0) if add else None
    dq_refs = [take(2 if last else 1) for _, last in plan]
    dkv_refs = take(len(js)) if split else [refs.pop(0)]
    dv_acc, dk_acc = refs
    count = len(js)
    half = count * BLK

    def keys(array):
        at = array * 2 * BLK
        return jnp.concatenate([y_ref[j, at + b * BLK : at + (b + 1) * BLK, :] for b in range(2) for j in js], 0)

    k, v = keys(0), keys(1)
    kt = k.T
    low_j = [jnp.concatenate([y_ref[j, 4 * BLK :, :].astype(F32)[0:1, :]] * 4, 1) for j in js]

    for n, (first, last) in enumerate(plan):
        pair = q_refs[2 * n : 2 * n + 2]
        chunks = [(ref, a) for ref in pair for a in range(2)]

        def queries(array, b):
            at = (2 * array + b) * BLK
            return jnp.concatenate([ref[a, at : at + BLK, :] for ref, a in chunks], 0)

        tiles = [ref[a, 4 * BLK :, :].astype(F32) for ref, a in chunks]
        lse_low, lse_high, delta_low, delta_high, low_i = (
            jnp.concatenate([t[r : r + 1, :] for t in tiles], 1) for r in range(5)
        )
        lse_low, lse_high = lse_low * LOG2E, lse_high * LOG2E
        diagonal = own and n == 0

        lses = [lse_high] * count + [lse_high + jnp.where(low_i <= low, 0.0, HIDE) for low in low_j]
        dv, dk, dq_high = tile(
            k, v, kt, queries(0, 1), queries(1, 1), lses, delta_high, count if diagonal else None
        )
        dv_acc[...] = dv if n == 0 else dv_acc[...] + dv
        dk_acc[...] = dk if n == 0 else dk_acc[...] + dk
        lses = [lse_low + jnp.where(low <= low_i, 0.0, HIDE) for low in low_j]
        dv, dk, dq_low = tile(
            k[:half], v[:half], kt[:, :half], queries(0, 0), queries(1, 0), lses, delta_low, 0 if diagonal else None
        )
        dv_acc[:half] += dv
        dk_acc[:half] += dk
        for b, dq in ((0, dq_low), (1, dq_high)):
            if not first:
                dq = dqin_refs[n][b] + dq
            if not last:
                dq_refs[n][0][b] = dq
            else:
                for c in range(4):
                    ref = dq_refs[n][c // 2]
                    ref[c % 2, b * BLK : (b + 1) * BLK, :] = dq[:, c * BLK : (c + 1) * BLK].T.astype(ref.dtype)

    for m in range(count):
        for b in range(2):
            source = slice(b * half + m * BLK, b * half + (m + 1) * BLK)
            for array, acc in ((0, dk_acc), (1, dv_acc)):
                rows = slice((2 * array + b) * BLK, (2 * array + b + 1) * BLK)
                part = acc[source]
                if add:
                    part = addin_ref[m, rows, :] + part
                if split:
                    dkv_refs[m][rows, :] = part.astype(BF16)
                else:
                    dkv_refs[0][m, rows, :] = part.astype(dkv_refs[0].dtype)


def meet_kernel(parts, *refs):
    out_refs = refs[-2:]
    for half, out_ref in enumerate(out_refs):
        total = None
        for ref, index in zip(refs, parts):
            if index[half] is not None:
                part = ref[index[half]].astype(F32)
                total = part if total is None else total + part
        out_ref[...] = total.astype(out_ref.dtype)


def last_kernel(rows_ref, dq_ref, dqx_ref, dkv_ref, dkvz_ref, q_ref, k_ref, v_ref):
    swapped = rows_ref[0, 4 * BLK :, :].astype(F32)[5:6, :] > 0.5

    def restore(out_ref, total):
        low, high = total[:BLK], total[BLK:]
        out_ref[:BLK, :] = jnp.where(swapped, high, low).astype(BF16)
        out_ref[BLK:, :] = jnp.where(swapped, low, high).astype(BF16)

    restore(q_ref, (dq_ref[...] + dqx_ref[...].astype(F32)) * FACTOR)
    dkv = dkv_ref[...] + dkvz_ref[...].astype(F32)
    restore(k_ref, dkv[: 2 * BLK] * FACTOR)
    restore(v_ref, dkv[2 * BLK :])


def z_step(step):
    return [(i, (i + step) % 8) for i in range(8)]


def y_step(step):
    return [(i, (i + step) % 4) for i in range(4)]


Z_PAIRS = [(i, (i - 2) % 8 if i % 2 == 0 else (i + 2) % 8) for i in range(8)]
Z_BACK = [(b, a) for a, b in Z_PAIRS]
X_SWAP = [(0, 1), (1, 0)]


def call(kernel, outs, operands, scratch=(), hbm=False, **options):
    space = pl.BlockSpec(memory_space=pltpu.HBM if hbm else pltpu.VMEM)
    return pl.pallas_call(
        kernel,
        out_shape=[jax.ShapeDtypeStruct(s, t) for s, t in outs],
        in_specs=[space] * len(operands),
        out_specs=[space] * len(outs),
        scratch_shapes=list(scratch),
        compiler_params=pltpu.CompilerParams(vmem_limit_bytes=PREP_VMEM if hbm else VMEM_LIMIT),
        **options,
    )(*operands)


def body(queries, key_rows, value_rows, outputs, out_grad, saved_lse, fold_map):
    operands = (fold_map, out_grad, outputs, saved_lse.T, key_rows, value_rows, queries)
    buffers = [(pltpu.SMEM if n == 0 else pltpu.VMEM)(a.shape, a.dtype) for n, a in enumerate(operands)]
    rows = pltpu.VMEM((ROWS - 4 * BLK, DIM), BF16)
    sems = [pltpu.SemaphoreType.DMA((7,)), pltpu.SemaphoreType.DMA((10,))]
    payload = ((ROWS, DIM), BF16)
    mine_q, mine_k = call(prep_kernel, [payload] * 2, operands, buffers + [rows] * 2 + sems, hbm=True)

    def beside(mine, other):
        both = lax.optimization_barrier(jnp.pad(mine[None], ((0, 1), (0, 0), (0, 0))))
        return lax.dynamic_update_slice(both, other[None], (1, 0, 0))

    other_k = lax.ppermute(mine_k, "kz", z_step(4))
    q0 = beside(mine_q, lax.ppermute(mine_q, "kx", X_SWAP))
    late_q, other_k = lax.optimization_barrier((q0, other_k))
    k0 = jnp.stack([mine_k, other_k])
    q_sets = [q0] + [lax.ppermute(q, "kz", p) for q, p in ((q0, z_step(1)), (q0, z_step(-1)), (late_q, Z_PAIRS))]
    k_sets = [k0] + [lax.ppermute(k0, "pb", y_step(-s)) for s in Y_FROM[1:]]
    q_pairs = ([q_sets[0], q_sets[3]], [q_sets[1], q_sets[2]])

    def grad(turn, js, pairs, dq_in, last, dkv_type, add=None, split=False):
        plan = tuple((d is None, e) for d, e in zip(dq_in, last))
        outs = []
        for pair, end in zip(pairs, last):
            if end:
                outs += [((2, 2 * BLK, DIM), F32 if (pair, s) == (0, 0) else BF16) for s in range(2)]
            else:
                outs.append(((2, DIM, 4 * BLK), F32))
        dkv_out = [((4 * BLK, DIM), BF16)] * len(js) if split else [((len(js), 4 * BLK, DIM), dkv_type)]
        acc = pltpu.VMEM((2 * len(js) * BLK, DIM), F32)
        results = call(
            functools.partial(grad_kernel, js, plan, turn == 0 and pairs[0] == 0, add is not None, split),
            outs + dkv_out,
            [q for p in pairs for q in q_pairs[p]] + [k_sets[turn]] + [d for d in (*dq_in, add) if d is not None],
            [acc, acc],
            cost_estimate=COST,
        )
        return results[: len(outs)], results[len(outs) :]

    def send_back(turn, part):
        return lax.ppermute(part, "pb", y_step(Y_FROM[turn]))

    both = (0, 1)
    parts = []
    dq1 = None
    for turn in range(4):
        dq1, (part,) = grad(turn, both, (1,), (dq1,), (turn == 3,), F32)
        dq1 = dq1[0] if turn < 3 else dq1
        parts.append(part)
    dq_back = [lax.ppermute(d, "kz", p) for d, p in zip(dq1, (z_step(-1), z_step(1)))]
    q_pairs[0][1], parts[3] = lax.optimization_barrier((q_pairs[0][1], parts[3]))
    back = []
    dq0 = None
    for turn in (1, 2, 3):
        (dq0,), (part,) = grad(turn, both, (0,), (dq0,), (False,), BF16, add=parts[turn])
        back.append(send_back(turn, part))
    dq0, back[0] = lax.optimization_barrier((dq0, back[0]))
    (dq_keep, dq_z2), (own,) = grad(0, both, (0,), (dq0,), (True,), F32, add=parts[0])
    dq_back.append(lax.ppermute(dq_z2, "kz", Z_BACK))

    def meet(operands, parts, shape):
        return call(functools.partial(meet_kernel, parts), [(shape, F32), (shape, BF16)], operands)

    dkv_keep, dkv_send = meet(
        [own] + back, [both] * 4, (4 * BLK, DIM)
    )
    dkv_last = lax.ppermute(dkv_send, "kz", z_step(4))
    dq_keep, dq_send = meet([dq_keep] + dq_back, [both] * 4, (2 * BLK, DIM))
    dq_last = lax.ppermute(dq_send, "kx", X_SWAP)
    operands = (q0, dq_keep, dq_last, dkv_keep, dkv_last)
    return tuple(call(last_kernel, [((2 * BLK, DIM), BF16)] * 3, operands))


def solution(mesh):
    fine = Mesh(mesh.devices.reshape(4, 8, 2, 2, 2), ("pb", "kz", "kx", "hx", "hc"))
    rows = P(("pb", "kz", "kx"), ("hx", "hc"))
    return jax.shard_map(
        body,
        mesh=fine,
        in_specs=(rows,) * 6 + (P(),),
        out_specs=(rows,) * 3,
        check_vma=False,
    )
```

```python
import functools
import math

import jax
import jax.numpy as jnp
from jax import lax
from jax.experimental import pallas as pl
from jax.experimental.pallas import tpu as pltpu
from jax.sharding import Mesh, PartitionSpec as P

F32 = jnp.float32
BF16 = jnp.bfloat16
BLK = 128
DIM = 128
LOG2E = math.log2(math.e)
FACTOR = 1.0 / math.sqrt(DIM)
VMEM_LIMIT = 48 * 1024 * 1024
PREP_VMEM = 62 * 1024 * 1024
COST = pl.CostEstimate(flops=500000000, bytes_accessed=1000000, transcendentals=0)
HIDE = 1e30
Y_FROM = (0, 2, 3, 1)
NT = (((1,), (1,)), ((), ()))
ROWS = 4 * BLK + 16


def dot(a, b):
    return jnp.dot(a, b, preferred_element_type=F32)


def dot_nt(a, b):
    return lax.dot_general(a, b, NT, preferred_element_type=F32)


def prep_kernel(*refs):
    sources, (qout_ref, kout_ref), buffers, refs = refs[:7], refs[7:9], refs[9:16], refs[16:]
    qrows_buf, krows_buf, load_sems, store_sems = refs
    loads = [pltpu.make_async_copy(s, d, load_sems.at[n]) for n, (s, d) in enumerate(zip(sources, buffers))]
    for copy in loads:
        copy.start()
    stores = []

    def store(source, target):
        stores.append(pltpu.make_async_copy(source, target, store_sems.at[len(stores)]))
        stores[-1].start()

    def store_blocks(n, out_ref, at):
        loads[n].wait()
        store(buffers[n].at[pl.ds(low_at, BLK)], out_ref.at[at : at + BLK])
        store(buffers[n].at[pl.ds(high_at, BLK)], out_ref.at[at + BLK : at + 2 * BLK])

    fold_ref, g_buf, o_buf, lse_buf = buffers[:4]
    device = lax.axis_index("pb") * 16 + lax.axis_index("kz") * 2 + lax.axis_index("kx")
    loads[0].wait()
    first, second = fold_ref[2 * device], fold_ref[2 * device + 1]
    swapped = second < first
    low_at = pl.multiple_of(jnp.where(swapped, BLK, 0), BLK)
    high_at = pl.multiple_of(jnp.where(swapped, 0, BLK), BLK)
    low = jnp.minimum(first, second).astype(F32)
    krows_buf[...] = jnp.full(krows_buf.shape, low, F32).astype(BF16)
    store(krows_buf, kout_ref.at[4 * BLK :])
    store_blocks(1, qout_ref, 2 * BLK)
    loads[2].wait()
    loads[3].wait()
    lse = lse_buf[...].astype(F32)
    rows = [jnp.where(swapped, lse[:, BLK:], lse[:, :BLK]), jnp.where(swapped, lse[:, :BLK], lse[:, BLK:])]
    for at in (low_at, high_at):
        prod = g_buf[pl.ds(at, BLK), :].astype(F32) * o_buf[pl.ds(at, BLK), :].astype(F32)
        rows.append(jnp.sum(prod.T, axis=0, keepdims=True))
    rows.append(jnp.full((1, DIM), low, F32))
    rows.append(jnp.full((1, DIM), jnp.where(swapped, 1.0, 0.0), F32))
    qrows_buf[...] = jnp.concatenate(rows + [jnp.zeros((10, DIM), F32)], axis=0).astype(BF16)
    store(qrows_buf, qout_ref.at[4 * BLK :])
    store_blocks(6, qout_ref, 0)
    store_blocks(4, kout_ref, 0)
    store_blocks(5, kout_ref, 2 * BLK)
    for copy in stores:
        copy.wait()


def tile(k, v, kt, q, g, lses, delta, diagonal=None):
    s = dot_nt(k, q)
    probs = []
    for b, lse in enumerate(lses):
        p = jnp.exp2(s[b * BLK : (b + 1) * BLK] * (FACTOR * LOG2E) - lse)
        if b == diagonal:
            shape = (BLK, BLK)
            seen = lax.broadcasted_iota(jnp.int32, shape, 0) <= lax.broadcasted_iota(jnp.int32, shape, 1)
            p = jnp.concatenate([jnp.where(seen, p[:, :BLK], 0.0), p[:, BLK:]], 1)
        probs.append(p)
    p = jnp.concatenate(probs, 0)
    dp = dot_nt(v, g)
    ds = (p * (dp - delta)).astype(BF16)
    return dot(p.astype(BF16), g), dot(ds, q), dot(kt, ds)


def grad_kernel(js, plan, own, add, split, *refs):
    refs = list(refs)

    def take(count):
        taken = refs[:count]
        del refs[:count]
        return taken

    q_refs, (y_ref,) = take(2 * len(plan)), take(1)
    dqin_refs = [None if first else take(1)[0] for first, _ in plan]
    addin_ref = refs.pop(0) if add else None
    dq_refs = [take(2 if last else 1) for _, last in plan]
    dkv_refs = take(len(js)) if split else [refs.pop(0)]
    dv_acc, dk_acc = refs
    count = len(js)
    half = count * BLK

    def keys(array):
        at = array * 2 * BLK
        return jnp.concatenate([y_ref[j, at + b * BLK : at + (b + 1) * BLK, :] for b in range(2) for j in js], 0)

    k, v = keys(0), keys(1)
    kt = k.T
    low_j = [jnp.concatenate([y_ref[j, 4 * BLK :, :].astype(F32)[0:1, :]] * 4, 1) for j in js]

    for n, (first, last) in enumerate(plan):
        pair = q_refs[2 * n : 2 * n + 2]
        chunks = [(ref, a) for ref in pair for a in range(2)]

        def queries(array, b):
            at = (2 * array + b) * BLK
            return jnp.concatenate([ref[a, at : at + BLK, :] for ref, a in chunks], 0)

        tiles = [ref[a, 4 * BLK :, :].astype(F32) for ref, a in chunks]
        lse_low, lse_high, delta_low, delta_high, low_i = (
            jnp.concatenate([t[r : r + 1, :] for t in tiles], 1) for r in range(5)
        )
        lse_low, lse_high = lse_low * LOG2E, lse_high * LOG2E
        diagonal = own and n == 0

        lses = [lse_high] * count + [lse_high + jnp.where(low_i <= low, 0.0, HIDE) for low in low_j]
        dv, dk, dq_high = tile(
            k, v, kt, queries(0, 1), queries(1, 1), lses, delta_high, count if diagonal else None
        )
        dv_acc[...] = dv if n == 0 else dv_acc[...] + dv
        dk_acc[...] = dk if n == 0 else dk_acc[...] + dk
        lses = [lse_low + jnp.where(low <= low_i, 0.0, HIDE) for low in low_j]
        dv, dk, dq_low = tile(
            k[:half], v[:half], kt[:, :half], queries(0, 0), queries(1, 0), lses, delta_low, 0 if diagonal else None
        )
        dv_acc[:half] += dv
        dk_acc[:half] += dk
        for b, dq in ((0, dq_low), (1, dq_high)):
            if not first:
                dq = dqin_refs[n][b] + dq
            if not last:
                dq_refs[n][0][b] = dq
            else:
                for c in range(4):
                    ref = dq_refs[n][c // 2]
                    ref[c % 2, b * BLK : (b + 1) * BLK, :] = dq[:, c * BLK : (c + 1) * BLK].T.astype(ref.dtype)

    for m in range(count):
        for b in range(2):
            source = slice(b * half + m * BLK, b * half + (m + 1) * BLK)
            for array, acc in ((0, dk_acc), (1, dv_acc)):
                rows = slice((2 * array + b) * BLK, (2 * array + b + 1) * BLK)
                part = acc[source]
                if add:
                    part = addin_ref[m, rows, :] + part
                if split:
                    dkv_refs[m][rows, :] = part.astype(BF16)
                else:
                    dkv_refs[0][m, rows, :] = part.astype(dkv_refs[0].dtype)


def meet_kernel(parts, *refs):
    out_refs = refs[-2:]
    for half, out_ref in enumerate(out_refs):
        total = None
        for ref, index in zip(refs, parts):
            if index[half] is not None:
                part = ref[index[half]].astype(F32)
                total = part if total is None else total + part
        out_ref[...] = total.astype(out_ref.dtype)


def last_kernel(rows_ref, dq_ref, dqx_ref, dkv_ref, dkvz_ref, q_ref, k_ref, v_ref):
    swapped = rows_ref[0, 4 * BLK :, :].astype(F32)[5:6, :] > 0.5

    def restore(out_ref, total):
        low, high = total[:BLK], total[BLK:]
        out_ref[:BLK, :] = jnp.where(swapped, high, low).astype(BF16)
        out_ref[BLK:, :] = jnp.where(swapped, low, high).astype(BF16)

    restore(q_ref, (dq_ref[...] + dqx_ref[...].astype(F32)) * FACTOR)
    dkv = dkv_ref[...] + dkvz_ref[...].astype(F32)
    restore(k_ref, dkv[: 2 * BLK] * FACTOR)
    restore(v_ref, dkv[2 * BLK :])


def z_step(step):
    return [(i, (i + step) % 8) for i in range(8)]


def y_step(step):
    return [(i, (i + step) % 4) for i in range(4)]


Z_PAIRS = [(i, (i - 2) % 8 if i % 2 == 0 else (i + 2) % 8) for i in range(8)]
Z_BACK = [(b, a) for a, b in Z_PAIRS]
X_SWAP = [(0, 1), (1, 0)]


def call(kernel, outs, operands, scratch=(), hbm=False, **options):
    space = pl.BlockSpec(memory_space=pltpu.HBM if hbm else pltpu.VMEM)
    return pl.pallas_call(
        kernel,
        out_shape=[jax.ShapeDtypeStruct(s, t) for s, t in outs],
        in_specs=[space] * len(operands),
        out_specs=[space] * len(outs),
        scratch_shapes=list(scratch),
        compiler_params=pltpu.CompilerParams(vmem_limit_bytes=PREP_VMEM if hbm else VMEM_LIMIT),
        **options,
    )(*operands)


def body(queries, key_rows, value_rows, outputs, out_grad, saved_lse, fold_map):
    operands = (fold_map, out_grad, outputs, saved_lse.T, key_rows, value_rows, queries)
    buffers = [(pltpu.SMEM if n == 0 else pltpu.VMEM)(a.shape, a.dtype) for n, a in enumerate(operands)]
    rows = pltpu.VMEM((ROWS - 4 * BLK, DIM), BF16)
    sems = [pltpu.SemaphoreType.DMA((7,)), pltpu.SemaphoreType.DMA((10,))]
    payload = ((ROWS, DIM), BF16)
    mine_q, mine_k = call(prep_kernel, [payload] * 2, operands, buffers + [rows] * 2 + sems, hbm=True)

    def beside(mine, other):
        both = lax.optimization_barrier(jnp.pad(mine[None], ((0, 1), (0, 0), (0, 0))))
        return lax.dynamic_update_slice(both, other[None], (1, 0, 0))

    other_k = lax.ppermute(mine_k, "kx", X_SWAP)
    q0 = beside(mine_q, lax.ppermute(mine_q, "kz", z_step(4)))
    _, other_k = lax.optimization_barrier((q0, other_k))
    k0 = jnp.stack([mine_k, other_k])
    q_sets = [q0] + [lax.ppermute(q, "kz", p) for q, p in ((q0, z_step(1)), (q0, z_step(-1)), (q0, Z_PAIRS))]
    k_sets = [k0] + [lax.ppermute(k0, "pb", y_step(-s)) for s in Y_FROM[1:]]
    q_pairs = ([q_sets[0], q_sets[3]], [q_sets[1], q_sets[2]])

    def grad(turn, js, pairs, dq_in, last, dkv_type, add=None, split=False):
        plan = tuple((d is None, e) for d, e in zip(dq_in, last))
        outs = []
        for pair, end in zip(pairs, last):
            if end:
                outs += [((2, 2 * BLK, DIM), F32 if (pair, s) == (0, 0) else BF16) for s in range(2)]
            else:
                outs.append(((2, DIM, 4 * BLK), F32))
        dkv_out = [((4 * BLK, DIM), BF16)] * len(js) if split else [((len(js), 4 * BLK, DIM), dkv_type)]
        acc = pltpu.VMEM((2 * len(js) * BLK, DIM), F32)
        results = call(
            functools.partial(grad_kernel, js, plan, turn == 0 and pairs[0] == 0, add is not None, split),
            outs + dkv_out,
            [q for p in pairs for q in q_pairs[p]] + [k_sets[turn]] + [d for d in (*dq_in, add) if d is not None],
            [acc, acc],
            cost_estimate=COST,
        )
        return results[: len(outs)], results[len(outs) :]

    def send_back(turn, part):
        return lax.ppermute(part, "pb", y_step(Y_FROM[turn]))

    both = (0, 1)
    (dq1,), (own1,) = grad(0, both, (1,), (None,), (False,), F32)
    (dq1,), (part,) = grad(1, both, (1,), (dq1,), (False,), F32)
    q_pairs[0][1], part = lax.optimization_barrier((q_pairs[0][1], part))
    (dq0,), (own0,) = grad(0, both, (0,), (None,), (False,), F32)
    (dq0,), (part,) = grad(1, both, (0,), (dq0,), (False,), BF16, add=part)
    back = [send_back(1, part)]
    (dq0, dq1), (part,) = grad(2, both, both, (dq0, dq1), (False, False), BF16)
    back.append(send_back(2, part))
    (dq_keep, *dqs), (part,) = grad(3, both, both, (dq0, dq1), (True, True), BF16)
    back.append(send_back(3, part))
    dqs[0], back[0] = lax.optimization_barrier((dqs[0], back[0]))
    own = (own0, own1)
    dq_back = [lax.ppermute(d, "kz", p) for d, p in zip(dqs, (Z_BACK, z_step(-1), z_step(1)))]

    def meet(operands, parts, shape):
        return call(functools.partial(meet_kernel, parts), [(shape, F32), (shape, BF16)], operands)

    dkv_keep, dkv_send = meet(
        [*own, *back], [both] * 5, (4 * BLK, DIM)
    )
    dkv_last = lax.ppermute(dkv_send, "kx", X_SWAP)
    dq_keep, dq_send = meet([dq_keep] + dq_back, [both] * 4, (2 * BLK, DIM))
    dq_last = lax.ppermute(dq_send, "kz", z_step(4))
    operands = (q0, dq_keep, dq_last, dkv_keep, dkv_last)
    return tuple(call(last_kernel, [((2 * BLK, DIM), BF16)] * 3, operands))


def solution(mesh):
    fine = Mesh(mesh.devices.reshape(4, 8, 2, 2, 2), ("pb", "kz", "kx", "hx", "hc"))
    rows = P(("pb", "kz", "kx"), ("hx", "hc"))
    return jax.shard_map(
        body,
        mesh=fine,
        in_specs=(rows,) * 6 + (P(),),
        out_specs=(rows,) * 3,
        check_vma=False,
    )
```

```python
import functools
import math

import jax
import jax.numpy as jnp
from jax import lax
from jax.experimental import pallas as pl
from jax.experimental.pallas import tpu as pltpu
from jax.sharding import Mesh, PartitionSpec as P

F32 = jnp.float32
BF16 = jnp.bfloat16
BLK = 128
DIM = 128
LOG2E = math.log2(math.e)
FACTOR = 1.0 / math.sqrt(DIM)
VMEM_LIMIT = 48 * 1024 * 1024
PREP_VMEM = 62 * 1024 * 1024
COST = pl.CostEstimate(flops=500000000, bytes_accessed=1000000, transcendentals=0)
HIDE = 1e30
Y_FROM = (0, 2, 3, 1)
NT = (((1,), (1,)), ((), ()))
ROWS = 4 * BLK + 16


def dot(a, b):
    return jnp.dot(a, b, preferred_element_type=F32)


def dot_nt(a, b):
    return lax.dot_general(a, b, NT, preferred_element_type=F32)


def prep_kernel(*refs):
    sources, (qout_ref, kout_ref), buffers, refs = refs[:7], refs[7:9], refs[9:16], refs[16:]
    qrows_buf, krows_buf, load_sems, store_sems = refs
    loads = [pltpu.make_async_copy(s, d, load_sems.at[n]) for n, (s, d) in enumerate(zip(sources, buffers))]
    for copy in loads:
        copy.start()
    stores = []

    def store(source, target):
        stores.append(pltpu.make_async_copy(source, target, store_sems.at[len(stores)]))
        stores[-1].start()

    def store_blocks(n, out_ref, at):
        loads[n].wait()
        store(buffers[n].at[pl.ds(low_at, BLK)], out_ref.at[at : at + BLK])
        store(buffers[n].at[pl.ds(high_at, BLK)], out_ref.at[at + BLK : at + 2 * BLK])

    fold_ref, g_buf, o_buf, lse_buf = buffers[:4]
    device = lax.axis_index("pb") * 16 + lax.axis_index("kz") * 2 + lax.axis_index("kx")
    loads[0].wait()
    first, second = fold_ref[2 * device], fold_ref[2 * device + 1]
    swapped = second < first
    low_at = pl.multiple_of(jnp.where(swapped, BLK, 0), BLK)
    high_at = pl.multiple_of(jnp.where(swapped, 0, BLK), BLK)
    low = jnp.minimum(first, second).astype(F32)
    krows_buf[...] = jnp.full(krows_buf.shape, low, F32).astype(BF16)
    store(krows_buf, kout_ref.at[4 * BLK :])
    store_blocks(1, qout_ref, 2 * BLK)
    loads[2].wait()
    loads[3].wait()
    lse = lse_buf[...].astype(F32)
    rows = [jnp.where(swapped, lse[:, BLK:], lse[:, :BLK]), jnp.where(swapped, lse[:, :BLK], lse[:, BLK:])]
    for at in (low_at, high_at):
        prod = g_buf[pl.ds(at, BLK), :].astype(F32) * o_buf[pl.ds(at, BLK), :].astype(F32)
        rows.append(jnp.sum(prod.T, axis=0, keepdims=True))
    rows.append(jnp.full((1, DIM), low, F32))
    rows.append(jnp.full((1, DIM), jnp.where(swapped, 1.0, 0.0), F32))
    qrows_buf[...] = jnp.concatenate(rows + [jnp.zeros((10, DIM), F32)], axis=0).astype(BF16)
    store(qrows_buf, qout_ref.at[4 * BLK :])
    store_blocks(6, qout_ref, 0)
    store_blocks(4, kout_ref, 0)
    store_blocks(5, kout_ref, 2 * BLK)
    for copy in stores:
        copy.wait()


def tile(k, v, kt, q, g, lses, delta, diagonal=None):
    s = dot_nt(k, q)
    probs = []
    for b, lse in enumerate(lses):
        p = jnp.exp2(s[b * BLK : (b + 1) * BLK] * (FACTOR * LOG2E) - lse)
        if b == diagonal:
            shape = (BLK, BLK)
            seen = lax.broadcasted_iota(jnp.int32, shape, 0) <= lax.broadcasted_iota(jnp.int32, shape, 1)
            p = jnp.concatenate([jnp.where(seen, p[:, :BLK], 0.0), p[:, BLK:]], 1)
        probs.append(p)
    p = jnp.concatenate(probs, 0)
    dp = dot_nt(v, g)
    ds = (p * (dp - delta)).astype(BF16)
    return dot(p.astype(BF16), g), dot(ds, q), dot(kt, ds)


def grad_kernel(js, group, own, first, add, last, *refs):
    refs = list(refs)

    def take(count):
        taken = refs[:count]
        del refs[:count]
        return taken

    q_refs, (y_ref,) = take(2), take(1)
    (dqin_ref,) = (None,) if first else take(1)
    (addin_ref,) = take(1) if add else (None,)
    (other_ref,) = take(1) if last else (None,)
    dq_refs, (dkv_ref, dv_acc, dk_acc) = take(4 if last else 1), refs
    count = len(js)
    half = count * BLK

    def keys(array):
        at = array * 2 * BLK
        return jnp.concatenate([y_ref[j, at + b * BLK : at + (b + 1) * BLK, :] for b in range(2) for j in js], 0)

    k, v = keys(0), keys(1)
    kt = k.T
    low_j = [jnp.concatenate([y_ref[j, 4 * BLK :, :].astype(F32)[0:1, :]] * 4, 1) for j in js]

    chunks = [(ref, c) for ref in q_refs for c in range(ref.shape[0])]

    def queries(array, b):
        at = (2 * array + b) * BLK
        return jnp.concatenate([ref[a, at : at + BLK, :] for ref, a in chunks], 0)

    tiles = [ref[a, 4 * BLK :, :].astype(F32) for ref, a in chunks]
    lse_low, lse_high, delta_low, delta_high, low_i = (
        jnp.concatenate([t[r : r + 1, :] for t in tiles], 1) for r in range(5)
    )
    lse_low, lse_high = lse_low * LOG2E, lse_high * LOG2E
    diagonal = own

    lses = [lse_high] * count + [lse_high + jnp.where(low_i <= low, 0.0, HIDE) for low in low_j]
    dv, dk, dq_high = tile(
        k, v, kt, queries(0, 1), queries(1, 1), lses, delta_high, count if diagonal else None
    )
    dv_acc[...] = dv
    dk_acc[...] = dk
    lses = [lse_low + jnp.where(low <= low_i, 0.0, HIDE) for low in low_j]
    dv, dk, dq_low = tile(
        k[:half], v[:half], kt[:, :half], queries(0, 0), queries(1, 0), lses, delta_low, 0 if diagonal else None
    )
    dv_acc[:half] += dv
    dk_acc[:half] += dk
    for b, dq in ((0, dq_low), (1, dq_high)):
        if not first:
            dq = dqin_ref[b] + dq
        if not last:
            dq_refs[0][b] = dq
        else:
            for a, part in ((group, dq), (1 - group, other_ref[b])):
                for s, ref in enumerate(dq_refs):
                    ref[a, b * BLK : (b + 1) * BLK, :] = part[:, s * BLK : (s + 1) * BLK].T.astype(ref.dtype)

    for m in range(count):
        for b in range(2):
            source = slice(b * half + m * BLK, b * half + (m + 1) * BLK)
            for array, acc in ((0, dk_acc), (1, dv_acc)):
                rows = slice((2 * array + b) * BLK, (2 * array + b + 1) * BLK)
                part = acc[source]
                if add:
                    part = addin_ref[m, rows, :] + part
                dkv_ref[m, rows, :] = part.astype(dkv_ref.dtype)


def meet_kernel(parts, *refs):
    out_refs = refs[-2:]
    for half, out_ref in enumerate(out_refs):
        total = None
        for ref, index in zip(refs, parts):
            if index[half] is not None:
                part = ref[index[half]].astype(F32)
                total = part if total is None else total + part
        out_ref[...] = total.astype(out_ref.dtype)


def last_kernel(rows_ref, dq_ref, dqx_ref, dkv_ref, dkvz_ref, q_ref, k_ref, v_ref):
    swapped = rows_ref[0, 4 * BLK :, :].astype(F32)[5:6, :] > 0.5

    def restore(out_ref, total):
        low, high = total[:BLK], total[BLK:]
        out_ref[:BLK, :] = jnp.where(swapped, high, low).astype(BF16)
        out_ref[BLK:, :] = jnp.where(swapped, low, high).astype(BF16)

    restore(q_ref, (dq_ref[...] + dqx_ref[...].astype(F32)) * FACTOR)
    dkv = dkv_ref[...] + dkvz_ref[...].astype(F32)
    restore(k_ref, dkv[: 2 * BLK] * FACTOR)
    restore(v_ref, dkv[2 * BLK :])


def z_step(step):
    return [(i, (i + step) % 8) for i in range(8)]


def y_step(step):
    return [(i, (i + step) % 4) for i in range(4)]


Z_PAIRS = [(i, (i - 2) % 8 if i % 2 == 0 else (i + 2) % 8) for i in range(8)]
Z_BACK = [(b, a) for a, b in Z_PAIRS]
X_SWAP = [(0, 1), (1, 0)]


def call(kernel, outs, operands, scratch=(), hbm=False, **options):
    space = pl.BlockSpec(memory_space=pltpu.HBM if hbm else pltpu.VMEM)
    return pl.pallas_call(
        kernel,
        out_shape=[jax.ShapeDtypeStruct(s, t) for s, t in outs],
        in_specs=[space] * len(operands),
        out_specs=[space] * len(outs),
        scratch_shapes=list(scratch),
        compiler_params=pltpu.CompilerParams(vmem_limit_bytes=PREP_VMEM if hbm else VMEM_LIMIT),
        **options,
    )(*operands)


def body(queries, key_rows, value_rows, outputs, out_grad, saved_lse, fold_map):
    operands = (fold_map, out_grad, outputs, saved_lse.T, key_rows, value_rows, queries)
    buffers = [(pltpu.SMEM if n == 0 else pltpu.VMEM)(a.shape, a.dtype) for n, a in enumerate(operands)]
    rows = pltpu.VMEM((ROWS - 4 * BLK, DIM), BF16)
    sems = [pltpu.SemaphoreType.DMA((7,)), pltpu.SemaphoreType.DMA((10,))]
    payload = ((ROWS, DIM), BF16)
    mine_q, mine_k = call(prep_kernel, [payload] * 2, operands, buffers + [rows] * 2 + sems, hbm=True)

    def gather(arrays):
        out = jnp.pad(arrays[0][None], ((0, len(arrays) - 1), (0, 0), (0, 0)))
        out = lax.optimization_barrier(out)
        for n, array in enumerate(arrays[1:]):
            out = lax.dynamic_update_slice(out, array[None], (n + 1, 0, 0))
        return out

    other_k = lax.ppermute(mine_k, "kz", z_step(4))
    near = [lax.ppermute(mine_q, "kz", p) for p in (z_step(1), z_step(-1), Z_PAIRS)]
    near = jnp.stack(near)
    q_groups = [
        (mine_q[None], near),
        (lax.ppermute(mine_q, "kx", X_SWAP)[None], lax.ppermute(near, "kx", X_SWAP)),
    ]
    k0 = gather([mine_k, other_k])
    k_sets = [k0] + [lax.ppermute(k0, "pb", y_step(-s)) for s in Y_FROM[1:]]

    def grad(turn, group, dq_in, add, dkv_type, other=None):
        last = other is not None
        outs = [((2, DIM, 4 * BLK), F32)]
        if last:
            outs = [((2, 2 * BLK, DIM), BF16 if s else F32) for s in range(4)]
        acc = pltpu.VMEM((4 * BLK, DIM), F32)
        own = turn == 0 and group == 0
        *dq, part = call(
            functools.partial(grad_kernel, (0, 1), group, own, dq_in is None, add is not None, last),
            outs + [((2, 4 * BLK, DIM), dkv_type)],
            [*q_groups[group], k_sets[turn]] + [d for d in (dq_in, add, other) if d is not None],
            [acc, acc],
            cost_estimate=COST,
        )
        return (dq if last else dq[0]), part

    def send_back(turn, part):
        return lax.ppermute(part, "pb", y_step(Y_FROM[turn]))

    both = (0, 1)
    parts = []
    dq0 = dq1 = None
    for turn in range(4):
        dq0, part = grad(turn, 0, dq0, None, F32)
        parts.append(part)
    q_groups[1], parts[1] = lax.optimization_barrier((q_groups[1], parts[1]))
    back = []
    for turn in (1, 2, 3):
        dq1, part = grad(turn, 1, dq1, parts[turn], BF16)
        back.append(send_back(turn, part))
    dq1, back[0] = lax.optimization_barrier((dq1, back[0]))
    (dq_keep, *dqs), own = grad(0, 1, dq1, parts[0], F32, other=dq0)
    dq_back = [lax.ppermute(d, "kz", p) for d, p in zip(dqs, (z_step(-1), z_step(1), Z_BACK))]

    def meet(operands, parts, shape):
        return call(functools.partial(meet_kernel, parts), [(shape, F32), (shape, BF16)], operands)

    dkv_keep, dkv_send = meet([own, *back], [both] * 4, (4 * BLK, DIM))
    dkv_last = lax.ppermute(dkv_send, "kz", z_step(4))
    dq_keep, dq_send = meet([dq_keep] + dq_back, [both] * 4, (2 * BLK, DIM))
    dq_last = lax.ppermute(dq_send, "kx", X_SWAP)
    operands = (mine_q[None], dq_keep, dq_last, dkv_keep, dkv_last)
    return tuple(call(last_kernel, [((2 * BLK, DIM), BF16)] * 3, operands))


def solution(mesh):
    fine = Mesh(mesh.devices.reshape(4, 8, 2, 2, 2), ("pb", "kz", "kx", "hx", "hc"))
    rows = P(("pb", "kz", "kx"), ("hx", "hc"))
    return jax.shard_map(
        body,
        mesh=fine,
        in_specs=(rows,) * 6 + (P(),),
        out_specs=(rows,) * 3,
        check_vma=False,
    )
```

```python
import functools
import math

import jax
import jax.numpy as jnp
from jax import lax
from jax.experimental import pallas as pl
from jax.experimental.pallas import tpu as pltpu
from jax.sharding import Mesh, PartitionSpec as P

F32 = jnp.float32
BF16 = jnp.bfloat16
BLK = 128
DIM = 128
LOG2E = math.log2(math.e)
FACTOR = 1.0 / math.sqrt(DIM)
VMEM_LIMIT = 48 * 1024 * 1024
PREP_VMEM = 62 * 1024 * 1024
COST = pl.CostEstimate(flops=500000000, bytes_accessed=1000000, transcendentals=0)
HIDE = 1e30
Y_FROM = (0, 2, 3, 1)
NT = (((1,), (1,)), ((), ()))
ROWS = 4 * BLK + 16


def dot(a, b):
    return jnp.dot(a, b, preferred_element_type=F32)


def dot_nt(a, b):
    return lax.dot_general(a, b, NT, preferred_element_type=F32)


def prep_kernel(*refs):
    sources, (qout_ref, kout_ref), buffers, refs = refs[:7], refs[7:9], refs[9:16], refs[16:]
    qrows_buf, krows_buf, load_sems, store_sems = refs
    loads = [pltpu.make_async_copy(s, d, load_sems.at[n]) for n, (s, d) in enumerate(zip(sources, buffers))]
    for copy in loads:
        copy.start()
    stores = []

    def store(source, target):
        stores.append(pltpu.make_async_copy(source, target, store_sems.at[len(stores)]))
        stores[-1].start()

    def store_blocks(n, out_ref, at):
        loads[n].wait()
        store(buffers[n].at[pl.ds(low_at, BLK)], out_ref.at[at : at + BLK])
        store(buffers[n].at[pl.ds(high_at, BLK)], out_ref.at[at + BLK : at + 2 * BLK])

    fold_ref, g_buf, o_buf, lse_buf = buffers[:4]
    device = lax.axis_index("pb") * 16 + lax.axis_index("kz") * 2 + lax.axis_index("kx")
    loads[0].wait()
    first, second = fold_ref[2 * device], fold_ref[2 * device + 1]
    swapped = second < first
    low_at = pl.multiple_of(jnp.where(swapped, BLK, 0), BLK)
    high_at = pl.multiple_of(jnp.where(swapped, 0, BLK), BLK)
    low = jnp.minimum(first, second).astype(F32)
    krows_buf[...] = jnp.full(krows_buf.shape, low, F32).astype(BF16)
    store(krows_buf, kout_ref.at[4 * BLK :])
    store_blocks(1, qout_ref, 2 * BLK)
    loads[2].wait()
    loads[3].wait()
    lse = lse_buf[...].astype(F32)
    rows = [jnp.where(swapped, lse[:, BLK:], lse[:, :BLK]), jnp.where(swapped, lse[:, :BLK], lse[:, BLK:])]
    for at in (low_at, high_at):
        prod = g_buf[pl.ds(at, BLK), :].astype(F32) * o_buf[pl.ds(at, BLK), :].astype(F32)
        rows.append(jnp.sum(prod.T, axis=0, keepdims=True))
    rows.append(jnp.full((1, DIM), low, F32))
    rows.append(jnp.full((1, DIM), jnp.where(swapped, 1.0, 0.0), F32))
    qrows_buf[...] = jnp.concatenate(rows + [jnp.zeros((10, DIM), F32)], axis=0).astype(BF16)
    store(qrows_buf, qout_ref.at[4 * BLK :])
    store_blocks(6, qout_ref, 0)
    store_blocks(4, kout_ref, 0)
    store_blocks(5, kout_ref, 2 * BLK)
    for copy in stores:
        copy.wait()


def tile(k, v, kt, q, g, lses, delta, diagonal=None):
    s = dot_nt(k, q)
    probs = []
    for b, lse in enumerate(lses):
        p = jnp.exp2(s[b * BLK : (b + 1) * BLK] * (FACTOR * LOG2E) - lse)
        if b == diagonal:
            shape = (BLK, BLK)
            seen = lax.broadcasted_iota(jnp.int32, shape, 0) <= lax.broadcasted_iota(jnp.int32, shape, 1)
            p = jnp.concatenate([jnp.where(seen, p[:, :BLK], 0.0), p[:, BLK:]], 1)
        probs.append(p)
    p = jnp.concatenate(probs, 0)
    dp = dot_nt(v, g)
    ds = (p * (dp - delta)).astype(BF16)
    return dot(p.astype(BF16), g), dot(ds, q), dot(kt, ds)


def grad_kernel(js, plan, own, add, split, *refs):
    refs = list(refs)

    def take(count):
        taken = refs[:count]
        del refs[:count]
        return taken

    q_refs, (y_ref,) = take(2 * len(plan)), take(1)
    dqin_refs = [None if first else take(1)[0] for first, _ in plan]
    addin_ref = refs.pop(0) if add else None
    dq_refs = [take(2 if last else 1) for _, last in plan]
    dkv_refs = take(len(js)) if split else [refs.pop(0)]
    dv_acc, dk_acc = refs
    count = len(js)
    half = count * BLK

    def keys(array):
        at = array * 2 * BLK
        return jnp.concatenate([y_ref[j, at + b * BLK : at + (b + 1) * BLK, :] for b in range(2) for j in js], 0)

    k, v = keys(0), keys(1)
    kt = k.T
    low_j = [jnp.concatenate([y_ref[j, 4 * BLK :, :].astype(F32)[0:1, :]] * 4, 1) for j in js]

    for n, (first, last) in enumerate(plan):
        pair = q_refs[2 * n : 2 * n + 2]
        chunks = [(ref, a) for ref in pair for a in range(2)]

        def queries(array, b):
            at = (2 * array + b) * BLK
            return jnp.concatenate([ref[a, at : at + BLK, :] for ref, a in chunks], 0)

        tiles = [ref[a, 4 * BLK :, :].astype(F32) for ref, a in chunks]
        lse_low, lse_high, delta_low, delta_high, low_i = (
            jnp.concatenate([t[r : r + 1, :] for t in tiles], 1) for r in range(5)
        )
        lse_low, lse_high = lse_low * LOG2E, lse_high * LOG2E
        diagonal = own and n == 0

        lses = [lse_high] * count + [lse_high + jnp.where(low_i <= low, 0.0, HIDE) for low in low_j]
        dv, dk, dq_high = tile(
            k, v, kt, queries(0, 1), queries(1, 1), lses, delta_high, count if diagonal else None
        )
        dv_acc[...] = dv if n == 0 else dv_acc[...] + dv
        dk_acc[...] = dk if n == 0 else dk_acc[...] + dk
        lses = [lse_low + jnp.where(low <= low_i, 0.0, HIDE) for low in low_j]
        dv, dk, dq_low = tile(
            k[:half], v[:half], kt[:, :half], queries(0, 0), queries(1, 0), lses, delta_low, 0 if diagonal else None
        )
        dv_acc[:half] += dv
        dk_acc[:half] += dk
        for b, dq in ((0, dq_low), (1, dq_high)):
            if not first:
                dq = dqin_refs[n][b] + dq
            if not last:
                dq_refs[n][0][b] = dq
            else:
                for c in range(4):
                    ref = dq_refs[n][c // 2]
                    ref[c % 2, b * BLK : (b + 1) * BLK, :] = dq[:, c * BLK : (c + 1) * BLK].T.astype(ref.dtype)

    for m in range(count):
        for b in range(2):
            source = slice(b * half + m * BLK, b * half + (m + 1) * BLK)
            for array, acc in ((0, dk_acc), (1, dv_acc)):
                rows = slice((2 * array + b) * BLK, (2 * array + b + 1) * BLK)
                part = acc[source]
                if add:
                    part = addin_ref[m, rows, :] + part
                if split:
                    dkv_refs[m][rows, :] = part.astype(BF16)
                else:
                    dkv_refs[0][m, rows, :] = part.astype(dkv_refs[0].dtype)


def meet_kernel(parts, *refs):
    out_refs = refs[-2:]
    for half, out_ref in enumerate(out_refs):
        total = None
        for ref, index in zip(refs, parts):
            if index[half] is not None:
                part = ref[index[half]].astype(F32)
                total = part if total is None else total + part
        out_ref[...] = total.astype(out_ref.dtype)


def last_kernel(rows_ref, dq_ref, dqx_ref, dkv_ref, dkvz_ref, q_ref, k_ref, v_ref):
    swapped = rows_ref[0, 4 * BLK :, :].astype(F32)[5:6, :] > 0.5

    def restore(out_ref, total):
        low, high = total[:BLK], total[BLK:]
        out_ref[:BLK, :] = jnp.where(swapped, high, low).astype(BF16)
        out_ref[BLK:, :] = jnp.where(swapped, low, high).astype(BF16)

    restore(q_ref, (dq_ref[...] + dqx_ref[...].astype(F32)) * FACTOR)
    dkv = dkv_ref[...] + dkvz_ref[...].astype(F32)
    restore(k_ref, dkv[: 2 * BLK] * FACTOR)
    restore(v_ref, dkv[2 * BLK :])


def z_step(step):
    return [(i, (i + step) % 8) for i in range(8)]


def y_step(step):
    return [(i, (i + step) % 4) for i in range(4)]


Z_PAIRS = [(i, (i - 2) % 8 if i % 2 == 0 else (i + 2) % 8) for i in range(8)]
Z_BACK = [(b, a) for a, b in Z_PAIRS]
X_SWAP = [(0, 1), (1, 0)]


def call(kernel, outs, operands, scratch=(), hbm=False, **options):
    space = pl.BlockSpec(memory_space=pltpu.HBM if hbm else pltpu.VMEM)
    return pl.pallas_call(
        kernel,
        out_shape=[jax.ShapeDtypeStruct(s, t) for s, t in outs],
        in_specs=[space] * len(operands),
        out_specs=[space] * len(outs),
        scratch_shapes=list(scratch),
        compiler_params=pltpu.CompilerParams(vmem_limit_bytes=PREP_VMEM if hbm else VMEM_LIMIT),
        **options,
    )(*operands)


def body(queries, key_rows, value_rows, outputs, out_grad, saved_lse, fold_map):
    operands = (fold_map, out_grad, outputs, saved_lse.T, key_rows, value_rows, queries)
    buffers = [(pltpu.SMEM if n == 0 else pltpu.VMEM)(a.shape, a.dtype) for n, a in enumerate(operands)]
    rows = pltpu.VMEM((ROWS - 4 * BLK, DIM), BF16)
    sems = [pltpu.SemaphoreType.DMA((7,)), pltpu.SemaphoreType.DMA((10,))]
    payload = ((ROWS, DIM), BF16)
    mine_q, mine_k = call(prep_kernel, [payload] * 2, operands, buffers + [rows] * 2 + sems, hbm=True)

    def beside(mine, other):
        both = lax.optimization_barrier(jnp.pad(mine[None], ((0, 1), (0, 0), (0, 0))))
        return lax.dynamic_update_slice(both, other[None], (1, 0, 0))

    other_k = lax.ppermute(mine_k, "kz", z_step(4))
    q0 = beside(mine_q, lax.ppermute(mine_q, "kx", X_SWAP))
    _, other_k = lax.optimization_barrier((q0, other_k))
    k0 = jnp.stack([mine_k, other_k])
    q_sets = [q0] + [lax.ppermute(q, "kz", p) for q, p in ((q0, z_step(1)), (q0, z_step(-1)), (q0, Z_PAIRS))]
    k_sets = [k0] + [lax.ppermute(k0, "pb", y_step(-s)) for s in Y_FROM[1:]]
    q_pairs = ([q_sets[0], q_sets[3]], [q_sets[1], q_sets[2]])

    def grad(turn, js, pairs, dq_in, last, dkv_type, add=None, split=False):
        plan = tuple((d is None, e) for d, e in zip(dq_in, last))
        outs = []
        for pair, end in zip(pairs, last):
            if end:
                outs += [((2, 2 * BLK, DIM), F32 if (pair, s) == (0, 0) else BF16) for s in range(2)]
            else:
                outs.append(((2, DIM, 4 * BLK), F32))
        dkv_out = [((4 * BLK, DIM), BF16)] * len(js) if split else [((len(js), 4 * BLK, DIM), dkv_type)]
        acc = pltpu.VMEM((2 * len(js) * BLK, DIM), F32)
        results = call(
            functools.partial(grad_kernel, js, plan, turn == 0 and pairs[0] == 0, add is not None, split),
            outs + dkv_out,
            [q for p in pairs for q in q_pairs[p]] + [k_sets[turn]] + [d for d in (*dq_in, add) if d is not None],
            [acc, acc],
            cost_estimate=COST,
        )
        return results[: len(outs)], results[len(outs) :]

    def send_back(turn, part):
        return lax.ppermute(part, "pb", y_step(Y_FROM[turn]))

    both = (0, 1)
    (dq1,), (own1,) = grad(0, both, (1,), (None,), (False,), F32)
    k_sets[0], own1 = lax.optimization_barrier((k_sets[0], own1))
    (dq0,), (own0,) = grad(0, both, (0,), (None,), (False,), F32)
    (dq0, dq1), (part,) = grad(1, both, both, (dq0, dq1), (False, False), BF16)
    back = [send_back(1, part)]
    (dq0, dq1), (part,) = grad(2, both, both, (dq0, dq1), (False, False), BF16)
    back.append(send_back(2, part))
    (dq_keep, *dqs), (part,) = grad(3, both, both, (dq0, dq1), (True, True), BF16)
    back.append(send_back(3, part))
    dqs[0], back[0] = lax.optimization_barrier((dqs[0], back[0]))
    own = (own0, own1)
    dq_back = [lax.ppermute(d, "kz", p) for d, p in zip(dqs, (Z_BACK, z_step(-1), z_step(1)))]

    def meet(operands, parts, shape):
        return call(functools.partial(meet_kernel, parts), [(shape, F32), (shape, BF16)], operands)

    dkv_keep, dkv_send = meet(
        [*own, *back], [both] * 5, (4 * BLK, DIM)
    )
    dkv_last = lax.ppermute(dkv_send, "kz", z_step(4))
    dq_keep, dq_send = meet([dq_keep] + dq_back, [both] * 4, (2 * BLK, DIM))
    dq_last = lax.ppermute(dq_send, "kx", X_SWAP)
    operands = (q0, dq_keep, dq_last, dkv_keep, dkv_last)
    return tuple(call(last_kernel, [((2 * BLK, DIM), BF16)] * 3, operands))


def solution(mesh):
    fine = Mesh(mesh.devices.reshape(4, 8, 2, 2, 2), ("pb", "kz", "kx", "hx", "hc"))
    rows = P(("pb", "kz", "kx"), ("hx", "hc"))
    return jax.shard_map(
        body,
        mesh=fine,
        in_specs=(rows,) * 6 + (P(),),
        out_specs=(rows,) * 3,
        check_vma=False,
    )
```

```python
import functools
import math

import jax
import jax.numpy as jnp
from jax import lax
from jax.experimental import pallas as pl
from jax.experimental.pallas import tpu as pltpu
from jax.sharding import Mesh, PartitionSpec as P

F32 = jnp.float32
BF16 = jnp.bfloat16
BLK = 128
DIM = 128
LOG2E = math.log2(math.e)
FACTOR = 1.0 / math.sqrt(DIM)
VMEM_LIMIT = 48 * 1024 * 1024
PREP_VMEM = 62 * 1024 * 1024
COST = pl.CostEstimate(flops=500000000, bytes_accessed=1000000, transcendentals=0)
HIDE = 1e30
Y_FROM = (0, 2, 3, 1)
NT = (((1,), (1,)), ((), ()))
ROWS = 4 * BLK + 16


def dot(a, b):
    return jnp.dot(a, b, preferred_element_type=F32)


def dot_nt(a, b):
    return lax.dot_general(a, b, NT, preferred_element_type=F32)


def prep_kernel(*refs):
    sources, (qout_ref, kout_ref), buffers, refs = refs[:7], refs[7:9], refs[9:16], refs[16:]
    qrows_buf, krows_buf, load_sems, store_sems = refs
    loads = [pltpu.make_async_copy(s, d, load_sems.at[n]) for n, (s, d) in enumerate(zip(sources, buffers))]
    for copy in loads:
        copy.start()
    stores = []

    def store(source, target):
        stores.append(pltpu.make_async_copy(source, target, store_sems.at[len(stores)]))
        stores[-1].start()

    def store_blocks(n, out_ref, at):
        loads[n].wait()
        store(buffers[n].at[pl.ds(low_at, BLK)], out_ref.at[at : at + BLK])
        store(buffers[n].at[pl.ds(high_at, BLK)], out_ref.at[at + BLK : at + 2 * BLK])

    fold_ref, g_buf, o_buf, lse_buf = buffers[:4]
    device = lax.axis_index("pb") * 16 + lax.axis_index("kz") * 2 + lax.axis_index("kx")
    loads[0].wait()
    first, second = fold_ref[2 * device], fold_ref[2 * device + 1]
    swapped = second < first
    low_at = pl.multiple_of(jnp.where(swapped, BLK, 0), BLK)
    high_at = pl.multiple_of(jnp.where(swapped, 0, BLK), BLK)
    low = jnp.minimum(first, second).astype(F32)
    krows_buf[...] = jnp.full(krows_buf.shape, low, F32).astype(BF16)
    store(krows_buf, kout_ref.at[4 * BLK :])
    store_blocks(1, qout_ref, 2 * BLK)
    loads[2].wait()
    loads[3].wait()
    lse = lse_buf[...].astype(F32)
    rows = [jnp.where(swapped, lse[:, BLK:], lse[:, :BLK]), jnp.where(swapped, lse[:, :BLK], lse[:, BLK:])]
    for at in (low_at, high_at):
        prod = g_buf[pl.ds(at, BLK), :].astype(F32) * o_buf[pl.ds(at, BLK), :].astype(F32)
        rows.append(jnp.sum(prod.T, axis=0, keepdims=True))
    rows.append(jnp.full((1, DIM), low, F32))
    rows.append(jnp.full((1, DIM), jnp.where(swapped, 1.0, 0.0), F32))
    qrows_buf[...] = jnp.concatenate(rows + [jnp.zeros((10, DIM), F32)], axis=0).astype(BF16)
    store(qrows_buf, qout_ref.at[4 * BLK :])
    store_blocks(6, qout_ref, 0)
    store_blocks(4, kout_ref, 0)
    store_blocks(5, kout_ref, 2 * BLK)
    for copy in stores:
        copy.wait()


def tile(k, v, kt, q, g, lses, delta, diagonal=None):
    s = dot_nt(k, q)
    probs = []
    for b, lse in enumerate(lses):
        p = jnp.exp2(s[b * BLK : (b + 1) * BLK] * (FACTOR * LOG2E) - lse)
        if b == diagonal:
            shape = (BLK, BLK)
            seen = lax.broadcasted_iota(jnp.int32, shape, 0) <= lax.broadcasted_iota(jnp.int32, shape, 1)
            p = jnp.concatenate([jnp.where(seen, p[:, :BLK], 0.0), p[:, BLK:]], 1)
        probs.append(p)
    p = jnp.concatenate(probs, 0)
    dp = dot_nt(v, g)
    ds = (p * (dp - delta)).astype(BF16)
    return dot(p.astype(BF16), g), dot(ds, q), dot(kt, ds)


def grad_kernel(js, groups, plan, own, add, *refs):
    refs = list(refs)

    def take(count):
        taken = refs[:count]
        del refs[:count]
        return taken

    q_refs, (y_ref,) = [take(size) for size in groups], take(1)
    dqin_refs = [None if first else take(1)[0] for first, _ in plan]
    addin_ref = refs.pop(0) if add else None
    dq_refs = [take(size if last else 1) for size, (_, last) in zip(groups, plan)]
    dkv_ref, dv_acc, dk_acc = refs
    count = len(js)
    half = count * BLK

    def keys(array):
        at = array * 2 * BLK
        return jnp.concatenate([y_ref[j, at + b * BLK : at + (b + 1) * BLK, :] for b in range(2) for j in js], 0)

    k, v = keys(0), keys(1)
    kt = k.T
    low_j = [y_ref[j, 4 * BLK :, :].astype(F32)[0:1, :] for j in js]

    for n, (first, last) in enumerate(plan):
        chunks = [(ref, a) for ref in q_refs[n] for a in range(2)]
        lows = [jnp.concatenate([low] * len(chunks), 1) for low in low_j]

        def queries(array, b):
            at = (2 * array + b) * BLK
            return jnp.concatenate([ref[a, at : at + BLK, :] for ref, a in chunks], 0)

        tiles = [ref[a, 4 * BLK :, :].astype(F32) for ref, a in chunks]
        lse_low, lse_high, delta_low, delta_high, low_i = (
            jnp.concatenate([t[r : r + 1, :] for t in tiles], 1) for r in range(5)
        )
        lse_low, lse_high = lse_low * LOG2E, lse_high * LOG2E
        diagonal = own and n == 0

        lses = [lse_high] * count + [lse_high + jnp.where(low_i <= low, 0.0, HIDE) for low in lows]
        dv, dk, dq_high = tile(
            k, v, kt, queries(0, 1), queries(1, 1), lses, delta_high, count if diagonal else None
        )
        dv_acc[...] = dv if n == 0 else dv_acc[...] + dv
        dk_acc[...] = dk if n == 0 else dk_acc[...] + dk
        lses = [lse_low + jnp.where(low <= low_i, 0.0, HIDE) for low in lows]
        dv, dk, dq_low = tile(
            k[:half], v[:half], kt[:, :half], queries(0, 0), queries(1, 0), lses, delta_low, 0 if diagonal else None
        )
        dv_acc[:half] += dv
        dk_acc[:half] += dk
        for b, dq in ((0, dq_low), (1, dq_high)):
            if not first:
                dq = dqin_refs[n][b] + dq
            if not last:
                dq_refs[n][0][b] = dq
            else:
                for c in range(len(chunks)):
                    ref = dq_refs[n][c // 2]
                    ref[c % 2, b * BLK : (b + 1) * BLK, :] = dq[:, c * BLK : (c + 1) * BLK].T.astype(ref.dtype)

    for m in range(count):
        for b in range(2):
            source = slice(b * half + m * BLK, b * half + (m + 1) * BLK)
            for array, acc in ((0, dk_acc), (1, dv_acc)):
                rows = slice((2 * array + b) * BLK, (2 * array + b + 1) * BLK)
                part = acc[source]
                if add:
                    part = addin_ref[m, rows, :] + part
                dkv_ref[m, rows, :] = part.astype(dkv_ref.dtype)


def meet_kernel(parts, *refs):
    out_refs = refs[-2:]
    for half, out_ref in enumerate(out_refs):
        total = None
        for ref, index in zip(refs, parts):
            if index[half] is not None:
                part = ref[index[half]].astype(F32)
                total = part if total is None else total + part
        out_ref[...] = total.astype(out_ref.dtype)


def last_kernel(rows_ref, dq_ref, dqx_ref, dkv_ref, dkvz_ref, q_ref, k_ref, v_ref):
    swapped = rows_ref[0, 4 * BLK :, :].astype(F32)[5:6, :] > 0.5

    def restore(out_ref, total):
        low, high = total[:BLK], total[BLK:]
        out_ref[:BLK, :] = jnp.where(swapped, high, low).astype(BF16)
        out_ref[BLK:, :] = jnp.where(swapped, low, high).astype(BF16)

    restore(q_ref, (dq_ref[...] + dqx_ref[...].astype(F32)) * FACTOR)
    dkv = dkv_ref[...] + dkvz_ref[...].astype(F32)
    restore(k_ref, dkv[: 2 * BLK] * FACTOR)
    restore(v_ref, dkv[2 * BLK :])


def z_step(step):
    return [(i, (i + step) % 8) for i in range(8)]


def y_step(step):
    return [(i, (i + step) % 4) for i in range(4)]


Z_PAIRS = [(i, (i - 2) % 8 if i % 2 == 0 else (i + 2) % 8) for i in range(8)]
Z_BACK = [(b, a) for a, b in Z_PAIRS]
X_SWAP = [(0, 1), (1, 0)]


def call(kernel, outs, operands, scratch=(), hbm=False, **options):
    space = pl.BlockSpec(memory_space=pltpu.HBM if hbm else pltpu.VMEM)
    return pl.pallas_call(
        kernel,
        out_shape=[jax.ShapeDtypeStruct(s, t) for s, t in outs],
        in_specs=[space] * len(operands),
        out_specs=[space] * len(outs),
        scratch_shapes=list(scratch),
        compiler_params=pltpu.CompilerParams(vmem_limit_bytes=PREP_VMEM if hbm else VMEM_LIMIT),
        **options,
    )(*operands)


def body(queries, key_rows, value_rows, outputs, out_grad, saved_lse, fold_map):
    operands = (fold_map, out_grad, outputs, saved_lse.T, key_rows, value_rows, queries)
    buffers = [(pltpu.SMEM if n == 0 else pltpu.VMEM)(a.shape, a.dtype) for n, a in enumerate(operands)]
    rows = pltpu.VMEM((ROWS - 4 * BLK, DIM), BF16)
    sems = [pltpu.SemaphoreType.DMA((7,)), pltpu.SemaphoreType.DMA((10,))]
    payload = ((ROWS, DIM), BF16)
    mine_q, mine_k = call(prep_kernel, [payload] * 2, operands, buffers + [rows] * 2 + sems, hbm=True)

    def beside(mine, other):
        both = lax.optimization_barrier(jnp.pad(mine[None], ((0, 1), (0, 0), (0, 0))))
        return lax.dynamic_update_slice(both, other[None], (1, 0, 0))

    other_k = lax.ppermute(mine_k, "kz", z_step(4))
    q0 = beside(mine_q, lax.ppermute(mine_q, "kx", X_SWAP))
    late_q, other_k = lax.optimization_barrier((q0, other_k))
    k0 = jnp.stack([mine_k, other_k])
    q_sets = [q0] + [lax.ppermute(q, "kz", p) for q, p in ((q0, z_step(1)), (q0, z_step(-1)), (late_q, Z_PAIRS))]
    k_sets = [k0] + [lax.ppermute(k0, "pb", y_step(-s)) for s in Y_FROM[1:]]
    q_groups = [q_sets[:3], q_sets[3:]]

    def grad(turn, group, dq_in, add, last, dkv_type):
        sets = q_groups[group]
        outs = [((2, DIM, 2 * len(sets) * BLK), F32)]
        if last:
            outs = [((2, 2 * BLK, DIM), F32 if (group, s) == (0, 0) else BF16) for s in range(len(sets))]
        acc = pltpu.VMEM((4 * BLK, DIM), F32)
        plan = ((dq_in is None, last),)
        *dq, part = call(
            functools.partial(grad_kernel, (0, 1), (len(sets),), plan, turn == 0 and group == 0, add is not None),
            outs + [((2, 4 * BLK, DIM), dkv_type)],
            [*sets, k_sets[turn]] + [d for d in (dq_in, add) if d is not None],
            [acc, acc],
            cost_estimate=COST,
        )
        return (dq if last else dq[0]), part

    def send_back(turn, part):
        return lax.ppermute(part, "pb", y_step(Y_FROM[turn]))

    both = (0, 1)
    parts = []
    dq = None
    for turn in range(4):
        dq, part = grad(turn, 0, dq, None, turn == 3, F32)
        parts.append(part)
    dq_keep, *dqs = dq
    dq_back = [lax.ppermute(d, "kz", p) for d, p in zip(dqs, (z_step(-1), z_step(1)))]
    q_groups[1][0], parts[3] = lax.optimization_barrier((q_groups[1][0], parts[3]))
    back = []
    dq = None
    for turn in (1, 2, 3):
        dq, part = grad(turn, 1, dq, parts[turn], False, BF16)
        back.append(send_back(turn, part))
    dq, back[0] = lax.optimization_barrier((dq, back[0]))
    (dq_z2,), own = grad(0, 1, dq, parts[0], True, F32)
    dq_back.append(lax.ppermute(dq_z2, "kz", Z_BACK))

    def meet(operands, parts, shape):
        return call(functools.partial(meet_kernel, parts), [(shape, F32), (shape, BF16)], operands)

    dkv_keep, dkv_send = meet(
        [own] + back, [both] * 4, (4 * BLK, DIM)
    )
    dkv_last = lax.ppermute(dkv_send, "kz", z_step(4))
    dq_keep, dq_send = meet([dq_keep] + dq_back, [both] * 4, (2 * BLK, DIM))
    dq_last = lax.ppermute(dq_send, "kx", X_SWAP)
    operands = (q0, dq_keep, dq_last, dkv_keep, dkv_last)
    return tuple(call(last_kernel, [((2 * BLK, DIM), BF16)] * 3, operands))


def solution(mesh):
    fine = Mesh(mesh.devices.reshape(4, 8, 2, 2, 2), ("pb", "kz", "kx", "hx", "hc"))
    rows = P(("pb", "kz", "kx"), ("hx", "hc"))
    return jax.shard_map(
        body,
        mesh=fine,
        in_specs=(rows,) * 6 + (P(),),
        out_specs=(rows,) * 3,
        check_vma=False,
    )
```

```python
import functools
import math

import jax
import jax.numpy as jnp
from jax import lax
from jax.experimental import pallas as pl
from jax.experimental.pallas import tpu as pltpu
from jax.sharding import Mesh, PartitionSpec as P

F32 = jnp.float32
BF16 = jnp.bfloat16
BLK = 128
DIM = 128
LOG2E = math.log2(math.e)
FACTOR = 1.0 / math.sqrt(DIM)
VMEM_LIMIT = 48 * 1024 * 1024
PREP_VMEM = 62 * 1024 * 1024
COST = pl.CostEstimate(flops=500000000, bytes_accessed=1000000, transcendentals=0)
HIDE = 1e30
Y_FROM = (0, 2, 3, 1)
NT = (((1,), (1,)), ((), ()))
ROWS = 4 * BLK + 16


def dot(a, b):
    return jnp.dot(a, b, preferred_element_type=F32)


def dot_nt(a, b):
    return lax.dot_general(a, b, NT, preferred_element_type=F32)


def prep_kernel(*refs):
    sources, (qout_ref, kout_ref), buffers, refs = refs[:7], refs[7:9], refs[9:16], refs[16:]
    qrows_buf, krows_buf, load_sems, store_sems = refs
    loads = [pltpu.make_async_copy(s, d, load_sems.at[n]) for n, (s, d) in enumerate(zip(sources, buffers))]
    for copy in loads:
        copy.start()
    stores = []

    def store(source, target):
        stores.append(pltpu.make_async_copy(source, target, store_sems.at[len(stores)]))
        stores[-1].start()

    def store_blocks(n, out_ref, at):
        loads[n].wait()
        store(buffers[n].at[pl.ds(low_at, BLK)], out_ref.at[at : at + BLK])
        store(buffers[n].at[pl.ds(high_at, BLK)], out_ref.at[at + BLK : at + 2 * BLK])

    fold_ref, g_buf, o_buf, lse_buf = buffers[:4]
    device = lax.axis_index("pb") * 16 + lax.axis_index("kz") * 2 + lax.axis_index("kx")
    loads[0].wait()
    first, second = fold_ref[2 * device], fold_ref[2 * device + 1]
    swapped = second < first
    low_at = pl.multiple_of(jnp.where(swapped, BLK, 0), BLK)
    high_at = pl.multiple_of(jnp.where(swapped, 0, BLK), BLK)
    low = jnp.minimum(first, second).astype(F32)
    krows_buf[...] = jnp.full(krows_buf.shape, low, F32).astype(BF16)
    store(krows_buf, kout_ref.at[4 * BLK :])
    store_blocks(1, qout_ref, 2 * BLK)
    loads[2].wait()
    loads[3].wait()
    lse = lse_buf[...].astype(F32)
    rows = [jnp.where(swapped, lse[:, BLK:], lse[:, :BLK]), jnp.where(swapped, lse[:, :BLK], lse[:, BLK:])]
    for at in (low_at, high_at):
        prod = g_buf[pl.ds(at, BLK), :].astype(F32) * o_buf[pl.ds(at, BLK), :].astype(F32)
        rows.append(jnp.sum(prod.T, axis=0, keepdims=True))
    rows.append(jnp.full((1, DIM), low, F32))
    rows.append(jnp.full((1, DIM), jnp.where(swapped, 1.0, 0.0), F32))
    qrows_buf[...] = jnp.concatenate(rows + [jnp.zeros((10, DIM), F32)], axis=0).astype(BF16)
    store(qrows_buf, qout_ref.at[4 * BLK :])
    store_blocks(6, qout_ref, 0)
    store_blocks(4, kout_ref, 0)
    store_blocks(5, kout_ref, 2 * BLK)
    for copy in stores:
        copy.wait()


def tile(k, v, kt, q, g, lses, delta, diagonal=None):
    s = dot_nt(k, q)
    probs = []
    for b, lse in enumerate(lses):
        p = jnp.exp2(s[b * BLK : (b + 1) * BLK] * (FACTOR * LOG2E) - lse)
        if b == diagonal:
            shape = (BLK, BLK)
            seen = lax.broadcasted_iota(jnp.int32, shape, 0) <= lax.broadcasted_iota(jnp.int32, shape, 1)
            p = jnp.concatenate([jnp.where(seen, p[:, :BLK], 0.0), p[:, BLK:]], 1)
        probs.append(p)
    p = jnp.concatenate(probs, 0)
    dp = dot_nt(v, g)
    ds = (p * (dp - delta)).astype(BF16)
    return dot(p.astype(BF16), g), dot(ds, q), dot(kt, ds)


def grad_kernel(js, groups, plan, own, add, *refs):
    refs = list(refs)

    def take(count):
        taken = refs[:count]
        del refs[:count]
        return taken

    q_refs, (y_ref,) = [take(size) for size in groups], take(1)
    dqin_refs = [None if first else take(1)[0] for first, _ in plan]
    addin_ref = refs.pop(0) if add else None
    dq_refs = [take(size if last else 1) for size, (_, last) in zip(groups, plan)]
    dkv_ref, dv_acc, dk_acc = refs
    count = len(js)
    half = count * BLK

    def keys(array):
        at = array * 2 * BLK
        return jnp.concatenate([y_ref[j, at + b * BLK : at + (b + 1) * BLK, :] for b in range(2) for j in js], 0)

    k, v = keys(0), keys(1)
    kt = k.T
    low_j = [y_ref[j, 4 * BLK :, :].astype(F32)[0:1, :] for j in js]

    for n, (first, last) in enumerate(plan):
        chunks = [(ref, a) for ref in q_refs[n] for a in range(2)]
        lows = [jnp.concatenate([low] * len(chunks), 1) for low in low_j]

        def queries(array, b):
            at = (2 * array + b) * BLK
            return jnp.concatenate([ref[a, at : at + BLK, :] for ref, a in chunks], 0)

        tiles = [ref[a, 4 * BLK :, :].astype(F32) for ref, a in chunks]
        lse_low, lse_high, delta_low, delta_high, low_i = (
            jnp.concatenate([t[r : r + 1, :] for t in tiles], 1) for r in range(5)
        )
        lse_low, lse_high = lse_low * LOG2E, lse_high * LOG2E
        diagonal = own and n == 0

        lses = [lse_high] * count + [lse_high + jnp.where(low_i <= low, 0.0, HIDE) for low in lows]
        dv, dk, dq_high = tile(
            k, v, kt, queries(0, 1), queries(1, 1), lses, delta_high, count if diagonal else None
        )
        dv_acc[...] = dv if n == 0 else dv_acc[...] + dv
        dk_acc[...] = dk if n == 0 else dk_acc[...] + dk
        lses = [lse_low + jnp.where(low <= low_i, 0.0, HIDE) for low in lows]
        dv, dk, dq_low = tile(
            k[:half], v[:half], kt[:, :half], queries(0, 0), queries(1, 0), lses, delta_low, 0 if diagonal else None
        )
        dv_acc[:half] += dv
        dk_acc[:half] += dk
        for b, dq in ((0, dq_low), (1, dq_high)):
            if not first:
                dq = dqin_refs[n][b] + dq
            if not last:
                dq_refs[n][0][b] = dq
            else:
                for c in range(len(chunks)):
                    ref = dq_refs[n][c // 2]
                    ref[c % 2, b * BLK : (b + 1) * BLK, :] = dq[:, c * BLK : (c + 1) * BLK].T.astype(ref.dtype)

    for m in range(count):
        for b in range(2):
            source = slice(b * half + m * BLK, b * half + (m + 1) * BLK)
            for array, acc in ((0, dk_acc), (1, dv_acc)):
                rows = slice((2 * array + b) * BLK, (2 * array + b + 1) * BLK)
                part = acc[source]
                if add:
                    part = addin_ref[m, rows, :] + part
                dkv_ref[m, rows, :] = part.astype(dkv_ref.dtype)


def meet_kernel(parts, *refs):
    out_refs = refs[-2:]
    for half, out_ref in enumerate(out_refs):
        total = None
        for ref, index in zip(refs, parts):
            if index[half] is not None:
                part = ref[index[half]].astype(F32)
                total = part if total is None else total + part
        out_ref[...] = total.astype(out_ref.dtype)


def last_kernel(rows_ref, dq_ref, dqx_ref, dkv_ref, dkvz_ref, q_ref, k_ref, v_ref):
    swapped = rows_ref[0, 4 * BLK :, :].astype(F32)[5:6, :] > 0.5

    def restore(out_ref, total):
        low, high = total[:BLK], total[BLK:]
        out_ref[:BLK, :] = jnp.where(swapped, high, low).astype(BF16)
        out_ref[BLK:, :] = jnp.where(swapped, low, high).astype(BF16)

    restore(q_ref, (dq_ref[...] + dqx_ref[...].astype(F32)) * FACTOR)
    dkv = dkv_ref[...] + dkvz_ref[...].astype(F32)
    restore(k_ref, dkv[: 2 * BLK] * FACTOR)
    restore(v_ref, dkv[2 * BLK :])


def z_step(step):
    return [(i, (i + step) % 8) for i in range(8)]


def y_step(step):
    return [(i, (i + step) % 4) for i in range(4)]


Z_PAIRS = [(i, (i - 2) % 8 if i % 2 == 0 else (i + 2) % 8) for i in range(8)]
Z_BACK = [(b, a) for a, b in Z_PAIRS]
X_SWAP = [(0, 1), (1, 0)]


def call(kernel, outs, operands, scratch=(), hbm=False, **options):
    space = pl.BlockSpec(memory_space=pltpu.HBM if hbm else pltpu.VMEM)
    return pl.pallas_call(
        kernel,
        out_shape=[jax.ShapeDtypeStruct(s, t) for s, t in outs],
        in_specs=[space] * len(operands),
        out_specs=[space] * len(outs),
        scratch_shapes=list(scratch),
        compiler_params=pltpu.CompilerParams(vmem_limit_bytes=PREP_VMEM if hbm else VMEM_LIMIT),
        **options,
    )(*operands)


def body(queries, key_rows, value_rows, outputs, out_grad, saved_lse, fold_map):
    operands = (fold_map, out_grad, outputs, saved_lse.T, key_rows, value_rows, queries)
    buffers = [(pltpu.SMEM if n == 0 else pltpu.VMEM)(a.shape, a.dtype) for n, a in enumerate(operands)]
    rows = pltpu.VMEM((ROWS - 4 * BLK, DIM), BF16)
    sems = [pltpu.SemaphoreType.DMA((7,)), pltpu.SemaphoreType.DMA((10,))]
    payload = ((ROWS, DIM), BF16)
    mine_q, mine_k = call(prep_kernel, [payload] * 2, operands, buffers + [rows] * 2 + sems, hbm=True)

    def beside(mine, other):
        both = lax.optimization_barrier(jnp.pad(mine[None], ((0, 1), (0, 0), (0, 0))))
        return lax.dynamic_update_slice(both, other[None], (1, 0, 0))

    other_k = lax.ppermute(mine_k, "kz", z_step(4))
    q0 = beside(mine_q, lax.ppermute(mine_q, "kx", X_SWAP))
    late_q, other_k = lax.optimization_barrier((q0, other_k))
    k0 = jnp.stack([mine_k, other_k])
    q_sets = [q0] + [lax.ppermute(q, "kz", p) for q, p in ((q0, z_step(1)), (q0, Z_PAIRS), (late_q, z_step(-1)))]
    k_sets = [k0] + [lax.ppermute(k0, "pb", y_step(-s)) for s in Y_FROM[1:]]
    q_groups = [q_sets[:3], q_sets[3:]]

    def grad(turn, group, dq_in, add, last, dkv_type):
        sets = q_groups[group]
        outs = [((2, DIM, 2 * len(sets) * BLK), F32)]
        if last:
            outs = [((2, 2 * BLK, DIM), F32 if (group, s) == (0, 0) else BF16) for s in range(len(sets))]
        acc = pltpu.VMEM((4 * BLK, DIM), F32)
        plan = ((dq_in is None, last),)
        *dq, part = call(
            functools.partial(grad_kernel, (0, 1), (len(sets),), plan, turn == 0 and group == 0, add is not None),
            outs + [((2, 4 * BLK, DIM), dkv_type)],
            [*sets, k_sets[turn]] + [d for d in (dq_in, add) if d is not None],
            [acc, acc],
            cost_estimate=COST,
        )
        return (dq if last else dq[0]), part

    def send_back(turn, part):
        return lax.ppermute(part, "pb", y_step(Y_FROM[turn]))

    both = (0, 1)
    parts = []
    dq = None
    for turn in range(4):
        dq, part = grad(turn, 0, dq, None, turn == 3, F32)
        parts.append(part)
    dq_keep, *dqs = dq
    dq_back = [lax.ppermute(d, "kz", p) for d, p in zip(dqs, (z_step(-1), Z_BACK))]
    q_groups[1][0], parts[3] = lax.optimization_barrier((q_groups[1][0], parts[3]))
    back = []
    dq = None
    for turn in (1, 2, 3):
        dq, part = grad(turn, 1, dq, parts[turn], False, BF16)
        back.append(send_back(turn, part))
    dq, back[0] = lax.optimization_barrier((dq, back[0]))
    (dq_late,), own = grad(0, 1, dq, parts[0], True, F32)
    dq_back.append(lax.ppermute(dq_late, "kz", z_step(1)))

    def meet(operands, parts, shape):
        return call(functools.partial(meet_kernel, parts), [(shape, F32), (shape, BF16)], operands)

    dkv_keep, dkv_send = meet(
        [own] + back, [both] * 4, (4 * BLK, DIM)
    )
    dkv_last = lax.ppermute(dkv_send, "kz", z_step(4))
    dq_keep, dq_send = meet([dq_keep] + dq_back, [both] * 4, (2 * BLK, DIM))
    dq_last = lax.ppermute(dq_send, "kx", X_SWAP)
    operands = (q0, dq_keep, dq_last, dkv_keep, dkv_last)
    return tuple(call(last_kernel, [((2 * BLK, DIM), BF16)] * 3, operands))


def solution(mesh):
    fine = Mesh(mesh.devices.reshape(4, 8, 2, 2, 2), ("pb", "kz", "kx", "hx", "hc"))
    rows = P(("pb", "kz", "kx"), ("hx", "hc"))
    return jax.shard_map(
        body,
        mesh=fine,
        in_specs=(rows,) * 6 + (P(),),
        out_specs=(rows,) * 3,
        check_vma=False,
    )
```

```python
import functools
import math

import jax
import jax.numpy as jnp
from jax import lax
from jax.experimental import pallas as pl
from jax.experimental.pallas import tpu as pltpu
from jax.sharding import Mesh, PartitionSpec as P

F32 = jnp.float32
BF16 = jnp.bfloat16
BLK = 128
DIM = 128
LOG2E = math.log2(math.e)
FACTOR = 1.0 / math.sqrt(DIM)
VMEM_LIMIT = 48 * 1024 * 1024
PREP_VMEM = 62 * 1024 * 1024
COST = pl.CostEstimate(flops=500000000, bytes_accessed=1000000, transcendentals=0)
HIDE = 1e30
Y_FROM = (0, 2, 3, 1)
NT = (((1,), (1,)), ((), ()))
ROWS = 4 * BLK + 16


def dot(a, b):
    return jnp.dot(a, b, preferred_element_type=F32)


def dot_nt(a, b):
    return lax.dot_general(a, b, NT, preferred_element_type=F32)


def prep_kernel(*refs):
    sources, (qout_ref, kout_ref), buffers, refs = refs[:7], refs[7:9], refs[9:16], refs[16:]
    qrows_buf, krows_buf, load_sems, store_sems = refs
    loads = [pltpu.make_async_copy(s, d, load_sems.at[n]) for n, (s, d) in enumerate(zip(sources, buffers))]
    for copy in loads:
        copy.start()
    stores = []

    def store(source, target):
        stores.append(pltpu.make_async_copy(source, target, store_sems.at[len(stores)]))
        stores[-1].start()

    def store_blocks(n, out_ref, at):
        loads[n].wait()
        store(buffers[n].at[pl.ds(low_at, BLK)], out_ref.at[at : at + BLK])
        store(buffers[n].at[pl.ds(high_at, BLK)], out_ref.at[at + BLK : at + 2 * BLK])

    fold_ref, g_buf, o_buf, lse_buf = buffers[:4]
    device = lax.axis_index("pb") * 16 + lax.axis_index("kz") * 2 + lax.axis_index("kx")
    loads[0].wait()
    first, second = fold_ref[2 * device], fold_ref[2 * device + 1]
    swapped = second < first
    low_at = pl.multiple_of(jnp.where(swapped, BLK, 0), BLK)
    high_at = pl.multiple_of(jnp.where(swapped, 0, BLK), BLK)
    low = jnp.minimum(first, second).astype(F32)
    krows_buf[...] = jnp.full(krows_buf.shape, low, F32).astype(BF16)
    store(krows_buf, kout_ref.at[4 * BLK :])
    store_blocks(1, qout_ref, 2 * BLK)
    loads[2].wait()
    loads[3].wait()
    lse = lse_buf[...].astype(F32)
    rows = [jnp.where(swapped, lse[:, BLK:], lse[:, :BLK]), jnp.where(swapped, lse[:, :BLK], lse[:, BLK:])]
    for at in (low_at, high_at):
        prod = g_buf[pl.ds(at, BLK), :].astype(F32) * o_buf[pl.ds(at, BLK), :].astype(F32)
        rows.append(jnp.sum(prod.T, axis=0, keepdims=True))
    rows.append(jnp.full((1, DIM), low, F32))
    rows.append(jnp.full((1, DIM), jnp.where(swapped, 1.0, 0.0), F32))
    qrows_buf[...] = jnp.concatenate(rows + [jnp.zeros((10, DIM), F32)], axis=0).astype(BF16)
    store(qrows_buf, qout_ref.at[4 * BLK :])
    store_blocks(6, qout_ref, 0)
    store_blocks(4, kout_ref, 0)
    store_blocks(5, kout_ref, 2 * BLK)
    for copy in stores:
        copy.wait()


def tile(k, v, kt, q, g, lses, delta, diagonal=None):
    s = dot_nt(k, q)
    probs = []
    for b, lse in enumerate(lses):
        p = jnp.exp2(s[b * BLK : (b + 1) * BLK] * (FACTOR * LOG2E) - lse)
        if b == diagonal:
            shape = (BLK, BLK)
            seen = lax.broadcasted_iota(jnp.int32, shape, 0) <= lax.broadcasted_iota(jnp.int32, shape, 1)
            p = jnp.concatenate([jnp.where(seen, p[:, :BLK], 0.0), p[:, BLK:]], 1)
        probs.append(p)
    p = jnp.concatenate(probs, 0)
    dp = dot_nt(v, g)
    ds = (p * (dp - delta)).astype(BF16)
    return dot(p.astype(BF16), g), dot(ds, q), dot(kt, ds)


def grad_kernel(js, groups, plan, own, add, *refs):
    refs = list(refs)

    def take(count):
        taken = refs[:count]
        del refs[:count]
        return taken

    q_refs, (y_ref,) = [take(size) for size in groups], take(1)
    dqin_refs = [None if first else take(1)[0] for first, _ in plan]
    addin_ref = refs.pop(0) if add else None
    dq_refs = [take(size if last else 1) for size, (_, last) in zip(groups, plan)]
    dkv_ref, dv_acc, dk_acc = refs
    count = len(js)
    half = count * BLK

    def keys(array):
        at = array * 2 * BLK
        return jnp.concatenate([y_ref[j, at + b * BLK : at + (b + 1) * BLK, :] for b in range(2) for j in js], 0)

    k, v = keys(0), keys(1)
    kt = k.T
    low_j = [y_ref[j, 4 * BLK :, :].astype(F32)[0:1, :] for j in js]

    for n, (first, last) in enumerate(plan):
        chunks = [(ref, a) for ref in q_refs[n] for a in range(2)]
        lows = [jnp.concatenate([low] * len(chunks), 1) for low in low_j]

        def queries(array, b):
            at = (2 * array + b) * BLK
            return jnp.concatenate([ref[a, at : at + BLK, :] for ref, a in chunks], 0)

        tiles = [ref[a, 4 * BLK :, :].astype(F32) for ref, a in chunks]
        lse_low, lse_high, delta_low, delta_high, low_i = (
            jnp.concatenate([t[r : r + 1, :] for t in tiles], 1) for r in range(5)
        )
        lse_low, lse_high = lse_low * LOG2E, lse_high * LOG2E
        diagonal = own and n == 0

        lses = [lse_high] * count + [lse_high + jnp.where(low_i <= low, 0.0, HIDE) for low in lows]
        dv, dk, dq_high = tile(
            k, v, kt, queries(0, 1), queries(1, 1), lses, delta_high, count if diagonal else None
        )
        dv_acc[...] = dv if n == 0 else dv_acc[...] + dv
        dk_acc[...] = dk if n == 0 else dk_acc[...] + dk
        lses = [lse_low + jnp.where(low <= low_i, 0.0, HIDE) for low in lows]
        dv, dk, dq_low = tile(
            k[:half], v[:half], kt[:, :half], queries(0, 0), queries(1, 0), lses, delta_low, 0 if diagonal else None
        )
        dv_acc[:half] += dv
        dk_acc[:half] += dk
        for b, dq in ((0, dq_low), (1, dq_high)):
            if not first:
                dq = dqin_refs[n][b] + dq
            if not last:
                dq_refs[n][0][b] = dq
            else:
                for c in range(len(chunks)):
                    ref = dq_refs[n][c // 2]
                    ref[c % 2, b * BLK : (b + 1) * BLK, :] = dq[:, c * BLK : (c + 1) * BLK].T.astype(ref.dtype)

    for m in range(count):
        for b in range(2):
            source = slice(b * half + m * BLK, b * half + (m + 1) * BLK)
            for array, acc in ((0, dk_acc), (1, dv_acc)):
                rows = slice((2 * array + b) * BLK, (2 * array + b + 1) * BLK)
                part = acc[source]
                if add:
                    part = addin_ref[m, rows, :] + part
                dkv_ref[m, rows, :] = part.astype(dkv_ref.dtype)


def meet_kernel(parts, *refs):
    out_refs = refs[-2:]
    for half, out_ref in enumerate(out_refs):
        total = None
        for ref, index in zip(refs, parts):
            if index[half] is not None:
                part = ref[index[half]].astype(F32)
                total = part if total is None else total + part
        out_ref[...] = total.astype(out_ref.dtype)


def last_kernel(rows_ref, dq_ref, dqx_ref, dkv_ref, dkvz_ref, q_ref, k_ref, v_ref):
    swapped = rows_ref[0, 4 * BLK :, :].astype(F32)[5:6, :] > 0.5

    def restore(out_ref, total):
        low, high = total[:BLK], total[BLK:]
        out_ref[:BLK, :] = jnp.where(swapped, high, low).astype(BF16)
        out_ref[BLK:, :] = jnp.where(swapped, low, high).astype(BF16)

    restore(q_ref, (dq_ref[...] + dqx_ref[...].astype(F32)) * FACTOR)
    dkv = dkv_ref[...] + dkvz_ref[...].astype(F32)
    restore(k_ref, dkv[: 2 * BLK] * FACTOR)
    restore(v_ref, dkv[2 * BLK :])


def z_step(step):
    return [(i, (i + step) % 8) for i in range(8)]


def y_step(step):
    return [(i, (i + step) % 4) for i in range(4)]


Z_PAIRS = [(i, (i - 2) % 8 if i % 2 == 0 else (i + 2) % 8) for i in range(8)]
Z_BACK = [(b, a) for a, b in Z_PAIRS]
X_SWAP = [(0, 1), (1, 0)]


def call(kernel, outs, operands, scratch=(), hbm=False, **options):
    space = pl.BlockSpec(memory_space=pltpu.HBM if hbm else pltpu.VMEM)
    return pl.pallas_call(
        kernel,
        out_shape=[jax.ShapeDtypeStruct(s, t) for s, t in outs],
        in_specs=[space] * len(operands),
        out_specs=[space] * len(outs),
        scratch_shapes=list(scratch),
        compiler_params=pltpu.CompilerParams(vmem_limit_bytes=PREP_VMEM if hbm else VMEM_LIMIT),
        **options,
    )(*operands)


def body(queries, key_rows, value_rows, outputs, out_grad, saved_lse, fold_map):
    operands = (fold_map, out_grad, outputs, saved_lse.T, key_rows, value_rows, queries)
    buffers = [(pltpu.SMEM if n == 0 else pltpu.VMEM)(a.shape, a.dtype) for n, a in enumerate(operands)]
    rows = pltpu.VMEM((ROWS - 4 * BLK, DIM), BF16)
    sems = [pltpu.SemaphoreType.DMA((7,)), pltpu.SemaphoreType.DMA((10,))]
    payload = ((ROWS, DIM), BF16)
    mine_q, mine_k = call(prep_kernel, [payload] * 2, operands, buffers + [rows] * 2 + sems, hbm=True)

    def beside(mine, other):
        both = lax.optimization_barrier(jnp.pad(mine[None], ((0, 1), (0, 0), (0, 0))))
        return lax.dynamic_update_slice(both, other[None], (1, 0, 0))

    other_k = lax.ppermute(mine_k, "kz", z_step(4))
    q0 = beside(mine_q, lax.ppermute(mine_q, "kx", X_SWAP))
    late_q, other_k = lax.optimization_barrier((q0, other_k))
    k0 = jnp.stack([mine_k, other_k])
    q_sets = [q0] + [lax.ppermute(q, "kz", p) for q, p in ((q0, z_step(1)), (q0, z_step(-1)), (late_q, Z_PAIRS))]
    k_sets = [k0] + [lax.ppermute(k0, "pb", y_step(-s)) for s in Y_FROM[1:]]
    q_groups = [q_sets[:3], q_sets[3:]]

    def grad(turn, group, dq_in, add, last, dkv_type):
        sets = q_groups[group]
        outs = [((2, DIM, 2 * len(sets) * BLK), F32)]
        if last:
            outs = [((2, 2 * BLK, DIM), F32 if (group, s) == (0, 0) else BF16) for s in range(len(sets))]
        acc = pltpu.VMEM((4 * BLK, DIM), F32)
        plan = ((dq_in is None, last),)
        *dq, part = call(
            functools.partial(grad_kernel, (0, 1), (len(sets),), plan, turn == 0 and group == 0, add is not None),
            outs + [((2, 4 * BLK, DIM), dkv_type)],
            [*sets, k_sets[turn]] + [d for d in (dq_in, add) if d is not None],
            [acc, acc],
            cost_estimate=COST,
        )
        return (dq if last else dq[0]), part

    def send_back(turn, part):
        return lax.ppermute(part, "pb", y_step(Y_FROM[turn]))

    both = (0, 1)
    parts = []
    dq = None
    for turn in range(4):
        dq, part = grad(turn, 0, dq, None, turn == 3, F32)
        parts.append(part)
    dq_keep, *dqs = dq
    dq_back = [lax.ppermute(d, "kz", p) for d, p in zip(dqs, (z_step(-1), z_step(1)))]
    q_groups[1][0], parts[3] = lax.optimization_barrier((q_groups[1][0], parts[3]))
    back = []
    dq = None
    for turn in (1, 2, 3):
        dq, part = grad(turn, 1, dq, parts[turn], False, BF16)
        back.append(send_back(turn, part))
    (dq_z2,), own = grad(0, 1, dq, parts[0], True, F32)
    dq_z2, back[0] = lax.optimization_barrier((dq_z2, back[0]))
    dq_back.append(lax.ppermute(dq_z2, "kz", Z_BACK))

    def meet(operands, parts, shape):
        return call(functools.partial(meet_kernel, parts), [(shape, F32), (shape, BF16)], operands)

    dkv_keep, dkv_send = meet(
        [own] + back, [both] * 4, (4 * BLK, DIM)
    )
    dkv_last = lax.ppermute(dkv_send, "kz", z_step(4))
    dq_keep, dq_send = meet([dq_keep] + dq_back, [both] * 4, (2 * BLK, DIM))
    dq_last = lax.ppermute(dq_send, "kx", X_SWAP)
    operands = (q0, dq_keep, dq_last, dkv_keep, dkv_last)
    return tuple(call(last_kernel, [((2 * BLK, DIM), BF16)] * 3, operands))


def solution(mesh):
    fine = Mesh(mesh.devices.reshape(4, 8, 2, 2, 2), ("pb", "kz", "kx", "hx", "hc"))
    rows = P(("pb", "kz", "kx"), ("hx", "hc"))
    return jax.shard_map(
        body,
        mesh=fine,
        in_specs=(rows,) * 6 + (P(),),
        out_specs=(rows,) * 3,
        check_vma=False,
    )
```

```python
import functools
import math

import jax
import jax.numpy as jnp
from jax import lax
from jax.experimental import pallas as pl
from jax.experimental.pallas import tpu as pltpu
from jax.sharding import Mesh, PartitionSpec as P

F32 = jnp.float32
BF16 = jnp.bfloat16
BLK = 128
DIM = 128
LOG2E = math.log2(math.e)
FACTOR = 1.0 / math.sqrt(DIM)
VMEM_LIMIT = 48 * 1024 * 1024
PREP_VMEM = 62 * 1024 * 1024
COST = pl.CostEstimate(flops=500000000, bytes_accessed=1000000, transcendentals=0)
HIDE = 1e30
Y_FROM = (0, 2, 3, 1)
NT = (((1,), (1,)), ((), ()))
ROWS = 4 * BLK + 16


def dot(a, b):
    return jnp.dot(a, b, preferred_element_type=F32)


def dot_nt(a, b):
    return lax.dot_general(a, b, NT, preferred_element_type=F32)


def prep_kernel(*refs):
    sources, (qout_ref, kout_ref), buffers, refs = refs[:7], refs[7:9], refs[9:16], refs[16:]
    qrows_buf, krows_buf, load_sems, store_sems = refs
    loads = [pltpu.make_async_copy(s, d, load_sems.at[n]) for n, (s, d) in enumerate(zip(sources, buffers))]
    for copy in loads:
        copy.start()
    stores = []

    def store(source, target):
        stores.append(pltpu.make_async_copy(source, target, store_sems.at[len(stores)]))
        stores[-1].start()

    def store_blocks(n, out_ref, at):
        loads[n].wait()
        store(buffers[n].at[pl.ds(low_at, BLK)], out_ref.at[at : at + BLK])
        store(buffers[n].at[pl.ds(high_at, BLK)], out_ref.at[at + BLK : at + 2 * BLK])

    fold_ref, g_buf, o_buf, lse_buf = buffers[:4]
    device = lax.axis_index("pb") * 16 + lax.axis_index("kz") * 2 + lax.axis_index("kx")
    loads[0].wait()
    first, second = fold_ref[2 * device], fold_ref[2 * device + 1]
    swapped = second < first
    low_at = pl.multiple_of(jnp.where(swapped, BLK, 0), BLK)
    high_at = pl.multiple_of(jnp.where(swapped, 0, BLK), BLK)
    low = jnp.minimum(first, second).astype(F32)
    krows_buf[...] = jnp.full(krows_buf.shape, low, F32).astype(BF16)
    store(krows_buf, kout_ref.at[4 * BLK :])
    store_blocks(1, qout_ref, 2 * BLK)
    store_blocks(6, qout_ref, 0)
    store_blocks(4, kout_ref, 0)
    store_blocks(5, kout_ref, 2 * BLK)
    loads[2].wait()
    loads[3].wait()
    lse = lse_buf[...].astype(F32)
    rows = [jnp.where(swapped, lse[:, BLK:], lse[:, :BLK]), jnp.where(swapped, lse[:, :BLK], lse[:, BLK:])]
    for at in (low_at, high_at):
        prod = g_buf[pl.ds(at, BLK), :].astype(F32) * o_buf[pl.ds(at, BLK), :].astype(F32)
        rows.append(jnp.sum(prod.T, axis=0, keepdims=True))
    rows.append(jnp.full((1, DIM), low, F32))
    rows.append(jnp.full((1, DIM), jnp.where(swapped, 1.0, 0.0), F32))
    qrows_buf[...] = jnp.concatenate(rows + [jnp.zeros((10, DIM), F32)], axis=0).astype(BF16)
    store(qrows_buf, qout_ref.at[4 * BLK :])
    for copy in stores:
        copy.wait()


def tile(k, v, kt, q, g, lses, delta, diagonal=None):
    s = dot_nt(k, q)
    probs = []
    for b, lse in enumerate(lses):
        p = jnp.exp2(s[b * BLK : (b + 1) * BLK] * (FACTOR * LOG2E) - lse)
        if b == diagonal:
            shape = (BLK, BLK)
            seen = lax.broadcasted_iota(jnp.int32, shape, 0) <= lax.broadcasted_iota(jnp.int32, shape, 1)
            p = jnp.concatenate([jnp.where(seen, p[:, :BLK], 0.0), p[:, BLK:]], 1)
        probs.append(p)
    p = jnp.concatenate(probs, 0)
    dp = dot_nt(v, g)
    ds = (p * (dp - delta)).astype(BF16)
    return dot(p.astype(BF16), g), dot(ds, q), dot(kt, ds)


def grad_kernel(js, groups, plan, own, add, *refs):
    refs = list(refs)

    def take(count):
        taken = refs[:count]
        del refs[:count]
        return taken

    q_refs, (y_ref,) = [take(size) for size in groups], take(1)
    dqin_refs = [None if first else take(1)[0] for first, _ in plan]
    addin_ref = refs.pop(0) if add else None
    dq_refs = [take(size if last else 1) for size, (_, last) in zip(groups, plan)]
    dkv_ref, dv_acc, dk_acc = refs
    count = len(js)
    half = count * BLK

    def keys(array):
        at = array * 2 * BLK
        return jnp.concatenate([y_ref[j, at + b * BLK : at + (b + 1) * BLK, :] for b in range(2) for j in js], 0)

    k, v = keys(0), keys(1)
    kt = k.T
    low_j = [y_ref[j, 4 * BLK :, :].astype(F32)[0:1, :] for j in js]

    for n, (first, last) in enumerate(plan):
        chunks = [(ref, a) for ref in q_refs[n] for a in range(2)]
        lows = [jnp.concatenate([low] * len(chunks), 1) for low in low_j]

        def queries(array, b):
            at = (2 * array + b) * BLK
            return jnp.concatenate([ref[a, at : at + BLK, :] for ref, a in chunks], 0)

        tiles = [ref[a, 4 * BLK :, :].astype(F32) for ref, a in chunks]
        lse_low, lse_high, delta_low, delta_high, low_i = (
            jnp.concatenate([t[r : r + 1, :] for t in tiles], 1) for r in range(5)
        )
        lse_low, lse_high = lse_low * LOG2E, lse_high * LOG2E
        diagonal = own and n == 0

        lses = [lse_high] * count + [lse_high + jnp.where(low_i <= low, 0.0, HIDE) for low in lows]
        dv, dk, dq_high = tile(
            k, v, kt, queries(0, 1), queries(1, 1), lses, delta_high, count if diagonal else None
        )
        dv_acc[...] = dv if n == 0 else dv_acc[...] + dv
        dk_acc[...] = dk if n == 0 else dk_acc[...] + dk
        lses = [lse_low + jnp.where(low <= low_i, 0.0, HIDE) for low in lows]
        dv, dk, dq_low = tile(
            k[:half], v[:half], kt[:, :half], queries(0, 0), queries(1, 0), lses, delta_low, 0 if diagonal else None
        )
        dv_acc[:half] += dv
        dk_acc[:half] += dk
        for b, dq in ((0, dq_low), (1, dq_high)):
            if not first:
                dq = dqin_refs[n][b] + dq
            if not last:
                dq_refs[n][0][b] = dq
            else:
                for c in range(len(chunks)):
                    ref = dq_refs[n][c // 2]
                    ref[c % 2, b * BLK : (b + 1) * BLK, :] = dq[:, c * BLK : (c + 1) * BLK].T.astype(ref.dtype)

    for m in range(count):
        for b in range(2):
            source = slice(b * half + m * BLK, b * half + (m + 1) * BLK)
            for array, acc in ((0, dk_acc), (1, dv_acc)):
                rows = slice((2 * array + b) * BLK, (2 * array + b + 1) * BLK)
                part = acc[source]
                if add:
                    part = addin_ref[m, rows, :] + part
                dkv_ref[m, rows, :] = part.astype(dkv_ref.dtype)


def meet_kernel(parts, *refs):
    out_refs = refs[-2:]
    for half, out_ref in enumerate(out_refs):
        total = None
        for ref, index in zip(refs, parts):
            if index[half] is not None:
                part = ref[index[half]].astype(F32)
                total = part if total is None else total + part
        out_ref[...] = total.astype(out_ref.dtype)


def last_kernel(rows_ref, dq_ref, dqx_ref, dkv_ref, dkvz_ref, q_ref, k_ref, v_ref):
    swapped = rows_ref[0, 4 * BLK :, :].astype(F32)[5:6, :] > 0.5

    def restore(out_ref, total):
        low, high = total[:BLK], total[BLK:]
        out_ref[:BLK, :] = jnp.where(swapped, high, low).astype(BF16)
        out_ref[BLK:, :] = jnp.where(swapped, low, high).astype(BF16)

    restore(q_ref, (dq_ref[...] + dqx_ref[...].astype(F32)) * FACTOR)
    dkv = dkv_ref[...] + dkvz_ref[...].astype(F32)
    restore(k_ref, dkv[: 2 * BLK] * FACTOR)
    restore(v_ref, dkv[2 * BLK :])


def z_step(step):
    return [(i, (i + step) % 8) for i in range(8)]


def y_step(step):
    return [(i, (i + step) % 4) for i in range(4)]


Z_PAIRS = [(i, (i - 2) % 8 if i % 2 == 0 else (i + 2) % 8) for i in range(8)]
Z_BACK = [(b, a) for a, b in Z_PAIRS]
X_SWAP = [(0, 1), (1, 0)]


def call(kernel, outs, operands, scratch=(), hbm=False, **options):
    space = pl.BlockSpec(memory_space=pltpu.HBM if hbm else pltpu.VMEM)
    return pl.pallas_call(
        kernel,
        out_shape=[jax.ShapeDtypeStruct(s, t) for s, t in outs],
        in_specs=[space] * len(operands),
        out_specs=[space] * len(outs),
        scratch_shapes=list(scratch),
        compiler_params=pltpu.CompilerParams(vmem_limit_bytes=PREP_VMEM if hbm else VMEM_LIMIT),
        **options,
    )(*operands)


def body(queries, key_rows, value_rows, outputs, out_grad, saved_lse, fold_map):
    operands = (fold_map, out_grad, outputs, saved_lse.T, key_rows, value_rows, queries)
    buffers = [(pltpu.SMEM if n == 0 else pltpu.VMEM)(a.shape, a.dtype) for n, a in enumerate(operands)]
    rows = pltpu.VMEM((ROWS - 4 * BLK, DIM), BF16)
    sems = [pltpu.SemaphoreType.DMA((7,)), pltpu.SemaphoreType.DMA((10,))]
    payload = ((ROWS, DIM), BF16)
    mine_q, mine_k = call(prep_kernel, [payload] * 2, operands, buffers + [rows] * 2 + sems, hbm=True)

    def beside(mine, other):
        both = lax.optimization_barrier(jnp.pad(mine[None], ((0, 1), (0, 0), (0, 0))))
        return lax.dynamic_update_slice(both, other[None], (1, 0, 0))

    other_k = lax.ppermute(mine_k, "kz", z_step(4))
    q0 = beside(mine_q, lax.ppermute(mine_q, "kx", X_SWAP))
    late_q, other_k = lax.optimization_barrier((q0, other_k))
    k0 = jnp.stack([mine_k, other_k])
    q_sets = [q0] + [lax.ppermute(q, "kz", p) for q, p in ((q0, z_step(1)), (q0, z_step(-1)), (late_q, Z_PAIRS))]
    k_sets = [k0] + [lax.ppermute(k0, "pb", y_step(-s)) for s in Y_FROM[1:]]
    q_groups = [q_sets[:3], q_sets[3:]]

    def grad(turn, group, dq_in, add, last, dkv_type):
        sets = q_groups[group]
        outs = [((2, DIM, 2 * len(sets) * BLK), F32)]
        if last:
            outs = [((2, 2 * BLK, DIM), F32 if (group, s) == (0, 0) else BF16) for s in range(len(sets))]
        acc = pltpu.VMEM((4 * BLK, DIM), F32)
        plan = ((dq_in is None, last),)
        *dq, part = call(
            functools.partial(grad_kernel, (0, 1), (len(sets),), plan, turn == 0 and group == 0, add is not None),
            outs + [((2, 4 * BLK, DIM), dkv_type)],
            [*sets, k_sets[turn]] + [d for d in (dq_in, add) if d is not None],
            [acc, acc],
            cost_estimate=COST,
        )
        return (dq if last else dq[0]), part

    def send_back(turn, part):
        return lax.ppermute(part, "pb", y_step(Y_FROM[turn]))

    both = (0, 1)
    parts = []
    dq = None
    for turn in range(4):
        dq, part = grad(turn, 0, dq, None, turn == 3, F32)
        parts.append(part)
    dq_keep, *dqs = dq
    dq_back = [lax.ppermute(d, "kz", p) for d, p in zip(dqs, (z_step(-1), z_step(1)))]
    q_groups[1][0], parts[3] = lax.optimization_barrier((q_groups[1][0], parts[3]))
    back = []
    dq = None
    for turn in (1, 2, 3):
        dq, part = grad(turn, 1, dq, parts[turn], False, BF16)
        back.append(send_back(turn, part))
    (dq_z2,), own = grad(0, 1, dq, parts[0], True, F32)
    dq_z2, back[0] = lax.optimization_barrier((dq_z2, back[0]))
    dq_back.append(lax.ppermute(dq_z2, "kz", Z_BACK))

    def meet(operands, parts, shape):
        return call(functools.partial(meet_kernel, parts), [(shape, F32), (shape, BF16)], operands)

    dkv_keep, dkv_send = meet(
        [own] + back, [both] * 4, (4 * BLK, DIM)
    )
    dkv_last = lax.ppermute(dkv_send, "kz", z_step(4))
    dq_keep, dq_send = meet([dq_keep] + dq_back, [both] * 4, (2 * BLK, DIM))
    dq_last = lax.ppermute(dq_send, "kx", X_SWAP)
    operands = (q0, dq_keep, dq_last, dkv_keep, dkv_last)
    return tuple(call(last_kernel, [((2 * BLK, DIM), BF16)] * 3, operands))


def solution(mesh):
    fine = Mesh(mesh.devices.reshape(4, 8, 2, 2, 2), ("pb", "kz", "kx", "hx", "hc"))
    rows = P(("pb", "kz", "kx"), ("hx", "hc"))
    return jax.shard_map(
        body,
        mesh=fine,
        in_specs=(rows,) * 6 + (P(),),
        out_specs=(rows,) * 3,
        check_vma=False,
    )
```
